32 devices in a mesh: ctx: 16 (over z, y, x), shard: 2 (over core).
Axes of the slice: x: 2, y: 2, z: 4, core: 2. Of those that a mesh axis runs over, the one named last changes fastest.
Arguments:
- tokens: bfloat16 [4096, 2560], P('ctx'), may hold values from -6 to 6
- cotangent: bfloat16 [4096, 2560], P('ctx'), may hold values from -6 to 6
- query_weight: float32 [2560, 2560], P('ctx', 'shard'), may hold values from -0.25 to 0.25
- query_first: float32 [2560, 2560], P('ctx', 'shard'), may hold values from -40 to 40
- query_second: float32 [2560, 2560], P('ctx', 'shard'), may hold values from 172.032 to 696.32
- keyval_weight: float32 [512, 2560], P(None, ('ctx', 'shard')), may hold values from -0.125 to 0.125
- keyval_first: float32 [512, 2560], P(None, ('ctx', 'shard')), may hold values from -128 to 128
- keyval_second: float32 [512, 2560], P(None, ('ctx', 'shard')), may hold values from 1925.12 to 7782.4
- merge_weight: float32 [2560, 2560], P('ctx', 'shard'), may hold values from -0.5 to 0.5
- merge_first: float32 [2560, 2560], P('ctx', 'shard'), may hold values from -4 to 4
- merge_second: float32 [2560, 2560], P('ctx', 'shard'), may hold values from 9.4208 to 38.0928
- gate_weight: float32 [2560, 7680], P('ctx', 'shard'), may hold values from -0.125 to 0.125
- gate_first: float32 [2560, 7680], P('ctx', 'shard'), may hold values from -16 to 16
- gate_second: float32 [2560, 7680], P('ctx', 'shard'), may hold values from 25.8048 to 102.4
- up_weight: float32 [2560, 7680], P('ctx', 'shard'), may hold values from -0.125 to 0.125
- up_first: float32 [2560, 7680], P('ctx', 'shard'), may hold values from -16 to 16
- up_second: float32 [2560, 7680], P('ctx', 'shard'), may hold values from 25.8048 to 102.4
- down_weight: float32 [2560, 7680], P('ctx', 'shard'), may hold values from -0.0625 to 0.0625
- down_first: float32 [2560, 7680], P('ctx', 'shard'), may hold values from -24 to 24
- down_second: float32 [2560, 7680], P('ctx', 'shard'), may hold values from 77.824 to 311.296
- gains: float32 [2, 2560], P(None, ('ctx', 'shard')), may hold values from 0.5 to 1.5
- gains_first: float32 [2, 2560], P(None, ('ctx', 'shard')), may hold values from -56 to 56
- gains_second: float32 [2, 2560], P(None, ('ctx', 'shard')), may hold values from 245.76 to 2457.6
Outputs:
- block_output: bfloat16 [4096, 2560], P('ctx')
- tokens_grad: float32 [4096, 2560], P('ctx')
- query_grad: float32 [2560, 2560], P('ctx', 'shard')
- query_variance: float32 [2560, 2560], P('ctx', 'shard')
- query_updated: float32 [2560, 2560], P('ctx', 'shard')
- keyval_grad: float32 [512, 2560], P(None, ('ctx', 'shard'))
- keyval_variance: float32 [512, 2560], P(None, ('ctx', 'shard'))
- keyval_updated: float32 [512, 2560], P(None, ('ctx', 'shard'))
- merge_grad: float32 [2560, 2560], P('ctx', 'shard')
- merge_variance: float32 [2560, 2560], P('ctx', 'shard')
- merge_updated: float32 [2560, 2560], P('ctx', 'shard')
- gate_grad: float32 [2560, 7680], P('ctx', 'shard')
- gate_variance: float32 [2560, 7680], P('ctx', 'shard')
- gate_updated: float32 [2560, 7680], P('ctx', 'shard')
- up_grad: float32 [2560, 7680], P('ctx', 'shard')
- up_variance: float32 [2560, 7680], P('ctx', 'shard')
- up_updated: float32 [2560, 7680], P('ctx', 'shard')
- down_grad: float32 [2560, 7680], P('ctx', 'shard')
- down_variance: float32 [2560, 7680], P('ctx', 'shard')
- down_updated: float32 [2560, 7680], P('ctx', 'shard')
- gains_grad: float32 [2, 2560], P(None, ('ctx', 'shard'))
- gains_variance: float32 [2, 2560], P(None, ('ctx', 'shard'))
- gains_updated: float32 [2, 2560], P(None, ('ctx', 'shard'))
The draws below stay inside these ranges and needn't reach their ends.
All inputs are finite; a program needn't handle non-finite values.
Results may differ from the reference program's by a relative error of at most 0.015.
The reference program's roundings to bfloat16 on the way count: a program that leaves them out, or rounds other values in their place, can miss the bound.
Values may be sent and summed in bfloat16 or wider, within the bound.
A program may use at most 384 MiB of HBM per device.

```python
import math
import jax
import jax.numpy as jnp
from jax import lax

D = 2560
NH = 10
HD = 256
FF = 7680
WINDOW = 2048
TOK_DEV = 256
STEP = 10
LENGTH = 4096


def steps_of(rng, extent, pieces, smallest, top_value):
    loudness, own = 1.0, jax.random.fold_in(rng, 6)
    for position, shards_of in pieces:
        steps = jnp.exp(jax.random.uniform(jax.random.fold_in(own, position), (shards_of,), jnp.float32, smallest / len(pieces), top_value / len(pieces)))
        loudness = loudness * jnp.repeat(steps, extent[position] // shards_of).reshape([-1 if axis == position else 1 for axis in range(len(extent))])
    return loudness


def bell_draw(key, shape, scale, most, split=(), kind=jnp.bfloat16):
    entries = scale * jax.random.normal(key, shape, jnp.float32)
    if split:
        entries = entries * steps_of(key, shape, split, -0.22, 0.18)
    return jnp.clip(entries, -most, most).astype(kind)


def setup_inputs(seed: int = 0) -> dict:
    splits = jax.random.split(jax.random.key(seed), 24)
    tokens = bell_draw(splits[0], (LENGTH, D), 1.0, 6.0, ((0, 16),))
    cotangent = bell_draw(splits[1], (LENGTH, D), 1.0, 6.0, ((0, 16),))
    query_weight = bell_draw(splits[2], (D, NH * HD), (D / 4) ** -0.5, 0.25, ((0, 16), (1, 2)), jnp.float32)
    query_first = bell_draw(splits[3], (D, NH * HD), (0.1 * LENGTH ** 0.5), 40.0, ((0, 16), (1, 2)), jnp.float32)
    query_second = jnp.clip(jnp.exp(math.log(696.32) - 1.39812884 * jax.random.uniform(splits[4], (D, NH * HD), jnp.float32) ** steps_of(splits[4], (D, NH * HD), ((0, 16), (1, 2)), -0.2, 0.2)), 172.032, 696.32)
    keyval_weight = bell_draw(splits[5], (2 * HD, D), D ** -0.5, 0.125, ((1, 32),), jnp.float32)
    keyval_first = bell_draw(splits[6], (2 * HD, D), (0.33 * LENGTH ** 0.5), 128.0, ((1, 32),), jnp.float32)
    keyval_second = jnp.clip(jnp.exp(math.log(7782.4) - 1.3968765 * jax.random.uniform(splits[7], (2 * HD, D), jnp.float32) ** steps_of(splits[7], (2 * HD, D), ((1, 32),), -0.2, 0.2)), 1925.12, 7782.4)
    merge_weight = bell_draw(splits[8], (D, NH * HD), (NH * HD / 16) ** -0.5, 0.5, ((0, 16), (1, 2)), jnp.float32)
    merge_first = bell_draw(splits[9], (D, NH * HD), (0.023 * LENGTH ** 0.5), 4.0, ((0, 16), (1, 2)), jnp.float32)
    merge_second = jnp.clip(jnp.exp(math.log(38.0928) - 1.39710526 * jax.random.uniform(splits[10], (D, NH * HD), jnp.float32) ** steps_of(splits[10], (D, NH * HD), ((0, 16), (1, 2)), -0.2, 0.2)), 9.4208, 38.0928)
    gate_weight = bell_draw(splits[11], (D, FF), D ** -0.5, 0.125, ((0, 16), (1, 2)), jnp.float32)
    gate_first = bell_draw(splits[12], (D, FF), (0.039 * LENGTH ** 0.5), 16.0, ((0, 16), (1, 2)), jnp.float32)
    gate_second = jnp.clip(jnp.exp(math.log(102.4) - 1.3783262 * jax.random.uniform(splits[13], (D, FF), jnp.float32) ** steps_of(splits[13], (D, FF), ((0, 16), (1, 2)), -0.2, 0.2)), 25.8048, 102.4)
    up_weight = bell_draw(splits[14], (D, FF), D ** -0.5, 0.125, ((0, 16), (1, 2)), jnp.float32)
    up_first = bell_draw(splits[15], (D, FF), (0.039 * LENGTH ** 0.5), 16.0, ((0, 16), (1, 2)), jnp.float32)
    up_second = jnp.clip(jnp.exp(math.log(102.4) - 1.3783262 * jax.random.uniform(splits[16], (D, FF), jnp.float32) ** steps_of(splits[16], (D, FF), ((0, 16), (1, 2)), -0.2, 0.2)), 25.8048, 102.4)
    down_weight = bell_draw(splits[17], (D, FF), FF ** -0.5, 0.0625, ((0, 16), (1, 2)), jnp.float32)
    down_first = bell_draw(splits[18], (D, FF), (0.067 * LENGTH ** 0.5), 24.0, ((0, 16), (1, 2)), jnp.float32)
    down_second = jnp.clip(jnp.exp(math.log(311.296) - 1.3862944 * jax.random.uniform(splits[19], (D, FF), jnp.float32) ** steps_of(splits[19], (D, FF), ((0, 16), (1, 2)), -0.2, 0.2)), 77.824, 311.296)
    gains = jnp.clip(1.0 + 0.1 * jax.random.normal(splits[20], (2, D), jnp.float32), 0.5, 1.5)
    gains_first = bell_draw(splits[21], (2, D), (0.15 * LENGTH ** 0.5), 56.0, ((1, 32),), jnp.float32)
    gains_second = jnp.clip(jnp.exp(math.log(2457.6) - 2.3025852 * jax.random.uniform(splits[22], (2, D), jnp.float32) ** steps_of(splits[22], (2, D), ((1, 32),), -0.2, 0.2)), 245.76, 2457.6)
    return dict(tokens=tokens, cotangent=cotangent, query_weight=query_weight, query_first=query_first, query_second=query_second, keyval_weight=keyval_weight, keyval_first=keyval_first, keyval_second=keyval_second, merge_weight=merge_weight, merge_first=merge_first, merge_second=merge_second, gate_weight=gate_weight, gate_first=gate_first, gate_second=gate_second, up_weight=up_weight, up_first=up_first, up_second=up_second, down_weight=down_weight, down_first=down_first, down_second=down_second, gains=gains, gains_first=gains_first, gains_second=gains_second)


@jax.custom_vjp
def low(v):
    return lax.optimization_barrier(v.astype(jnp.bfloat16)).astype(jnp.float32)

@jax.custom_vjp
def low_back(v):
    return v

def low_keep(v):
    return (low(v), None)

def low_pass(kept, grad):
    return (grad,)

def back_keep(v):
    return (v, None)

def back_low(kept, grad):
    return (low(grad),)
low.defvjp(low_keep, low_pass)
low_back.defvjp(back_keep, back_low)
beta_first = 0.9
beta_second = 0.95
adam_epsilon = 1e-08
weight_decay = 0.1
norm_epsilon = 1e-06
rotary_base = 10000.0
masked_score = -1e+30
highest = lax.Precision.HIGHEST

def product(left, right):
    return jnp.dot(left, right, precision=highest, preferred_element_type=jnp.float32)

def inverse_rms(values):
    return lax.rsqrt(lax.optimization_barrier(jnp.mean(values * values, axis=-1, keepdims=True)) + norm_epsilon)

def rotate(values, positions):
    quarter = values.shape[-1] // 4
    frequency = rotary_base ** (-jnp.arange(quarter, dtype=jnp.float32) / quarter)
    angles = positions.astype(jnp.float32)[:, None] * frequency[None, :]
    cosine = jnp.cos(angles)
    sine_part = jnp.sin(angles)
    lower_half = values[..., :quarter]
    upper_half = values[..., quarter:2 * quarter]
    return jnp.concatenate([lower_half * cosine - upper_half * sine_part, upper_half * cosine + lower_half * sine_part, values[..., 2 * quarter:]], axis=-1)

def attend(queries, key_pad, value_pad, block_rows, block_index):
    offset = (block_index * block_rows).astype(jnp.int32)
    query_block = lax.dynamic_slice_in_dim(queries, offset, block_rows, 1)
    key_block = lax.dynamic_slice_in_dim(key_pad, offset, WINDOW + block_rows, 0)
    value_block = lax.dynamic_slice_in_dim(value_pad, offset, WINDOW + block_rows, 0)
    scores = low_back(jnp.einsum('hqd,kd->hqk', query_block, key_block, precision=highest))
    query_pos = offset + jnp.arange(block_rows, dtype=jnp.int32)
    key_pos = offset - WINDOW + jnp.arange(WINDOW + block_rows, dtype=jnp.int32)
    allowed = (key_pos[None, :] <= query_pos[:, None]) & (key_pos[None, :] > query_pos[:, None] - WINDOW) & (key_pos[None, :] >= 0)
    scores = jnp.where(allowed[None], scores, masked_score)
    shifted = jnp.exp(scores - lax.optimization_barrier(jnp.max(scores, axis=-1, keepdims=True)))
    chances = shifted / lax.optimization_barrier(jnp.sum(shifted, axis=-1, keepdims=True))
    return jnp.einsum('hqk,kd->hqd', low(chances), value_block, precision=highest)

def forward(tokens, query_weight, keyval_weight, merge_weight, gate_weight, up_weight, down_weight, gains):
    length = tokens.shape[0]
    positions = jnp.arange(length, dtype=jnp.int32)
    gain_used = low(gains)
    normed = low(tokens * inverse_rms(tokens) * gain_used[0])
    query_lin = low_back(product(normed, low(query_weight)))
    queries = query_lin.reshape(length, NH, HD).transpose(1, 0, 2)
    queries = low(rotate(queries, positions) * HD ** (-0.5))
    keyval = low_back(product(normed, low(keyval_weight).T))
    keys_used = low(rotate(keyval[:, :HD], positions))
    values_used = low(keyval[:, HD:])
    padding = jnp.zeros((WINDOW, HD), jnp.float32)
    key_pad = jnp.concatenate([padding, keys_used], axis=0)
    value_pad = jnp.concatenate([padding, values_used], axis=0)
    block_count = length // TOK_DEV

    def one_block(block_index):
        return attend(queries, key_pad, value_pad, TOK_DEV, block_index)
    gathered_blocks = lax.map(jax.checkpoint(one_block), jnp.arange(block_count, dtype=jnp.int32))
    mixed = gathered_blocks.transpose(0, 2, 1, 3).reshape(length, NH * HD)
    mixed = low(low_back(mixed))
    branch = low_back(product(mixed, low(merge_weight).T))
    hidden = tokens + branch
    normed_two = low(hidden * inverse_rms(hidden) * gain_used[1])
    gate_value = low_back(product(normed_two, low(gate_weight)))
    upward = low_back(product(normed_two, low(up_weight)))
    active = low(jax.nn.gelu(gate_value, approximate=True) * upward)
    return hidden + product(active, low(down_weight).T)

def adamw(weight, first_moment, second_moment, gradient, rate_value):
    moment_new = beta_first * first_moment + (1.0 - beta_first) * gradient
    second_new = beta_second * second_moment + (1.0 - beta_second) * gradient * gradient
    step_size = moment_new / (1.0 - beta_first ** STEP) / (jnp.sqrt(second_new / (1.0 - beta_second ** STEP)) + adam_epsilon)
    return (second_new, weight - rate_value * (step_size + weight_decay * weight))

def reference(tokens, cotangent, query_weight, query_first, query_second, keyval_weight, keyval_first, keyval_second, merge_weight, merge_first, merge_second, gate_weight, gate_first, gate_second, up_weight, up_first, up_second, down_weight, down_first, down_second, gains, gains_first, gains_second):
    output, pullback = jax.vjp(forward, tokens.astype(jnp.float32), query_weight, keyval_weight, merge_weight, gate_weight, up_weight, down_weight, gains)
    gradients = pullback(cotangent.astype(jnp.float32))
    query_variance, query_updated = adamw(query_weight, query_first, query_second, gradients[1], 4.0 / math.sqrt(D))
    keyval_variance, keyval_updated = adamw(keyval_weight, keyval_first, keyval_second, gradients[2], 2.0 / math.sqrt(D))
    merge_variance, merge_updated = adamw(merge_weight, merge_first, merge_second, gradients[3], 8.0 / math.sqrt(NH * HD))
    gate_variance, gate_updated = adamw(gate_weight, gate_first, gate_second, gradients[4], 2.0 / math.sqrt(D))
    up_variance, up_updated = adamw(up_weight, up_first, up_second, gradients[5], 2.0 / math.sqrt(D))
    down_variance, down_updated = adamw(down_weight, down_first, down_second, gradients[6], 2.0 / math.sqrt(FF))
    gains_variance, gains_updated = adamw(gains, gains_first, gains_second, gradients[7], 0.8)
    return (output.astype(jnp.bfloat16), gradients[0], gradients[1], query_variance, query_updated, gradients[2], keyval_variance, keyval_updated, gradients[3], merge_variance, merge_updated, gradients[4], gate_variance, gate_updated, gradients[5], up_variance, up_updated, gradients[6], down_variance, down_updated, gradients[7], gains_variance, gains_updated)
```

```python
from functools import partial
import math

import jax
import jax.numpy as jnp
from jax import lax
from jax.sharding import PartitionSpec as P

D = 2560
NH = 10
HD = 256
FF = 7680
WINDOW = 2048
STEP = 10


beta_first = 0.9
beta_second = 0.95
adam_epsilon = 1e-08
weight_decay = 0.1
norm_epsilon = 1e-06
rotary_base = 10000.0
masked_score = -1e30


def inverse_rms(values):
    return lax.rsqrt(jnp.mean(values * values, axis=-1, keepdims=True) + norm_epsilon)


def normalize(values, gain_row):
    return values * inverse_rms(values) * gain_row


def gelu_product(gate_value, upward):
    return jax.nn.gelu(gate_value, approximate=True) * upward


def rotate(values, positions):
    quarter = values.shape[-1] // 4
    frequency = rotary_base ** (-jnp.arange(quarter, dtype=jnp.float32) / quarter)
    angles = positions.astype(jnp.float32)[:, None] * frequency[None, :]
    cosine = jnp.cos(angles)
    sine_part = jnp.sin(angles)
    lower_half = values[..., :quarter]
    upper_half = values[..., quarter : 2 * quarter]
    return jnp.concatenate(
        [
            lower_half * cosine - upper_half * sine_part,
            upper_half * cosine + lower_half * sine_part,
            values[..., 2 * quarter :],
        ],
        axis=-1,
    )


def contract(left, right, left_dim, right_dim):
    return lax.dot_general(
        left, right, (((left_dim,), (right_dim,)), ((), ())), preferred_element_type=jnp.float32
    )


def masked_scores(queries, key_part, allowed):
    scores = jnp.einsum("hqd,kd->hqk", queries, key_part, preferred_element_type=jnp.float32)
    return jnp.where(allowed[None], scores, masked_score)


def adamw(weight, first_moment, second_moment, gradient, rate_value):
    moment_new = beta_first * first_moment + (1.0 - beta_first) * gradient
    second_new = beta_second * second_moment + (1.0 - beta_second) * gradient * gradient
    step_size = (
        moment_new
        / (1.0 - beta_first**STEP)
        / (jnp.sqrt(second_new / (1.0 - beta_second**STEP)) + adam_epsilon)
    )
    return (second_new, weight - rate_value * (step_size + weight_decay * weight))


PLANE = 4


def hop(value, mask):
    count = lax.axis_size("ctx")
    return lax.ppermute(value, "ctx", [(i, i ^ mask) for i in range(count)])


def climb(value, by):
    count = lax.axis_size("ctx")
    return lax.ppermute(value, "ctx", [(i, i + by) for i in range(count) if 0 <= i + by < count])


def swap(value):
    count = lax.axis_size("shard")
    return lax.ppermute(value, "shard", [(i, count - 1 - i) for i in range(count)])


def place():
    me = lax.axis_index("ctx")
    return me // PLANE, me % PLANE


def pick(value, index, axis=0):
    return lax.dynamic_index_in_dim(value, index, axis, keepdims=False)


def put(buffer, piece, *start):
    return lax.dynamic_update_slice(
        buffer, piece, tuple(start) + (0,) * (buffer.ndim - len(start))
    )


def gather_column(block):
    planes = lax.axis_size("ctx") // PLANE
    z, _ = place()
    whole = put(jnp.zeros((planes,) + block.shape, block.dtype), block[None], z)
    for k in range(1, planes):
        whole = put(whole, hop(block, PLANE * k)[None], z ^ k)
    return whole


def deal_column(pieces):
    planes = pieces.shape[0]
    z, _ = place()
    whole = put(jnp.zeros_like(pieces), pick(pieces, z)[None], z)
    for k in range(1, planes):
        whole = put(whole, hop(pick(pieces, z ^ k), PLANE * k)[None], z ^ k)
    return whole


def gather_plane(column):
    planes = column.shape[0]
    half = planes // 2
    _, xy = place()
    first, second = column[:half], column[half:]
    first_near, second_near = hop(first, 1), hop(second, 2)
    first_far, second_far = hop(first, 2), hop(second, 1)
    first_cross, second_cross = hop(first_near, 2), hop(second_near, 1)
    whole = jnp.zeros((planes, PLANE) + column.shape[1:], column.dtype)
    whole = put(whole, column[:, None], 0, xy)
    whole = put(whole, first_near[:, None], 0, xy ^ 1)
    whole = put(whole, second_near[:, None], half, xy ^ 2)
    whole = put(whole, first_far[:, None], 0, xy ^ 2)
    whole = put(whole, second_far[:, None], half, xy ^ 1)
    whole = put(whole, first_cross[:, None], 0, xy ^ 3)
    whole = put(whole, second_cross[:, None], half, xy ^ 3)
    return whole.reshape((-1,) + column.shape[2:])


def gather_small(block):
    column = gather_column(block)
    _, xy = place()
    whole = jnp.zeros(column.shape[:1] + (PLANE,) + column.shape[1:], column.dtype)
    whole = put(whole, column[:, None], 0, xy)
    for m in range(1, PLANE):
        whole = put(whole, hop(column, m)[:, None], 0, xy ^ m)
    return whole.reshape((-1,) + block.shape)


def reduce_plane(terms):
    planes = terms.shape[0]
    half = planes // 2
    _, xy = place()
    cy, cx = xy // 2, xy % 2
    split = terms.reshape((planes, 2, 2) + terms.shape[2:])
    first, second = split[:half], split[half:]
    low = jnp.bfloat16
    first = pick(first, cy, 1) + hop(pick(first, 1 - cy, 1).astype(low), 2).astype(jnp.float32)
    second = pick(second, cx, 2) + hop(pick(second, 1 - cx, 2).astype(low), 1).astype(jnp.float32)
    first = pick(first, cx, 1) + hop(pick(first, 1 - cx, 1).astype(low), 1).astype(jnp.float32)
    second = pick(second, cy, 1) + hop(pick(second, 1 - cy, 1).astype(low), 2).astype(jnp.float32)
    return jnp.concatenate([first, second], axis=0)


def reduce_column(column, kind=jnp.bfloat16):
    z, _ = place()
    total = pick(column, z)
    for k in range(1, column.shape[0]):
        total = total + hop(pick(column, z ^ k).astype(kind), PLANE * k).astype(jnp.float32)
    return total


def reduce_small(terms, kind):
    _, xy = place()
    split = terms.reshape((-1, PLANE) + terms.shape[1:])
    column = pick(split, xy, 1)
    for m in range(1, PLANE):
        column = column + hop(pick(split, xy ^ m, 1).astype(kind), m).astype(jnp.float32)
    return reduce_column(column, kind)


def reduce_blocks(terms):
    blocks = lax.axis_size("ctx")
    split = terms.reshape(blocks // PLANE, PLANE, terms.shape[0] // blocks, terms.shape[1])
    return reduce_column(reduce_plane(split))


def reduce_units(terms):
    blocks = lax.axis_size("ctx")
    split = terms.reshape(blocks // PLANE, PLANE, terms.shape[0] // blocks, terms.shape[1])
    column = reduce_plane(split)
    z, _ = place()
    whole = put(jnp.zeros_like(column), pick(column, z)[None], z)
    low = column.astype(jnp.bfloat16)
    for k in range(1, column.shape[0]):
        arrived = hop(pick(low, z ^ k), PLANE * k).astype(jnp.float32)
        whole = put(whole, arrived[None], z ^ k)
    return jnp.concatenate([whole[j] for j in range(column.shape[0])], axis=1)


def gather_units(weight):
    planes = lax.axis_size("ctx") // PLANE
    units = weight.shape[1] // planes
    low = weight.astype(jnp.bfloat16)
    pieces = jnp.stack([low[:, j * units : (j + 1) * units] for j in range(planes)])
    return gather_plane(deal_column(pieces))


def fetch_tokens(half):
    planes = lax.axis_size("ctx") // PLANE
    return [half] + [hop(half, PLANE * k) for k in range(1, planes)]


def whole_block(half):
    return jnp.concatenate([half, swap(half)], axis=0)


def in_order(half):
    s = lax.axis_index("shard")
    other = swap(half)
    first = jnp.where(s == 0, half, other)
    last = jnp.where(s == 0, other, half)
    return jnp.concatenate([first, last], axis=0)


def return_tokens(parts, share):
    split = parts.reshape(-1, 2, share, parts.shape[-1])
    arrived = swap(split[:, 1].astype(jnp.bfloat16))
    return split[:, 0] + arrived.astype(jnp.float32)


def shards(
    tokens,
    cotangent,
    query_weight,
    query_first,
    query_second,
    keyval_weight,
    keyval_first,
    keyval_second,
    merge_weight,
    merge_first,
    merge_second,
    gate_weight,
    gate_first,
    gate_second,
    up_weight,
    up_first,
    up_second,
    down_weight,
    down_first,
    down_second,
    gains,
    gains_first,
    gains_second,
):
    low = jnp.bfloat16
    z, xy = place()
    s = lax.axis_index("shard")
    blocks = lax.axis_size("ctx")
    planes = blocks // PLANE
    row_count = tokens.shape[0]
    share = row_count // 2
    width = tokens.shape[1]

    def own_rows(value):
        return lax.dynamic_slice_in_dim(value, s * share, share, 0)

    small = jnp.concatenate([keyval_weight.astype(low), gains.astype(low)], axis=0).T
    small_mine = gather_small(small)
    small_other = swap(small_mine)
    small_all = jnp.stack(
        [jnp.where(s == 0, small_mine, small_other), jnp.where(s == 0, small_other, small_mine)],
        axis=1,
    ).reshape(width, -1)
    keyval_full = small_all[:, : 2 * HD]
    gain_used = small_all[:, 2 * HD :].T.astype(jnp.float32)

    query_full = gather_plane(gather_column(query_weight.astype(low)))
    merge_full = gather_plane(gather_column(merge_weight.astype(low)))
    gate_full = gather_units(gate_weight)
    upward_full = gather_units(up_weight)
    down_full = gather_units(down_weight)
    out_grad_parts = fetch_tokens(own_rows(cotangent))

    offset = lax.axis_index("ctx") * row_count
    positions = offset + jnp.arange(row_count, dtype=jnp.int32)
    inputs = tokens.astype(jnp.float32)
    normed = normalize(inputs, gain_used[0]).astype(low)

    keyval = jnp.dot(normed, keyval_full, preferred_element_type=jnp.float32)
    keyval_used = jnp.stack([rotate(keyval[:, :HD], positions), keyval[:, HD:]]).astype(low)
    halo_planes = WINDOW // (PLANE * row_count)
    mine = pick(keyval_used, s)
    pile = jnp.stack([climb(mine, PLANE * k) for k in range(halo_planes, 0, -1)] + [mine])
    frame = jnp.zeros((halo_planes + 1, PLANE) + mine.shape, low)
    frame = put(frame, pile[:, None], 0, xy)
    for m in range(1, PLANE):
        frame = put(frame, hop(pile, m)[:, None], 0, xy ^ m)
    frame = frame.reshape(-1, HD)
    extent = WINDOW + row_count
    mine = lax.dynamic_slice_in_dim(frame, xy * row_count, extent, 0)
    other = swap(mine)
    key_part = jnp.where(s == 0, mine, other)
    value_part = jnp.where(s == 0, other, mine)

    query_lin = jnp.dot(normed, query_full, preferred_element_type=jnp.float32)
    head_count = query_lin.shape[1] // HD
    queries = (
        rotate(query_lin.reshape(row_count, head_count, HD).transpose(1, 0, 2), positions)
        * HD ** (-0.5)
    ).astype(low)
    key_pos = offset - WINDOW + jnp.arange(extent, dtype=jnp.int32)
    allowed = (
        (key_pos[None, :] <= positions[:, None])
        & (key_pos[None, :] > positions[:, None] - WINDOW)
        & (key_pos[None, :] >= 0)
    )
    scores = masked_scores(queries, key_part, allowed)
    row_peak = jnp.max(scores, axis=-1, keepdims=True)
    shifted = jnp.exp(scores - row_peak)
    row_total = jnp.sum(shifted, axis=-1, keepdims=True)
    log_total = row_peak + jnp.log(row_total)
    chances = (shifted / row_total).astype(low)
    mixed = jnp.einsum("hqk,kd->hqd", chances, value_part, preferred_element_type=jnp.float32)
    mixed_flat = mixed.transpose(1, 0, 2).reshape(row_count, head_count * HD).astype(low)
    branch = contract(mixed_flat, merge_full, 1, 1)
    branch_other = lax.dynamic_slice_in_dim(branch, (1 - s) * share, share, 0)
    input_rows = own_rows(inputs)
    hidden = input_rows + own_rows(branch) + swap(branch_other)
    inverse_two = inverse_rms(hidden)
    normed_two = (hidden * inverse_two * gain_used[1]).astype(low)

    normed_parts = fetch_tokens(normed_two)
    chunk = planes // 2
    actives, gates_low, upwards_low, normed_all, grads_all = [], [], [], [], []
    feeds, backs = [], []
    for at in range(0, planes, chunk):
        rows = jnp.concatenate([whole_block(h) for h in normed_parts[at : at + chunk]], axis=0)
        pulls = jnp.concatenate([whole_block(h) for h in out_grad_parts[at : at + chunk]], axis=0)
        gate_value = jnp.dot(rows, gate_full, preferred_element_type=jnp.float32)
        upward = jnp.dot(rows, upward_full, preferred_element_type=jnp.float32)
        active_grad = jnp.dot(pulls, down_full, preferred_element_type=jnp.float32)
        active = gelu_product(gate_value, upward).astype(low)
        gate_pull = jax.vjp(gelu_product, gate_value, upward)[1]
        gate_low, upward_low = (g.astype(low) for g in gate_pull(active_grad))
        back = contract(gate_low, gate_full, 1, 1) + contract(upward_low, upward_full, 1, 1)
        backs.append(return_tokens(back, share))
        feeds.append(return_tokens(contract(active, down_full, 1, 1), share))
        normed_all.append(rows)
        grads_all.append(pulls)
        actives.append(active)
        gates_low.append(gate_low)
        upwards_low.append(upward_low)

    def home(pieces):
        total = pieces[0][0]
        for k in range(1, planes):
            piece = pieces[k // chunk][k % chunk].astype(low)
            total = total + hop(piece, PLANE * k).astype(jnp.float32)
        return total

    normtwo_grad = home(backs)
    gain_two_grad = jnp.sum(normtwo_grad * hidden * inverse_two, axis=0)
    norm_two_pull = jax.vjp(partial(normalize, gain_row=gain_used[1]), hidden)[1]
    hidden_grad = own_rows(cotangent).astype(jnp.float32) + norm_two_pull(normtwo_grad)[0]
    hidden_low = in_order(hidden_grad.astype(low))
    mixed_grad = jnp.dot(hidden_low, merge_full, preferred_element_type=jnp.float32)
    mixed_grad = mixed_grad.reshape(row_count, head_count, HD).transpose(1, 0, 2).astype(low)

    normed_all, grads_all, actives, gates_low, upwards_low = (
        jnp.concatenate(v, axis=0) for v in (normed_all, grads_all, actives, gates_low, upwards_low)
    )
    down_reduced = reduce_units(contract(grads_all, actives, 0, 0))
    gate_reduced = reduce_units(contract(normed_all, gates_low, 0, 0))
    upward_reduced = reduce_units(contract(normed_all, upwards_low, 0, 0))
    block_output = in_order((hidden + home(feeds)).astype(low))
    merge_reduced = reduce_blocks(contract(hidden_low, mixed_flat, 0, 0))

    chance_again = jnp.exp(masked_scores(queries, key_part, allowed) - log_total)
    chance_grad = jnp.einsum(
        "hqd,kd->hqk", mixed_grad, value_part, preferred_element_type=jnp.float32
    )
    row_inner = jnp.sum(chance_again * chance_grad, axis=-1, keepdims=True)
    score_low = (chance_again * (chance_grad - row_inner)).astype(low)
    key_grad = jnp.einsum("hqk,hqd->kd", score_low, queries, preferred_element_type=jnp.float32)
    value_grad = jnp.einsum(
        "hqk,hqd->kd", chance_again.astype(low), mixed_grad, preferred_element_type=jnp.float32
    )
    query_grad_full = jnp.einsum(
        "hqk,kd->hqd", score_low, key_part, preferred_element_type=jnp.float32
    )
    query_lin_grad = (
        rotate(query_grad_full * HD ** (-0.5), -positions)
        .transpose(1, 0, 2)
        .reshape(row_count, head_count * HD)
        .astype(low)
    )
    query_reduced = reduce_blocks(contract(normed, query_lin_grad, 0, 0))

    mine = jnp.where(s == 0, key_grad, value_grad)
    other = jnp.where(s == 0, value_grad, key_grad).astype(low)
    mine = mine + swap(other).astype(jnp.float32)
    frame = put(jnp.zeros(((halo_planes + 1) * PLANE * row_count, HD), jnp.float32), mine, xy * row_count)
    frame = frame.reshape(halo_planes + 1, PLANE, row_count, HD)
    pile = pick(frame, xy, 1)
    for m in range(1, PLANE):
        pile = pile + hop(pick(frame, xy ^ m, 1).astype(low), m).astype(jnp.float32)
    mine = pile[halo_planes]
    for k in range(1, halo_planes + 1):
        mine = mine + climb(pile[halo_planes - k].astype(low), -PLANE * k).astype(jnp.float32)
    mine = jnp.where(s == 0, rotate(mine, -positions), mine).astype(low)
    other = swap(mine)
    keyval_lin = jnp.concatenate(
        [jnp.where(s == 0, mine, other), jnp.where(s == 0, other, mine)], axis=1
    )

    normed_columns = pick(normed.reshape(row_count, blocks, 2, -1), s, 2)
    keyval_term = contract(normed_columns.reshape(row_count, -1), keyval_lin, 0, 0)
    keyval_term = keyval_term.reshape(blocks, -1, 2 * HD)
    keyval_reduced = reduce_small(keyval_term, low).T

    normone_part = contract(query_lin_grad, query_full, 1, 1)
    normone_other = lax.dynamic_slice_in_dim(normone_part, (1 - s) * share, share, 0)
    normone_grad = (
        own_rows(normone_part)
        + swap(normone_other.astype(low)).astype(jnp.float32)
        + contract(own_rows(keyval_lin), keyval_full, 1, 1)
    )
    gain_one_grad = jnp.sum(normone_grad * input_rows * inverse_rms(input_rows), axis=0)
    norm_one_pull = jax.vjp(partial(normalize, gain_row=gain_used[0]), input_rows)[1]
    tokens_grad = in_order(hidden_grad + norm_one_pull(normone_grad)[0])

    gain_terms = jnp.stack([gain_one_grad, gain_two_grad]).reshape(2, blocks, 2, -1)
    gain_terms = gain_terms.transpose(2, 1, 0, 3)
    gain_sums = pick(gain_terms, s) + swap(pick(gain_terms, 1 - s))
    gains_reduced = reduce_small(gain_sums, jnp.float32)

    query_variance, query_updated = adamw(
        query_weight, query_first, query_second, query_reduced, 4.0 / math.sqrt(D)
    )
    keyval_variance, keyval_updated = adamw(
        keyval_weight, keyval_first, keyval_second, keyval_reduced, 2.0 / math.sqrt(D)
    )
    merge_variance, merge_updated = adamw(
        merge_weight, merge_first, merge_second, merge_reduced, 8.0 / math.sqrt(NH * HD)
    )
    gate_variance, gate_updated = adamw(
        gate_weight, gate_first, gate_second, gate_reduced, 2.0 / math.sqrt(D)
    )
    up_variance, up_updated = adamw(
        up_weight, up_first, up_second, upward_reduced, 2.0 / math.sqrt(D)
    )
    down_variance, down_updated = adamw(
        down_weight, down_first, down_second, down_reduced, 2.0 / math.sqrt(FF)
    )
    gains_variance, gains_updated = adamw(gains, gains_first, gains_second, gains_reduced, 0.8)
    return (
        block_output,
        tokens_grad,
        query_reduced,
        query_variance,
        query_updated,
        keyval_reduced,
        keyval_variance,
        keyval_updated,
        merge_reduced,
        merge_variance,
        merge_updated,
        gate_reduced,
        gate_variance,
        gate_updated,
        upward_reduced,
        up_variance,
        up_updated,
        down_reduced,
        down_variance,
        down_updated,
        gains_reduced,
        gains_variance,
        gains_updated,
    )


def solution(mesh):
    return jax.shard_map(
        shards,
        mesh=mesh,
        in_specs=(
            P("ctx", None),
            P("ctx", None),
            P("ctx", "shard"),
            P("ctx", "shard"),
            P("ctx", "shard"),
            P(None, ("ctx", "shard")),
            P(None, ("ctx", "shard")),
            P(None, ("ctx", "shard")),
            P("ctx", "shard"),
            P("ctx", "shard"),
            P("ctx", "shard"),
            P("ctx", "shard"),
            P("ctx", "shard"),
            P("ctx", "shard"),
            P("ctx", "shard"),
            P("ctx", "shard"),
            P("ctx", "shard"),
            P("ctx", "shard"),
            P("ctx", "shard"),
            P("ctx", "shard"),
            P(None, ("ctx", "shard")),
            P(None, ("ctx", "shard")),
            P(None, ("ctx", "shard")),
        ),
        out_specs=(
            P("ctx", None),
            P("ctx", None),
            P("ctx", "shard"),
            P("ctx", "shard"),
            P("ctx", "shard"),
            P(None, ("ctx", "shard")),
            P(None, ("ctx", "shard")),
            P(None, ("ctx", "shard")),
            P("ctx", "shard"),
            P("ctx", "shard"),
            P("ctx", "shard"),
            P("ctx", "shard"),
            P("ctx", "shard"),
            P("ctx", "shard"),
            P("ctx", "shard"),
            P("ctx", "shard"),
            P("ctx", "shard"),
            P("ctx", "shard"),
            P("ctx", "shard"),
            P("ctx", "shard"),
            P(None, ("ctx", "shard")),
            P(None, ("ctx", "shard")),
            P(None, ("ctx", "shard")),
        ),
        check_vma=False,
    )
```

```python
from functools import partial
import math

import jax
import jax.numpy as jnp
from jax import lax
from jax.experimental import pallas as pl
from jax.experimental.pallas import tpu as pltpu
from jax.sharding import PartitionSpec as P

D = 2560
NH = 10
HD = 256
FF = 7680
WINDOW = 2048
STEP = 10


beta_first = 0.9
beta_second = 0.95
adam_epsilon = 1e-08
weight_decay = 0.1
norm_epsilon = 1e-06
rotary_base = 10000.0
masked_score = -1e30


def inverse_rms(values):
    return lax.rsqrt(jnp.mean(values * values, axis=-1, keepdims=True) + norm_epsilon)


def normalize(values, gain_row):
    return values * inverse_rms(values) * gain_row


def gelu_product(gate_value, upward):
    return jax.nn.gelu(gate_value, approximate=True) * upward


def rotate(values, positions):
    quarter = values.shape[-1] // 4
    frequency = rotary_base ** (-jnp.arange(quarter, dtype=jnp.float32) / quarter)
    angles = positions.astype(jnp.float32)[:, None] * frequency[None, :]
    cosine = jnp.cos(angles)
    sine_part = jnp.sin(angles)
    lower_half = values[..., :quarter]
    upper_half = values[..., quarter : 2 * quarter]
    return jnp.concatenate(
        [
            lower_half * cosine - upper_half * sine_part,
            upper_half * cosine + lower_half * sine_part,
            values[..., 2 * quarter :],
        ],
        axis=-1,
    )


def contract(left, right, left_dim, right_dim):
    return lax.dot_general(
        left, right, (((left_dim,), (right_dim,)), ((), ())), preferred_element_type=jnp.float32
    )


def masked_scores(queries, key_part, allowed):
    scores = jnp.einsum("hqd,kd->hqk", queries, key_part, preferred_element_type=jnp.float32)
    return jnp.where(allowed[None], scores, masked_score)


def adamw(weight, first_moment, second_moment, gradient, rate_value):
    moment_new = beta_first * first_moment + (1.0 - beta_first) * gradient
    second_new = beta_second * second_moment + (1.0 - beta_second) * gradient * gradient
    step_size = (
        moment_new
        / (1.0 - beta_first**STEP)
        / (jnp.sqrt(second_new / (1.0 - beta_second**STEP)) + adam_epsilon)
    )
    return (second_new, weight - rate_value * (step_size + weight_decay * weight))


PLANE = 4


def hop(value, mask):
    count = lax.axis_size("ctx")
    return lax.ppermute(value, "ctx", [(i, i ^ mask) for i in range(count)])


def climb(value, by):
    count = lax.axis_size("ctx")
    return lax.ppermute(value, "ctx", [(i, i + by) for i in range(count) if 0 <= i + by < count])


def swap(value):
    count = lax.axis_size("shard")
    return lax.ppermute(value, "shard", [(i, count - 1 - i) for i in range(count)])


def place():
    me = lax.axis_index("ctx")
    return me // PLANE, me % PLANE


def turn(value, planes_up):
    count = lax.axis_size("ctx")
    step = PLANE * planes_up
    return lax.ppermute(value, "ctx", [(i, (i + step) % count) for i in range(count)])


def pick(value, index, axis=0):
    return lax.dynamic_index_in_dim(value, index, axis, keepdims=False)


def put(buffer, piece, *start):
    return lax.dynamic_update_slice(
        buffer, piece, tuple(start) + (0,) * (buffer.ndim - len(start))
    )


def gather_column(block):
    planes = lax.axis_size("ctx") // PLANE
    z, _ = place()
    whole = put(jnp.zeros((planes,) + block.shape, block.dtype), block[None], z)
    for k in range(1, planes):
        whole = put(whole, hop(block, PLANE * k)[None], z ^ k)
    return whole


def gather_small(block):
    column = gather_column(block)
    _, xy = place()
    whole = jnp.zeros(column.shape[:1] + (PLANE,) + column.shape[1:], column.dtype)
    whole = put(whole, column[:, None], 0, xy)
    for m in range(1, PLANE):
        whole = put(whole, hop(column, m)[:, None], 0, xy ^ m)
    return whole.reshape((-1,) + block.shape)


def reduce_column(column, kind=jnp.bfloat16):
    z, _ = place()
    total = pick(column, z)
    for k in range(1, column.shape[0]):
        total = total + hop(pick(column, z ^ k).astype(kind), PLANE * k).astype(jnp.float32)
    return total


def reduce_small(terms, kind):
    _, xy = place()
    split = terms.reshape((-1, PLANE) + terms.shape[1:])
    column = pick(split, xy, 1)
    for m in range(1, PLANE):
        column = column + hop(pick(split, xy ^ m, 1).astype(kind), m).astype(jnp.float32)
    return reduce_column(column, kind)


def unit_pieces(weight):
    planes = lax.axis_size("ctx") // PLANE
    units = weight.shape[1] // planes
    low = weight.astype(jnp.bfloat16)
    return jnp.stack([low[:, j * units : (j + 1) * units] for j in range(planes)])


def join_units(pieces):
    return jnp.concatenate([p.astype(jnp.float32) for p in pieces], axis=1)


def as_blocks(terms):
    blocks = lax.axis_size("ctx")
    return terms.astype(jnp.bfloat16).reshape(
        blocks // PLANE, PLANE, terms.shape[0] // blocks, terms.shape[1]
    )


def fetch_tokens(half):
    planes = lax.axis_size("ctx") // PLANE
    return [half] + [hop(half, PLANE * k) for k in range(1, planes)]


def whole_block(half):
    return jnp.concatenate([half, swap(half)], axis=0)


def in_order(half):
    s = lax.axis_index("shard")
    other = swap(half)
    first = jnp.where(s == 0, half, other)
    last = jnp.where(s == 0, other, half)
    return jnp.concatenate([first, last], axis=0)


def return_tokens(parts, share):
    split = parts.reshape(-1, 2, share, parts.shape[-1])
    arrived = swap(split[:, 1].astype(jnp.bfloat16))
    return split[:, 0] + arrived.astype(jnp.float32)


MESH = pl.DeviceIdType.MESH


def flip(index, mask):
    result = index
    bit = 1
    while bit <= mask:
        if mask & bit:
            result = result + bit * (1 - 2 * ((index // bit) % 2))
        bit *= 2
    return result


def greet(partners):
    barrier = pltpu.get_barrier_semaphore()
    for device in partners:
        pl.semaphore_signal(barrier, inc=1, device_id=device, device_id_type=MESH)
    pl.semaphore_wait(barrier, len(partners))


def send(source, target, sent, received, device):
    copy = pltpu.make_async_remote_copy(
        src_ref=source,
        dst_ref=target,
        send_sem=sent,
        recv_sem=received,
        device_id=device,
        device_id_type=MESH,
    )
    copy.start()
    return copy


def routes(planes, kz):
    return (1, 2) if kz < planes // 2 else (2, 1)


class Wires:
    def __init__(self, planes):
        self.planes = planes
        self.me = lax.axis_index("ctx")
        self.s = lax.axis_index("shard")
        self.z = self.me // PLANE
        self.xy = self.me % PLANE

    def across(self, mask):
        return (flip(self.me, mask), self.s)

    def twin(self):
        return (self.me, 1 - self.s)

    def partners(self):
        return [self.across(PLANE * k) for k in range(1, self.planes)] + [
            self.across(1),
            self.across(2),
        ]


def gather_kernel(planes, kinds, *refs):
    count = len(kinds)
    sources, wholes = refs[:count], refs[count : 2 * count]
    own_sem, sent, received = refs[2 * count :]
    w = Wires(planes)
    z, xy = w.z, w.xy
    greet(w.partners())
    copies = []

    def piece(i, kz, m):
        return wholes[i].at[flip(z, kz), flip(xy, m)]

    def push(i, kz, m, slot, source, target, device):
        copies.append(
            send(source, target, sent.at[i, slot, kz], received.at[i, kz, m], device)
        )

    def wait_for(i, kz, m):
        there = piece(i, kz, m)
        pltpu.make_async_copy(there, there, received.at[i, kz, m]).wait()

    own = []
    for i, kind in enumerate(kinds):
        mine = sources[i] if kind == "rows" else sources[i].at[z]
        own.append(pltpu.make_async_copy(mine, wholes[i].at[z, xy], own_sem.at[i]))
        own[-1].start()

    def rise(i):
        for k in range(1, planes):
            mine = sources[i] if kinds[i] == "rows" else sources[i].at[flip(z, k)]
            push(i, k, 0, 0, mine, wholes[i].at[z, xy], w.across(PLANE * k))

    def spread(i, kz):
        first, second = routes(planes, kz)
        if kz:
            wait_for(i, kz, 0)
            mine = wholes[i].at[flip(z, kz), xy]
        else:
            mine = sources[i] if kinds[i] == "rows" else sources[i].at[z]
        there = wholes[i].at[flip(z, kz), xy]
        push(i, kz, first, 1, mine, there, w.across(first))
        push(i, kz, second, 2, mine, there, w.across(second))

    def relay(i, kz):
        first, second = routes(planes, kz)
        wait_for(i, kz, first)
        there = piece(i, kz, first)
        push(i, kz, 3, 3, there, there, w.across(second))

    def settle(i, kz):
        first, second = routes(planes, kz)
        wait_for(i, kz, second)
        wait_for(i, kz, 3)

    rise(0)
    spread(0, 0)
    for i in range(count):
        if i + 1 < count:
            rise(i + 1)
        for kz in range(1, planes):
            spread(i, kz)
            relay(i, kz - 1)
        if i + 1 < count:
            spread(i + 1, 0)
        relay(i, planes - 1)
    for i in range(count):
        for kz in range(planes):
            settle(i, kz)
        own[i].wait()
    for copy in copies:
        copy.wait_send()


def gather_weights(blocks, kinds):
    planes = lax.axis_size("ctx") // PLANE
    count = len(blocks)
    shapes = [
        jax.ShapeDtypeStruct((planes, PLANE) + b.shape[-2:], b.dtype) for b in blocks
    ]
    return pl.pallas_call(
        partial(gather_kernel, planes, kinds),
        out_shape=shapes,
        in_specs=[pl.BlockSpec(memory_space=pl.ANY)] * count,
        out_specs=[pl.BlockSpec(memory_space=pl.ANY)] * count,
        scratch_shapes=[
            pltpu.SemaphoreType.DMA((count,)),
            pltpu.SemaphoreType.DMA((count, 4, planes)),
            pltpu.SemaphoreType.DMA((count, planes, PLANE)),
        ],
        compiler_params=pltpu.CompilerParams(collective_id=1, has_side_effects=True),
    )(*blocks)


def reduce_kernel(planes, kinds, *refs):
    count = len(kinds)
    terms, results = refs[:count], refs[count : 2 * count]
    rest = refs[2 * count :]
    far, near, own, pair, tops = (rest[j * count : (j + 1) * count] for j in range(5))
    local, sent, received, final_sent, final_received = rest[5 * count :]
    w = Wires(planes)
    z, xy = w.z, w.xy
    greet(w.partners())
    copies = []

    def term(i, kz, m):
        return terms[i].at[flip(z, kz), flip(xy, m)]

    def add(target, a, b):
        target[...] = (a[...].astype(jnp.float32) + b[...].astype(jnp.float32)).astype(target.dtype)

    loads = {}
    for i in range(count):
        for kz in range(planes):
            first, second = routes(planes, kz)
            for slot, m in ((0, 0), (1, first)):
                buffer = (own, pair)[slot][i].at[kz]
                loads[i, kz, slot] = pltpu.make_async_copy(
                    term(i, kz, m), buffer, local.at[i, kz, slot]
                )
                loads[i, kz, slot].start()

    def far_out(i, kz):
        first, second = routes(planes, kz)
        for slot, m in ((1, 3), (0, second)):
            copies.append(
                send(
                    term(i, kz, m),
                    far[i].at[kz, slot],
                    sent.at[i, kz, slot],
                    received.at[i, kz, slot],
                    w.across(second),
                )
            )

    def arrived(there, semaphore):
        pltpu.make_async_copy(there, there, semaphore).wait()

    def near_out(i, kz):
        first, second = routes(planes, kz)
        loads[i, kz, 1].wait()
        arrived(far[i].at[kz, 1], received.at[i, kz, 1])
        add(pair[i].at[kz], pair[i].at[kz], far[i].at[kz, 1])
        copies.append(
            send(
                pair[i].at[kz],
                near[i].at[kz],
                sent.at[i, kz, 2],
                received.at[i, kz, 2],
                w.across(first),
            )
        )
        loads[i, kz, 0].wait()
        arrived(far[i].at[kz, 0], received.at[i, kz, 0])

    def column_out(i, kz):
        arrived(near[i].at[kz], received.at[i, kz, 2])
        total = (
            own[i][kz].astype(jnp.float32)
            + far[i][kz, 0].astype(jnp.float32)
            + near[i][kz].astype(jnp.float32)
        )
        own[i][kz] = total.astype(own[i].dtype)
        if kz == 0:
            return
        target = tops[i].at[kz - 1] if kinds[i] == "rows" else results[i].at[z]
        copies.append(
            send(
                own[i].at[kz],
                target,
                final_sent.at[i, kz],
                final_received.at[i, kz],
                w.across(PLANE * kz),
            )
        )

    keeps = []

    def finish(i):
        if kinds[i] == "rows":
            total = own[i][0].astype(jnp.float32)
            for k in range(1, planes):
                arrived(tops[i].at[k - 1], final_received.at[i, k])
                total = total + tops[i][k - 1].astype(jnp.float32)
            results[i][...] = total
        else:
            keep = pltpu.make_async_copy(own[i].at[0], results[i].at[z], final_sent.at[i, 0])
            keep.start()
            keeps.append(keep)
            for k in range(1, planes):
                arrived(results[i].at[flip(z, k)], final_received.at[i, k])

    order = [(i, kz) for i in range(count) for kz in list(range(1, planes)) + [0]]
    ahead = planes
    for step in range(ahead):
        far_out(*order[step])
    for step, at in enumerate(order):
        if step + ahead < len(order):
            far_out(*order[step + ahead])
        near_out(*at)
        if step >= 1:
            column_out(*order[step - 1])
    column_out(*order[-1])
    for i in range(count):
        finish(i)
    for copy in copies:
        copy.wait_send()
    for keep in keeps:
        keep.wait()


def reduce_weights(terms, kinds):
    planes = lax.axis_size("ctx") // PLANE
    count = len(terms)
    low = jnp.bfloat16
    shapes, specs, tops = [], [], []
    for t, kind in zip(terms, kinds):
        rows, width = t.shape[-2:]
        if kind == "rows":
            shapes.append(jax.ShapeDtypeStruct((rows, width), jnp.float32))
            specs.append(pl.BlockSpec(memory_space=pltpu.VMEM))
            tops.append(pltpu.VMEM((planes - 1, rows, width), low))
        else:
            shapes.append(jax.ShapeDtypeStruct((planes, rows, width), low))
            specs.append(pl.BlockSpec(memory_space=pl.ANY))
            tops.append(pltpu.VMEM((1, 8, 128), low))
    return pl.pallas_call(
        partial(reduce_kernel, planes, kinds),
        out_shape=shapes,
        in_specs=[pl.BlockSpec(memory_space=pl.ANY)] * count,
        out_specs=specs,
        scratch_shapes=[pltpu.VMEM((planes, 2) + t.shape[-2:], low) for t in terms]
        + [pltpu.VMEM((planes,) + t.shape[-2:], low) for t in terms] * 3
        + tops
        + [
            pltpu.SemaphoreType.DMA((count, planes, 2)),
            pltpu.SemaphoreType.DMA((count, planes, 3)),
            pltpu.SemaphoreType.DMA((count, planes, 3)),
            pltpu.SemaphoreType.DMA((count, planes)),
            pltpu.SemaphoreType.DMA((count, planes)),
        ],
        compiler_params=pltpu.CompilerParams(
            collective_id=2, has_side_effects=True, vmem_limit_bytes=56 * 2**20
        ),
    )(*terms)


def gelu_parts(u):
    scale = math.sqrt(2.0 / math.pi)
    square = u * u
    bend = jnp.tanh(scale * u * (1.0 + 0.044715 * square))
    half = 0.5 * (1.0 + bend)
    slope = half + 0.5 * u * (1.0 - bend * bend) * scale * (1.0 + 3.0 * 0.044715 * square)
    return u * half, slope


def product_nt(left, right):
    return lax.dot_general(
        left, right, (((1,), (1,)), ((), ())), preferred_element_type=jnp.float32
    )


def product_tn(left, right):
    return lax.dot_general(
        left, right, (((0,), (0,)), ((), ())), preferred_element_type=jnp.float32
    )


STEP_COLUMNS = 256


def feed_kernel(
    planes,
    depth,
    lanes,
    half,
    pulls,
    gate,
    upward,
    down,
    back_out,
    feed_out,
    down_out,
    gate_out,
    upward_out,
    weights,
    rows,
    grads,
    acts,
    gates,
    ups,
    own,
    outgoing,
    incoming,
    sums,
    local,
    row_sent,
    row_received,
    twin_sent,
    twin_received,
    pair_sent,
    pair_received,
    back_sent,
    back_received,
    feed_local,
):
    w = Wires(planes)
    z = w.z
    share, width = half.shape
    units = weights.shape[2]

    def plane(index):
        return (lax.rem(index + planes, planes) * PLANE + w.xy, w.s)

    greet([plane(z + k) for k in range(1, planes)] + [w.twin()])

    top, bottom = pl.ds(0, share), pl.ds(share, share)

    def row_copy(k):
        return pltpu.make_async_remote_copy(
            src_ref=half,
            dst_ref=rows.at[k, top],
            send_sem=row_sent.at[k],
            recv_sem=row_received.at[k],
            device_id=plane(z + k),
            device_id_type=MESH,
        )

    def twin_copy(k):
        return pltpu.make_async_remote_copy(
            src_ref=rows.at[k, top],
            dst_ref=rows.at[k, bottom],
            send_sem=twin_sent.at[k],
            recv_sem=twin_received.at[k],
            device_id=w.twin(),
            device_id_type=MESH,
        )

    def pair_copy(k):
        return pltpu.make_async_remote_copy(
            src_ref=outgoing.at[lax.rem(k, depth)],
            dst_ref=incoming.at[lax.rem(k, 2)],
            send_sem=pair_sent.at[lax.rem(k, depth)],
            recv_sem=pair_received.at[lax.rem(k, 2)],
            device_id=w.twin(),
            device_id_type=MESH,
        )

    def back_copy(k):
        return pltpu.make_async_remote_copy(
            src_ref=sums.at[lax.rem(k, lanes), 0],
            dst_ref=back_out.at[k],
            send_sem=back_sent.at[k],
            recv_sem=back_received.at[k],
            device_id=plane(z - k),
            device_id_type=MESH,
        )

    def kept_copy():
        return pltpu.make_async_copy(sums.at[0, 0], back_out.at[0], back_sent.at[0])

    def feed_copy(k):
        return pltpu.make_async_copy(
            sums.at[lax.rem(k, lanes), 1], feed_out.at[k], feed_local.at[k]
        )

    def shipped(k):
        feed_copy(k).wait()

        @pl.when(k == 0)
        def _():
            kept_copy().wait()

        @pl.when(k > 0)
        def _():
            back_copy(k).wait_send()

    first = pltpu.make_async_copy(half, rows.at[0, top], local.at[0])
    first.start()
    for k in range(1, planes):
        row_copy(k).start()
    loads = []
    for i, source in enumerate((gate, upward, down)):
        loads.append(pltpu.make_async_copy(source, weights.at[i], local.at[1 + i]))
    for k in range(planes):
        loads.append(
            pltpu.make_async_copy(
                pulls.at[lax.rem(z - k + planes, planes)], grads.at[k], local.at[4 + k]
            )
        )
    for load in loads:
        load.start()
    first.wait()
    twin_copy(0).start()
    for load in loads:
        load.wait()

    def compute(k, slot):
        for at in range(0, units, STEP_COLUMNS):
            columns = slice(at, min(at + STEP_COLUMNS, units))
            here = rows[k]
            gate_value = jnp.dot(here, weights[0, :, columns], preferred_element_type=jnp.float32)
            up_value = jnp.dot(here, weights[1, :, columns], preferred_element_type=jnp.float32)
            pull = jnp.dot(grads[k], weights[2, :, columns], preferred_element_type=jnp.float32)
            bent, slope = gelu_parts(gate_value)
            acts[k, :, columns] = (bent * up_value).astype(acts.dtype)
            gates[k, :, columns] = (pull * up_value * slope).astype(gates.dtype)
            ups[k, :, columns] = (pull * bent).astype(ups.dtype)

        def part(j, _):
            at = pl.ds(pl.multiple_of(j * STEP_COLUMNS, STEP_COLUMNS), STEP_COLUMNS)
            back = product_nt(gates[k], weights[0, at, :]) + product_nt(ups[k], weights[1, at, :])
            feed = product_nt(acts[k], weights[2, at, :])
            for i, value in enumerate((back, feed)):
                own[slot, i, :, at] = value[:share]
                outgoing[slot, i, :, at] = value[share:].astype(outgoing.dtype)
            return 0

        lax.fori_loop(0, width // STEP_COLUMNS, part, 0)

    def settle(k):
        pair = pair_copy(k)
        pair.wait_recv()
        pair.wait_send()

        @pl.when(k >= lanes)
        def _():
            shipped(k - lanes)

        for i in range(2):
            arrived = incoming[lax.rem(k, 2), i].astype(jnp.float32)
            sums[lax.rem(k, lanes), i] = (own[lax.rem(k, depth), i] + arrived).astype(sums.dtype)

        @pl.when(k == 0)
        def _():
            kept_copy().start()

        @pl.when(k > 0)
        def _():
            back_copy(k).start()

        feed_copy(k).start()

    def step(k, _):
        @pl.when(k > 0)
        def _():
            row_copy(k).wait_recv()
            twin_copy(k).start()

        if depth > 1:

            @pl.when(k > 0)
            def _():
                settle(k - 1)

        twin_copy(k).wait_recv()
        compute(k, lax.rem(k, depth))
        pair_copy(k).start()
        if depth == 1:
            settle(k)
        return 0

    lax.fori_loop(0, planes, step, 0)
    if depth > 1:
        settle(jnp.int32(planes - 1))

    tokens = planes * 2 * share
    outs = (gate_out, upward_out, down_out)
    for i, (left, right) in enumerate(((rows, gates), (rows, ups), (grads, acts))):

        def weigh(j, _, i=i, left=left, right=right):
            at = pl.ds(pl.multiple_of(j * STEP_COLUMNS, STEP_COLUMNS), STEP_COLUMNS)
            value = product_tn(
                left[:, :, at].reshape(tokens, STEP_COLUMNS), right[...].reshape(tokens, units)
            )
            weights[i, at, :] = value.astype(weights.dtype)
            return 0

        lax.fori_loop(0, width // STEP_COLUMNS, weigh, 0)
        pltpu.make_async_copy(weights.at[i], outs[i], local.at[1 + i]).start()

    for i in range(3):
        pltpu.make_async_copy(weights.at[i], outs[i], local.at[1 + i]).wait()
    for k in range(planes):
        twin_copy(k).wait_send()
        if k >= planes - lanes:
            shipped(jnp.int32(k))
        if k:
            row_copy(k).wait_send()
            back_copy(k).wait_recv()


def feed_forward(half, pulls, gate, upward, down):
    planes = lax.axis_size("ctx") // PLANE
    depth, lanes = (2, planes) if planes <= 4 else (1, 2)
    share, width = half.shape
    units = gate.shape[1]
    low = jnp.bfloat16
    block = 2 * share
    some = pl.BlockSpec(memory_space=pl.ANY)
    dma = pltpu.SemaphoreType.DMA
    flops = 9 * 2 * planes * block * width * units
    return pl.pallas_call(
        partial(feed_kernel, planes, depth, lanes),
        out_shape=[jax.ShapeDtypeStruct((planes, share, width), low)] * 2
        + [jax.ShapeDtypeStruct((width, units), low)] * 3,
        in_specs=[some] * 5,
        out_specs=[some] * 5,
        scratch_shapes=[
            pltpu.VMEM((3, width, units), low),
            pltpu.VMEM((planes, block, width), low),
            pltpu.VMEM((planes, block, width), low),
        ]
        + [pltpu.VMEM((planes, block, units), low)] * 3
        + [
            pltpu.VMEM((depth, 2, share, width), jnp.float32),
            pltpu.VMEM((depth, 2, share, width), low),
            pltpu.VMEM((2, 2, share, width), low),
            pltpu.VMEM((lanes, 2, share, width), low),
            dma((4 + planes,)),
            dma((planes,)),
            dma((planes,)),
            dma((planes,)),
            dma((planes,)),
            dma((depth,)),
            dma((2,)),
            dma((planes,)),
            dma((planes,)),
            dma((planes,)),
        ],
        compiler_params=pltpu.CompilerParams(
            collective_id=3, has_side_effects=True, vmem_limit_bytes=62 * 2**20
        ),
        cost_estimate=pl.CostEstimate(
            flops=flops, bytes_accessed=8 * width * units * 2, transcendentals=0
        ),
    )(half, pulls, gate, upward, down)


def shards(
    tokens,
    cotangent,
    query_weight,
    query_first,
    query_second,
    keyval_weight,
    keyval_first,
    keyval_second,
    merge_weight,
    merge_first,
    merge_second,
    gate_weight,
    gate_first,
    gate_second,
    up_weight,
    up_first,
    up_second,
    down_weight,
    down_first,
    down_second,
    gains,
    gains_first,
    gains_second,
):
    low = jnp.bfloat16
    z, xy = place()
    s = lax.axis_index("shard")
    blocks = lax.axis_size("ctx")
    planes = blocks // PLANE
    row_count = tokens.shape[0]
    share = row_count // 2
    width = tokens.shape[1]

    def own_rows(value):
        return lax.dynamic_slice_in_dim(value, s * share, share, 0)

    small = jnp.concatenate([keyval_weight.astype(low), gains.astype(low)], axis=0).T
    small_mine = gather_small(small)
    small_other = swap(small_mine)
    small_all = jnp.stack(
        [jnp.where(s == 0, small_mine, small_other), jnp.where(s == 0, small_other, small_mine)],
        axis=1,
    ).reshape(width, -1)
    keyval_full = small_all[:, : 2 * HD]
    gain_used = small_all[:, 2 * HD :].T.astype(jnp.float32)

    query_full, merge_full, gate_full, upward_full, down_full = (
        w.reshape(width, -1)
        for w in gather_weights(
            [
                query_weight.astype(low),
                merge_weight.astype(low),
                unit_pieces(gate_weight),
                unit_pieces(up_weight),
                unit_pieces(down_weight),
            ],
            ("rows", "rows", "units", "units", "units"),
        )
    )
    out_grad_parts = fetch_tokens(own_rows(cotangent))

    offset = lax.axis_index("ctx") * row_count
    positions = offset + jnp.arange(row_count, dtype=jnp.int32)
    inputs = tokens.astype(jnp.float32)
    normed = normalize(inputs, gain_used[0]).astype(low)

    keyval = jnp.dot(normed, keyval_full, preferred_element_type=jnp.float32)
    keyval_used = jnp.stack([rotate(keyval[:, :HD], positions), keyval[:, HD:]]).astype(low)
    halo_planes = WINDOW // (PLANE * row_count)
    mine = pick(keyval_used, s)
    pile = jnp.stack([climb(mine, PLANE * k) for k in range(halo_planes, 0, -1)] + [mine])
    frame = jnp.zeros((halo_planes + 1, PLANE) + mine.shape, low)
    frame = put(frame, pile[:, None], 0, xy)
    for m in range(1, PLANE):
        frame = put(frame, hop(pile, m)[:, None], 0, xy ^ m)
    frame = frame.reshape(-1, HD)
    extent = WINDOW + row_count
    mine = lax.dynamic_slice_in_dim(frame, xy * row_count, extent, 0)
    other = swap(mine)
    key_part = jnp.where(s == 0, mine, other)
    value_part = jnp.where(s == 0, other, mine)

    query_lin = jnp.dot(normed, query_full, preferred_element_type=jnp.float32)
    head_count = query_lin.shape[1] // HD
    queries = (
        rotate(query_lin.reshape(row_count, head_count, HD).transpose(1, 0, 2), positions)
        * HD ** (-0.5)
    ).astype(low)
    key_pos = offset - WINDOW + jnp.arange(extent, dtype=jnp.int32)
    allowed = (
        (key_pos[None, :] <= positions[:, None])
        & (key_pos[None, :] > positions[:, None] - WINDOW)
        & (key_pos[None, :] >= 0)
    )
    scores = masked_scores(queries, key_part, allowed)
    row_peak = jnp.max(scores, axis=-1, keepdims=True)
    shifted = jnp.exp(scores - row_peak)
    row_total = jnp.sum(shifted, axis=-1, keepdims=True)
    log_total = row_peak + jnp.log(row_total)
    chances = (shifted / row_total).astype(low)
    mixed = jnp.einsum("hqk,kd->hqd", chances, value_part, preferred_element_type=jnp.float32)
    mixed_flat = mixed.transpose(1, 0, 2).reshape(row_count, head_count * HD).astype(low)
    branch = contract(mixed_flat, merge_full, 1, 1)
    branch_other = lax.dynamic_slice_in_dim(branch, (1 - s) * share, share, 0)
    input_rows = own_rows(inputs)
    hidden = input_rows + own_rows(branch) + swap(branch_other)
    inverse_two = inverse_rms(hidden)
    normed_two = (hidden * inverse_two * gain_used[1]).astype(low)

    out_grad_all = jnp.zeros((planes, row_count, width), low)
    for k in range(planes):
        out_grad_all = put(out_grad_all, whole_block(out_grad_parts[k])[None], z ^ k)
    backs, feeds, down_term, gate_term, upward_term = feed_forward(
        normed_two, out_grad_all, gate_full, upward_full, down_full
    )
    normtwo_grad = jnp.sum(backs.astype(jnp.float32), axis=0)
    gain_two_grad = jnp.sum(normtwo_grad * hidden * inverse_two, axis=0)
    norm_two_pull = jax.vjp(partial(normalize, gain_row=gain_used[1]), hidden)[1]
    hidden_grad = own_rows(cotangent).astype(jnp.float32) + norm_two_pull(normtwo_grad)[0]
    hidden_low = in_order(hidden_grad.astype(low))
    mixed_grad = jnp.dot(hidden_low, merge_full, preferred_element_type=jnp.float32)
    mixed_grad = mixed_grad.reshape(row_count, head_count, HD).transpose(1, 0, 2).astype(low)

    feed_sum = feeds[0].astype(jnp.float32)
    for k in range(1, planes):
        feed_sum = feed_sum + turn(feeds[k], -k).astype(jnp.float32)
    block_output = in_order((hidden + feed_sum).astype(low))

    chance_again = jnp.exp(masked_scores(queries, key_part, allowed) - log_total)
    chance_grad = jnp.einsum(
        "hqd,kd->hqk", mixed_grad, value_part, preferred_element_type=jnp.float32
    )
    row_inner = jnp.sum(chance_again * chance_grad, axis=-1, keepdims=True)
    score_low = (chance_again * (chance_grad - row_inner)).astype(low)
    key_grad = jnp.einsum("hqk,hqd->kd", score_low, queries, preferred_element_type=jnp.float32)
    value_grad = jnp.einsum(
        "hqk,hqd->kd", chance_again.astype(low), mixed_grad, preferred_element_type=jnp.float32
    )
    query_grad_full = jnp.einsum(
        "hqk,kd->hqd", score_low, key_part, preferred_element_type=jnp.float32
    )
    query_lin_grad = (
        rotate(query_grad_full * HD ** (-0.5), -positions)
        .transpose(1, 0, 2)
        .reshape(row_count, head_count * HD)
        .astype(low)
    )
    merge_reduced, query_reduced, down_reduced, gate_reduced, upward_reduced = reduce_weights(
        [
            as_blocks(contract(hidden_low, mixed_flat, 0, 0)),
            as_blocks(contract(normed, query_lin_grad, 0, 0)),
            as_blocks(down_term),
            as_blocks(gate_term),
            as_blocks(upward_term),
        ],
        ("rows", "rows", "units", "units", "units"),
    )
    down_reduced, gate_reduced, upward_reduced = (
        join_units(g) for g in (down_reduced, gate_reduced, upward_reduced)
    )

    mine = jnp.where(s == 0, key_grad, value_grad)
    other = jnp.where(s == 0, value_grad, key_grad).astype(low)
    mine = mine + swap(other).astype(jnp.float32)
    frame = put(jnp.zeros(((halo_planes + 1) * PLANE * row_count, HD), jnp.float32), mine, xy * row_count)
    frame = frame.reshape(halo_planes + 1, PLANE, row_count, HD)
    pile = pick(frame, xy, 1)
    for m in range(1, PLANE):
        pile = pile + hop(pick(frame, xy ^ m, 1).astype(low), m).astype(jnp.float32)
    mine = pile[halo_planes]
    for k in range(1, halo_planes + 1):
        mine = mine + climb(pile[halo_planes - k].astype(low), -PLANE * k).astype(jnp.float32)
    mine = jnp.where(s == 0, rotate(mine, -positions), mine).astype(low)
    other = swap(mine)
    keyval_lin = jnp.concatenate(
        [jnp.where(s == 0, mine, other), jnp.where(s == 0, other, mine)], axis=1
    )

    normed_columns = pick(normed.reshape(row_count, blocks, 2, -1), s, 2)
    keyval_term = contract(normed_columns.reshape(row_count, -1), keyval_lin, 0, 0)
    keyval_term = keyval_term.reshape(blocks, -1, 2 * HD)
    keyval_reduced = reduce_small(keyval_term, low).T

    normone_part = contract(query_lin_grad, query_full, 1, 1)
    normone_other = lax.dynamic_slice_in_dim(normone_part, (1 - s) * share, share, 0)
    normone_grad = (
        own_rows(normone_part)
        + swap(normone_other.astype(low)).astype(jnp.float32)
        + contract(own_rows(keyval_lin), keyval_full, 1, 1)
    )
    gain_one_grad = jnp.sum(normone_grad * input_rows * inverse_rms(input_rows), axis=0)
    norm_one_pull = jax.vjp(partial(normalize, gain_row=gain_used[0]), input_rows)[1]
    tokens_grad = in_order(hidden_grad + norm_one_pull(normone_grad)[0])

    gain_terms = jnp.stack([gain_one_grad, gain_two_grad]).reshape(2, blocks, 2, -1)
    gain_terms = gain_terms.transpose(2, 1, 0, 3)
    gain_sums = pick(gain_terms, s) + swap(pick(gain_terms, 1 - s))
    gains_reduced = reduce_small(gain_sums, jnp.float32)

    query_variance, query_updated = adamw(
        query_weight, query_first, query_second, query_reduced, 4.0 / math.sqrt(D)
    )
    keyval_variance, keyval_updated = adamw(
        keyval_weight, keyval_first, keyval_second, keyval_reduced, 2.0 / math.sqrt(D)
    )
    merge_variance, merge_updated = adamw(
        merge_weight, merge_first, merge_second, merge_reduced, 8.0 / math.sqrt(NH * HD)
    )
    gate_variance, gate_updated = adamw(
        gate_weight, gate_first, gate_second, gate_reduced, 2.0 / math.sqrt(D)
    )
    up_variance, up_updated = adamw(
        up_weight, up_first, up_second, upward_reduced, 2.0 / math.sqrt(D)
    )
    down_variance, down_updated = adamw(
        down_weight, down_first, down_second, down_reduced, 2.0 / math.sqrt(FF)
    )
    gains_variance, gains_updated = adamw(gains, gains_first, gains_second, gains_reduced, 0.8)
    return (
        block_output,
        tokens_grad,
        query_reduced,
        query_variance,
        query_updated,
        keyval_reduced,
        keyval_variance,
        keyval_updated,
        merge_reduced,
        merge_variance,
        merge_updated,
        gate_reduced,
        gate_variance,
        gate_updated,
        upward_reduced,
        up_variance,
        up_updated,
        down_reduced,
        down_variance,
        down_updated,
        gains_reduced,
        gains_variance,
        gains_updated,
    )


def solution(mesh):
    return jax.shard_map(
        shards,
        mesh=mesh,
        in_specs=(
            P("ctx", None),
            P("ctx", None),
            P("ctx", "shard"),
            P("ctx", "shard"),
            P("ctx", "shard"),
            P(None, ("ctx", "shard")),
            P(None, ("ctx", "shard")),
            P(None, ("ctx", "shard")),
            P("ctx", "shard"),
            P("ctx", "shard"),
            P("ctx", "shard"),
            P("ctx", "shard"),
            P("ctx", "shard"),
            P("ctx", "shard"),
            P("ctx", "shard"),
            P("ctx", "shard"),
            P("ctx", "shard"),
            P("ctx", "shard"),
            P("ctx", "shard"),
            P("ctx", "shard"),
            P(None, ("ctx", "shard")),
            P(None, ("ctx", "shard")),
            P(None, ("ctx", "shard")),
        ),
        out_specs=(
            P("ctx", None),
            P("ctx", None),
            P("ctx", "shard"),
            P("ctx", "shard"),
            P("ctx", "shard"),
            P(None, ("ctx", "shard")),
            P(None, ("ctx", "shard")),
            P(None, ("ctx", "shard")),
            P("ctx", "shard"),
            P("ctx", "shard"),
            P("ctx", "shard"),
            P("ctx", "shard"),
            P("ctx", "shard"),
            P("ctx", "shard"),
            P("ctx", "shard"),
            P("ctx", "shard"),
            P("ctx", "shard"),
            P("ctx", "shard"),
            P("ctx", "shard"),
            P("ctx", "shard"),
            P(None, ("ctx", "shard")),
            P(None, ("ctx", "shard")),
            P(None, ("ctx", "shard")),
        ),
        check_vma=False,
    )
```

```python
from functools import partial
import math

import jax
import jax.numpy as jnp
from jax import lax
from jax.experimental import pallas as pl
from jax.experimental.pallas import tpu as pltpu
from jax.sharding import PartitionSpec as P

D = 2560
NH = 10
HD = 256
FF = 7680
WINDOW = 2048
STEP = 10


beta_first = 0.9
beta_second = 0.95
adam_epsilon = 1e-08
weight_decay = 0.1
norm_epsilon = 1e-06
rotary_base = 10000.0
masked_score = -1e30


def inverse_rms(values):
    return lax.rsqrt(jnp.mean(values * values, axis=-1, keepdims=True) + norm_epsilon)


def normalize(values, gain_row):
    return values * inverse_rms(values) * gain_row


def gelu_product(gate_value, upward):
    return jax.nn.gelu(gate_value, approximate=True) * upward


def rotate(values, positions):
    quarter = values.shape[-1] // 4
    frequency = rotary_base ** (-jnp.arange(quarter, dtype=jnp.float32) / quarter)
    angles = positions.astype(jnp.float32)[:, None] * frequency[None, :]
    cosine = jnp.cos(angles)
    sine_part = jnp.sin(angles)
    lower_half = values[..., :quarter]
    upper_half = values[..., quarter : 2 * quarter]
    return jnp.concatenate(
        [
            lower_half * cosine - upper_half * sine_part,
            upper_half * cosine + lower_half * sine_part,
            values[..., 2 * quarter :],
        ],
        axis=-1,
    )


def rotary_tables(positions):
    quarter = HD // 4
    frequency = rotary_base ** (-jnp.arange(quarter, dtype=jnp.float32) / quarter)
    angles = positions.astype(jnp.float32)[:, None] * frequency[None, :]
    cosine, sine = jnp.cos(angles), jnp.sin(angles)
    return jnp.concatenate([cosine, cosine], axis=1), jnp.concatenate([-sine, sine], axis=1)


def contract(left, right, left_dim, right_dim):
    return lax.dot_general(
        left, right, (((left_dim,), (right_dim,)), ((), ())), preferred_element_type=jnp.float32
    )


def masked_scores(queries, key_part, allowed):
    scores = jnp.einsum("hqd,kd->hqk", queries, key_part, preferred_element_type=jnp.float32)
    return jnp.where(allowed[None], scores, masked_score)


def adamw(weight, first_moment, second_moment, gradient, rate_value):
    moment_new = beta_first * first_moment + (1.0 - beta_first) * gradient
    second_new = beta_second * second_moment + (1.0 - beta_second) * gradient * gradient
    step_size = (
        moment_new
        / (1.0 - beta_first**STEP)
        / (jnp.sqrt(second_new / (1.0 - beta_second**STEP)) + adam_epsilon)
    )
    return (second_new, weight - rate_value * (step_size + weight_decay * weight))


PLANE = 4


def hop(value, mask):
    count = lax.axis_size("ctx")
    return lax.ppermute(value, "ctx", [(i, i ^ mask) for i in range(count)])


def climb(value, by):
    count = lax.axis_size("ctx")
    return lax.ppermute(value, "ctx", [(i, i + by) for i in range(count) if 0 <= i + by < count])


def swap(value):
    count = lax.axis_size("shard")
    return lax.ppermute(value, "shard", [(i, count - 1 - i) for i in range(count)])


def place():
    me = lax.axis_index("ctx")
    return me // PLANE, me % PLANE


def turn(value, planes_up):
    count = lax.axis_size("ctx")
    step = PLANE * planes_up
    return lax.ppermute(value, "ctx", [(i, (i + step) % count) for i in range(count)])


def pick(value, index, axis=0):
    return lax.dynamic_index_in_dim(value, index, axis, keepdims=False)


def put(buffer, piece, *start):
    return lax.dynamic_update_slice(
        buffer, piece, tuple(start) + (0,) * (buffer.ndim - len(start))
    )


def reduce_column(column, kind=jnp.bfloat16):
    z, _ = place()
    total = pick(column, z)
    for k in range(1, column.shape[0]):
        total = total + hop(pick(column, z ^ k).astype(kind), PLANE * k).astype(jnp.float32)
    return total


def reduce_small(terms, kind):
    _, xy = place()
    split = terms.reshape((-1, PLANE) + terms.shape[1:])
    column = pick(split, xy, 1)
    for m in range(1, PLANE):
        column = column + hop(pick(split, xy ^ m, 1).astype(kind), m).astype(jnp.float32)
    return reduce_column(column, kind)


def unit_pieces(weight):
    planes = lax.axis_size("ctx") // PLANE
    units = weight.shape[1] // planes
    low = weight.astype(jnp.bfloat16)
    return jnp.stack([low[:, j * units : (j + 1) * units] for j in range(planes)])


def join_units(pieces):
    return jnp.concatenate([p.astype(jnp.float32) for p in pieces], axis=1)


def as_blocks(terms):
    blocks = lax.axis_size("ctx")
    return terms.astype(jnp.bfloat16).reshape(
        blocks // PLANE, PLANE, terms.shape[0] // blocks, terms.shape[1]
    )


def in_order(half):
    s = lax.axis_index("shard")
    other = swap(half)
    first = jnp.where(s == 0, half, other)
    last = jnp.where(s == 0, other, half)
    return jnp.concatenate([first, last], axis=0)


MESH = pl.DeviceIdType.MESH


def flip(index, mask):
    result = index
    bit = 1
    while bit <= mask:
        if mask & bit:
            result = result + bit * (1 - 2 * ((index // bit) % 2))
        bit *= 2
    return result


def greet(partners):
    barrier = pltpu.get_barrier_semaphore()
    for device in partners:
        pl.semaphore_signal(barrier, inc=1, device_id=device, device_id_type=MESH)
    pl.semaphore_wait(barrier, len(partners))


def send(source, target, sent, received, device):
    copy = pltpu.make_async_remote_copy(
        src_ref=source,
        dst_ref=target,
        send_sem=sent,
        recv_sem=received,
        device_id=device,
        device_id_type=MESH,
    )
    copy.start()
    return copy


def routes(planes, kz):
    return (1, 2) if kz < planes // 2 else (2, 1)


class Wires:
    def __init__(self, planes):
        self.planes = planes
        self.me = lax.axis_index("ctx")
        self.s = lax.axis_index("shard")
        self.z = self.me // PLANE
        self.xy = self.me % PLANE

    def across(self, mask):
        return (flip(self.me, mask), self.s)

    def twin(self):
        return (self.me, 1 - self.s)

    def partners(self):
        return [self.across(PLANE * k) for k in range(1, self.planes)] + [
            self.across(1),
            self.across(2),
        ]


def reduce_kernel(planes, kinds, *refs):
    count = len(kinds)
    terms, results = refs[:count], refs[count : 2 * count]
    rest = refs[2 * count :]
    far, near, own, pair, tops = (rest[j * count : (j + 1) * count] for j in range(5))
    local, sent, received, final_sent, final_received = rest[5 * count :]
    w = Wires(planes)
    z, xy = w.z, w.xy
    greet(w.partners())
    copies = []

    def term(i, kz, m):
        return terms[i].at[flip(z, kz), flip(xy, m)]

    def add(target, a, b):
        target[...] = (a[...].astype(jnp.float32) + b[...].astype(jnp.float32)).astype(target.dtype)

    loads = {}
    for i in range(count):
        for kz in range(planes):
            first, second = routes(planes, kz)
            for slot, m in ((0, 0), (1, first)):
                buffer = (own, pair)[slot][i].at[kz]
                loads[i, kz, slot] = pltpu.make_async_copy(
                    term(i, kz, m), buffer, local.at[i, kz, slot]
                )
                loads[i, kz, slot].start()

    def far_out(i, kz):
        first, second = routes(planes, kz)
        for slot, m in ((1, 3), (0, second)):
            copies.append(
                send(
                    term(i, kz, m),
                    far[i].at[kz, slot],
                    sent.at[i, kz, slot],
                    received.at[i, kz, slot],
                    w.across(second),
                )
            )

    def arrived(there, semaphore):
        pltpu.make_async_copy(there, there, semaphore).wait()

    def near_out(i, kz):
        first, second = routes(planes, kz)
        loads[i, kz, 1].wait()
        arrived(far[i].at[kz, 1], received.at[i, kz, 1])
        add(pair[i].at[kz], pair[i].at[kz], far[i].at[kz, 1])
        copies.append(
            send(
                pair[i].at[kz],
                near[i].at[kz],
                sent.at[i, kz, 2],
                received.at[i, kz, 2],
                w.across(first),
            )
        )
        loads[i, kz, 0].wait()
        arrived(far[i].at[kz, 0], received.at[i, kz, 0])

    def column_out(i, kz):
        arrived(near[i].at[kz], received.at[i, kz, 2])
        total = (
            own[i][kz].astype(jnp.float32)
            + far[i][kz, 0].astype(jnp.float32)
            + near[i][kz].astype(jnp.float32)
        )
        own[i][kz] = total.astype(own[i].dtype)
        if kz == 0:
            return
        target = tops[i].at[kz - 1] if kinds[i] == "rows" else results[i].at[z]
        copies.append(
            send(
                own[i].at[kz],
                target,
                final_sent.at[i, kz],
                final_received.at[i, kz],
                w.across(PLANE * kz),
            )
        )

    keeps = []

    def finish(i):
        if kinds[i] == "rows":
            total = own[i][0].astype(jnp.float32)
            for k in range(1, planes):
                arrived(tops[i].at[k - 1], final_received.at[i, k])
                total = total + tops[i][k - 1].astype(jnp.float32)
            results[i][...] = total
        else:
            keep = pltpu.make_async_copy(own[i].at[0], results[i].at[z], final_sent.at[i, 0])
            keep.start()
            keeps.append(keep)
            for k in range(1, planes):
                arrived(results[i].at[flip(z, k)], final_received.at[i, k])

    order = [(i, kz) for i in range(count) for kz in list(range(1, planes)) + [0]]
    ahead = planes
    for step in range(ahead):
        far_out(*order[step])
    for step, at in enumerate(order):
        if step + ahead < len(order):
            far_out(*order[step + ahead])
        near_out(*at)
        if step >= 1:
            column_out(*order[step - 1])
    column_out(*order[-1])
    for i in range(count):
        finish(i)
    for copy in copies:
        copy.wait_send()
    for keep in keeps:
        keep.wait()


def reduce_weights(terms, kinds):
    planes = lax.axis_size("ctx") // PLANE
    count = len(terms)
    low = jnp.bfloat16
    shapes, specs, tops = [], [], []
    for t, kind in zip(terms, kinds):
        rows, width = t.shape[-2:]
        if kind == "rows":
            shapes.append(jax.ShapeDtypeStruct((rows, width), jnp.float32))
            specs.append(pl.BlockSpec(memory_space=pltpu.VMEM))
            tops.append(pltpu.VMEM((planes - 1, rows, width), low))
        else:
            shapes.append(jax.ShapeDtypeStruct((planes, rows, width), low))
            specs.append(pl.BlockSpec(memory_space=pl.ANY))
            tops.append(pltpu.VMEM((1, 8, 128), low))
    return pl.pallas_call(
        partial(reduce_kernel, planes, kinds),
        out_shape=shapes,
        in_specs=[pl.BlockSpec(memory_space=pl.ANY)] * count,
        out_specs=specs,
        scratch_shapes=[pltpu.VMEM((planes, 2) + t.shape[-2:], low) for t in terms]
        + [pltpu.VMEM((planes,) + t.shape[-2:], low) for t in terms] * 3
        + tops
        + [
            pltpu.SemaphoreType.DMA((count, planes, 2)),
            pltpu.SemaphoreType.DMA((count, planes, 3)),
            pltpu.SemaphoreType.DMA((count, planes, 3)),
            pltpu.SemaphoreType.DMA((count, planes)),
            pltpu.SemaphoreType.DMA((count, planes)),
        ],
        compiler_params=pltpu.CompilerParams(
            collective_id=2, has_side_effects=True, vmem_limit_bytes=56 * 2**20
        ),
    )(*terms)


def gelu_parts(u):
    scale = math.sqrt(2.0 / math.pi)
    square = u * u
    bend = jnp.tanh(scale * u * (1.0 + 0.044715 * square))
    half = 0.5 * (1.0 + bend)
    slope = half + 0.5 * u * (1.0 - bend * bend) * scale * (1.0 + 3.0 * 0.044715 * square)
    return u * half, slope


def product_nt(left, right):
    return lax.dot_general(
        left, right, (((1,), (1,)), ((), ())), preferred_element_type=jnp.float32
    )


def product_tn(left, right):
    return lax.dot_general(
        left, right, (((0,), (0,)), ((), ())), preferred_element_type=jnp.float32
    )


class Spread:
    def __init__(self, w, kind, source, whole, semaphores):
        self.w, self.kind, self.source = w, kind, source
        self.own_sem, self.sent, self.received, *twin = semaphores
        self.everything = whole
        self.whole = whole.at[w.s] if kind == "pair" else whole
        self.twin = twin
        self.copies = []
        self.keep = pltpu.make_async_copy(self.mine(0), self.spot(0, 0), self.own_sem.at[0])

    def mine(self, k):
        return self.source.at[flip(self.w.z, k)] if self.kind == "units" else self.source

    def spot(self, kz, m):
        return self.whole.at[flip(self.w.z, kz), flip(self.w.xy, m)]

    def push(self, kz, m, slot, source, target, device):
        self.copies.append(
            send(source, target, self.sent.at[slot, kz], self.received.at[kz, m], device)
        )

    def wait_for(self, kz, m):
        there = self.spot(kz, m)
        pltpu.make_async_copy(there, there, self.received.at[kz, m]).wait()
        if self.kind == "pair":
            self.hand_over(kz, m, there)

    def hand_over(self, kz, m, piece):
        self.copies.append(
            send(
                piece,
                self.spot(kz, m),
                self.twin[0].at[kz, m],
                self.twin[1].at[kz, m],
                self.w.twin(),
            )
        )

    def rise(self):
        self.keep.start()
        if self.kind == "pair":
            self.hand_over(0, 0, self.source)
        for k in range(1, self.w.planes):
            self.push(k, 0, 0, self.mine(k), self.spot(0, 0), self.w.across(PLANE * k))

    def spread(self, kz):
        first, second = routes(self.w.planes, kz)
        if kz:
            self.wait_for(kz, 0)
        mine = self.spot(kz, 0) if kz else self.mine(0)
        self.push(kz, first, 1, mine, self.spot(kz, 0), self.w.across(first))
        self.push(kz, second, 2, mine, self.spot(kz, 0), self.w.across(second))

    def relay(self, kz):
        first, second = routes(self.w.planes, kz)
        self.wait_for(kz, first)
        there = self.spot(kz, first)
        self.push(kz, 3, 3, there, there, self.w.across(second))

    def settle(self):
        planes = self.w.planes
        for kz in range(planes):
            first, second = routes(planes, kz)
            self.wait_for(kz, second)
            self.wait_for(kz, 3)
        self.keep.wait()

    def close(self):
        if self.kind == "pair":
            for kz in range(self.w.planes):
                for m in range(PLANE):
                    there = self.everything.at[
                        1 - self.w.s, flip(self.w.z, kz), flip(self.w.xy, m)
                    ]
                    pltpu.make_async_copy(there, there, self.twin[1].at[kz, m]).wait()
        for copy in self.copies:
            copy.wait_send()

    def steps(self):
        for kz in range(1, self.w.planes):
            yield partial(self.spread, kz)
            yield partial(self.relay, kz - 1)
        yield partial(self.relay, self.w.planes - 1)
        yield self.settle


def spread_semaphores(planes, kind):
    dma = pltpu.SemaphoreType.DMA
    kinds = [dma((1,)), dma((4, planes)), dma((planes, PLANE))]
    return kinds + [dma((planes, PLANE))] * 2 if kind == "pair" else kinds


class Column:
    def __init__(self, w, half, whole, semaphores):
        self.w, self.half, self.whole = w, half, whole
        self.own_sem, self.sent, self.received, self.twin_sent, self.twin_received = semaphores
        self.share = half.shape[0]
        self.keep = pltpu.make_async_copy(half, self.spot(0, 0), self.own_sem.at[0])
        self.copies = []

    def spot(self, k, part):
        return self.whole.at[flip(self.w.z, k), pl.ds(part * self.share, self.share)]

    def rise(self, k):
        self.copies.append(
            send(
                self.half,
                self.spot(0, 0),
                self.sent.at[k],
                self.received.at[k],
                self.w.across(PLANE * k),
            )
        )

    def hand_over(self, k):
        if k:
            there = self.spot(k, 0)
            pltpu.make_async_copy(there, there, self.received.at[k]).wait()
        self.copies.append(
            send(
                self.spot(k, 0) if k else self.half,
                self.spot(k, 1),
                self.twin_sent.at[k],
                self.twin_received.at[k],
                self.w.twin(),
            )
        )

    def close(self):
        self.keep.wait()
        for k in range(self.w.planes):
            there = self.spot(k, 1)
            pltpu.make_async_copy(there, there, self.twin_received.at[k]).wait()
        for copy in self.copies:
            copy.wait_send()


def column_semaphores(planes):
    return [pltpu.SemaphoreType.DMA((1,))] + [pltpu.SemaphoreType.DMA((planes,))] * 4


def split(refs, sizes):
    at, groups = 0, []
    for size in sizes:
        groups.append(refs[at : at + size])
        at += size
    return groups


def open_kernel(planes, small, weight, half, small_out, weight_out, half_out, *semaphores):
    w = Wires(planes)
    ours, theirs, rows = split(semaphores, (5, 3, 5))
    greet(w.partners() + [w.twin()])
    first = Spread(w, "pair", small, small_out, ours)
    second = Spread(w, "rows", weight, weight_out, theirs)
    column = Column(w, half, half_out, rows)
    first.rise()
    first.spread(0)
    second.rise()
    second.spread(0)
    for step in first.steps():
        step()
    column.keep.start()
    column.hand_over(0)
    later = list(second.steps())
    for k, step in enumerate(later):
        step()
        if k % 2 == 0 and 1 <= k // 2 + 1 < planes:
            column.rise(k // 2 + 1)
    for k in range(1, planes):
        column.hand_over(k)
    for part in (first, second, column):
        part.close()


def open_gather(small, weight, half):
    planes = lax.axis_size("ctx") // PLANE
    some = pl.BlockSpec(memory_space=pl.ANY)
    return pl.pallas_call(
        partial(open_kernel, planes),
        out_shape=[
            jax.ShapeDtypeStruct((2, planes, PLANE) + small.shape, small.dtype),
            jax.ShapeDtypeStruct((planes, PLANE) + weight.shape, weight.dtype),
            jax.ShapeDtypeStruct((planes, 2 * half.shape[0], half.shape[1]), half.dtype),
        ],
        in_specs=[some] * 3,
        out_specs=[some] * 3,
        scratch_shapes=spread_semaphores(planes, "pair")
        + spread_semaphores(planes, "rows")
        + column_semaphores(planes),
        compiler_params=pltpu.CompilerParams(collective_id=1, has_side_effects=True),
    )(small, weight, half)


class Halo:
    def __init__(self, w, mine, frame, reach, semaphores):
        self.w, self.mine, self.frame, self.reach = w, mine, frame, reach
        (
            self.own_sem,
            self.climb_sent,
            self.climb_received,
            self.sent,
            self.received,
            self.twin_sent,
            self.twin_received,
        ) = semaphores

    def there(self, back):
        return self.w.z >= back

    def spot(self, back, m, part=None):
        part = self.w.s if part is None else part
        return self.frame.at[part, self.rows(back, flip(self.w.xy, m))]

    def rows(self, back, xy):
        block = self.mine.shape[0]
        start = ((self.reach - back) * PLANE + xy) * block
        return pl.ds(pl.multiple_of(start, block), block)

    def keep(self):
        return pltpu.make_async_copy(self.mine, self.spot(0, 0), self.own_sem.at[0])

    def climb(self, back):
        w = self.w
        return pltpu.make_async_remote_copy(
            src_ref=self.mine,
            dst_ref=self.spot(back, 0),
            send_sem=self.climb_sent.at[back],
            recv_sem=self.climb_received.at[back],
            device_id=(lax.rem(w.me + PLANE * back, PLANE * w.planes), w.s),
            device_id_type=MESH,
        )

    def cross(self, back, m):
        return pltpu.make_async_remote_copy(
            src_ref=self.spot(back, 0),
            dst_ref=self.spot(back, 0),
            send_sem=self.sent.at[back, m],
            recv_sem=self.received.at[back, m],
            device_id=self.w.across(m),
            device_id_type=MESH,
        )

    def hand_over(self, back, m):
        return pltpu.make_async_remote_copy(
            src_ref=self.spot(back, m),
            dst_ref=self.spot(back, m),
            send_sem=self.twin_sent.at[back, m],
            recv_sem=self.twin_received.at[back, m],
            device_id=self.w.twin(),
            device_id_type=MESH,
        )

    def begin(self):
        w = self.w
        self.keep().start()
        for back in range(1, self.reach + 1):

            @pl.when(w.z + back < w.planes)
            def _(back=back):
                self.climb(back).start()

            @pl.when(w.z < back)
            def _(back=back):
                block = self.mine.shape[0]
                empty = jnp.zeros((2, PLANE * block, HD), self.frame.dtype)
                self.frame[:, pl.ds((self.reach - back) * PLANE * block, PLANE * block)] = empty

        self.keep().wait()
        self.share(0)

    def share(self, back):
        for m in range(1, PLANE):
            self.cross(back, m).start()
        self.hand_over(back, 0).start()

    def forward(self, back):
        @pl.when(self.there(back))
        def _():
            self.climb(back).wait_recv()
            self.share(back)

    def collect(self, back):
        @pl.when(self.there(back))
        def _():
            for m in range(1, PLANE):
                self.cross(back, m).wait_recv()
                self.hand_over(back, m).start()

    def settle(self, back):
        @pl.when(self.there(back))
        def _():
            for m in range(PLANE):
                landed = self.spot(back, m, 1 - self.w.s)
                pltpu.make_async_copy(landed, landed, self.twin_received.at[back, m]).wait()

    def close(self):
        for back in range(self.reach + 1):

            @pl.when(self.there(back))
            def _(back=back):
                for m in range(PLANE):
                    if m:
                        self.cross(back, m).wait_send()
                    self.hand_over(back, m).wait_send()

            if back:

                @pl.when(self.w.z + back < self.w.planes)
                def _(back=back):
                    self.climb(back).wait_send()


def halo_semaphores(reach):
    dma = pltpu.SemaphoreType.DMA
    return [dma((1,))] + [dma((reach + 1,))] * 2 + [dma((reach + 1, PLANE))] * 4


def turned(value, cosine, sine):
    front = value[:, : HD // 2]
    rolled = pltpu.roll(front, HD // 4, 1)
    return jnp.concatenate([front * cosine + rolled * sine, value[:, HD // 2 :]], axis=1)


QUERY_ROWS = 128


def window_mask(first_row, rows, extent, key_floor):
    i = lax.broadcasted_iota(jnp.int32, (rows, extent), 0) + first_row
    j = lax.broadcasted_iota(jnp.int32, (rows, extent), 1)
    return (j > i) & (j <= i + WINDOW) & (j >= key_floor)


def flat_rows(pieces):
    width = pieces.shape[-1]
    if pieces.shape[-2] % 16:
        return pieces.astype(jnp.float32).reshape(-1, width).astype(pieces.dtype)
    return pieces.reshape(-1, width)


def planes_at_once(planes, rows):
    group = 1
    while group * PLANE * rows % 128:
        group *= 2
    return min(group, planes)


def front_kernel(
    planes,
    normed,
    query_weight,
    keyval,
    cosine,
    sine,
    inputs,
    gain,
    merge,
    gate,
    upward,
    down,
    merge_out,
    gate_out,
    upward_out,
    down_out,
    rows_out,
    queries,
    key_out,
    value_out,
    mixed,
    log_total,
    hidden,
    query_full,
    merge_full,
    frame,
    branch,
    arrived,
    normed_two,
    local,
    pair_sem,
    *semaphores,
):
    w = Wires(planes)
    parts = split(semaphores, (3, 3, 3, 3, 5, 7))
    count = queries.shape[0]
    block, width = normed.shape
    share = block // 2
    reach = WINDOW // (PLANE * block)
    extent = WINDOW + block
    low = jnp.bfloat16
    greet(w.partners() + [w.across(3), w.twin()])
    load = pltpu.make_async_copy(query_weight, query_full, local.at[0])
    load.start()
    project = Spread(w, "rows", merge, merge_full, parts[0])
    spreads = [
        Spread(w, "units", source, whole, sems)
        for source, whole, sems in zip(
            (gate, upward, down), (gate_out, upward_out, down_out), parts[1:4]
        )
    ]
    column = Column(w, normed_two, rows_out, parts[4])
    halo = Halo(w, keyval, frame, reach, parts[5])
    halo.begin()
    project.rise()
    project.spread(0)
    spreads[0].spread(0)

    steps = list(project.steps())
    steps.insert(4, spreads[0].rise)
    steps.insert(6, partial(spreads[1].spread, 0))
    steps.insert(8, spreads[1].rise)
    later = list(spreads[0].steps())[:-1]
    later += [partial(spreads[2].spread, 0), spreads[2].rise]
    for part in spreads[1:]:
        later += list(part.steps())[:-1]

    def move(many=1):
        for _ in range(many):
            if steps:
                steps.pop(0)()

    load.wait()
    for h in range(count):
        columns = slice(h * HD, (h + 1) * HD)
        value = jnp.dot(normed[...], query_full[:, columns], preferred_element_type=jnp.float32)
        queries[h] = (turned(value, cosine[...], sine[...]) * HD ** (-0.5)).astype(low)
    for back in range(1, reach + 1):
        halo.forward(back)
    move()
    for back in range(reach + 1):
        halo.collect(back)
    move()
    for back in range(reach + 1):
        halo.settle(back)

    window = pl.ds(pl.multiple_of(w.xy * block, block), extent)
    key_out[...] = frame[0, window]
    value_out[...] = frame[1, window]
    key_floor = WINDOW - w.me * block
    for h in range(count):
        for start in range(0, block, QUERY_ROWS):
            rows = pl.ds(start, QUERY_ROWS)
            scores = product_nt(queries[h, rows], key_out[...])
            allowed = window_mask(start, QUERY_ROWS, extent, key_floor)
            scores = jnp.where(allowed, scores, masked_score)
            peak = jnp.max(scores, axis=-1, keepdims=True)
            shifted = jnp.exp(scores - peak)
            total = jnp.sum(shifted, axis=-1, keepdims=True)
            log_total[h, rows] = peak + jnp.log(total)
            chances = (shifted / total).astype(low)
            value = jnp.dot(chances, value_out[...], preferred_element_type=jnp.float32)
            mixed[rows, h * HD : (h + 1) * HD] = value.astype(low)
            move()
    move(len(steps))
    keep = pltpu.make_async_copy(merge_full, merge_out, local.at[1])
    keep.start()

    group = planes_at_once(planes, merge_full.shape[2])
    columns = group * PLANE * merge_full.shape[2]
    for j in range(planes // group):
        piece = flat_rows(merge_full[j * group : (j + 1) * group])
        branch[:, j * columns : (j + 1) * columns] = product_nt(mixed[...], piece)
    ours = pl.ds(pl.multiple_of(w.s * share, share), share)
    other = pl.ds(pl.multiple_of((1 - w.s) * share, share), share)
    pair = pltpu.make_async_remote_copy(
        src_ref=branch.at[other],
        dst_ref=arrived,
        send_sem=pair_sem.at[0],
        recv_sem=pair_sem.at[1],
        device_id=w.twin(),
        device_id_type=MESH,
    )
    pair.start()
    steps = later
    move(2)
    pair.wait_recv()
    value = inputs[...].astype(jnp.float32) + branch[ours] + arrived[...]
    hidden[...] = value
    inverse = lax.rsqrt(jnp.mean(value * value, axis=-1, keepdims=True) + norm_epsilon)
    normed_two[...] = (value * inverse * gain[...]).astype(low)
    column.keep.start()
    column.hand_over(0)
    for k in range(1, planes):
        column.rise(k)
    move(len(steps))
    for part in spreads:
        part.settle()
    for k in range(1, planes):
        column.hand_over(k)
    pair.wait_send()
    keep.wait()
    for part in (project, *spreads, column, halo):
        part.close()


def front(normed, query_weight, keyval, cosine, sine, inputs, gain, merge, gate, upward, down):
    planes = lax.axis_size("ctx") // PLANE
    block, width = normed.shape
    share = block // 2
    heads = query_weight.shape[1] // HD
    reach = WINDOW // (PLANE * block)
    extent = WINDOW + block
    low = jnp.bfloat16
    some, near = pl.BlockSpec(memory_space=pl.ANY), pl.BlockSpec(memory_space=pltpu.VMEM)
    whole = lambda piece: jax.ShapeDtypeStruct((planes, PLANE) + piece.shape[-2:], low)
    dma = pltpu.SemaphoreType.DMA
    return pl.pallas_call(
        partial(front_kernel, planes),
        out_shape=[whole(p) for p in (merge, gate, upward, down)]
        + [
            jax.ShapeDtypeStruct((planes, block, width), low),
            jax.ShapeDtypeStruct((heads, block, HD), low),
            jax.ShapeDtypeStruct((extent, HD), low),
            jax.ShapeDtypeStruct((extent, HD), low),
            jax.ShapeDtypeStruct((block, heads * HD), low),
            jax.ShapeDtypeStruct((heads, block, 1), jnp.float32),
            jax.ShapeDtypeStruct((share, width), jnp.float32),
        ],
        in_specs=[near, some, some, near, near, near, near] + [some] * 4,
        out_specs=[some] * 5 + [near] * 6,
        scratch_shapes=[
            pltpu.VMEM(query_weight.shape, low),
            pltpu.VMEM((planes, PLANE) + merge.shape, low),
            pltpu.VMEM((2, (reach + 1) * PLANE * block, HD), low),
            pltpu.VMEM((block, width), jnp.float32),
            pltpu.VMEM((share, width), jnp.float32),
            pltpu.VMEM((share, width), low),
            dma((2,)),
            dma((2,)),
        ]
        + spread_semaphores(planes, "rows")
        + spread_semaphores(planes, "units") * 3
        + column_semaphores(planes)
        + halo_semaphores(reach),
        compiler_params=pltpu.CompilerParams(
            collective_id=4, has_side_effects=True, vmem_limit_bytes=60 * 2**20
        ),
    )(normed, query_weight, keyval, cosine, sine, inputs, gain, merge, gate, upward, down)


STEP_COLUMNS = 256


def feed_kernel(
    planes,
    depth,
    lanes,
    tokens,
    pulls,
    gate,
    upward,
    down,
    back_out,
    feed_out,
    down_out,
    gate_out,
    upward_out,
    weights,
    rows,
    grads,
    acts,
    gates,
    ups,
    own,
    outgoing,
    incoming,
    sums,
    local,
    row_local,
    pair_sent,
    pair_received,
    back_sent,
    back_received,
    feed_local,
):
    w = Wires(planes)
    z = w.z
    share, width = tokens.shape[1] // 2, tokens.shape[2]
    units = weights.shape[2]

    def plane(index):
        return (lax.rem(index + planes, planes) * PLANE + w.xy, w.s)

    greet([plane(z + k) for k in range(1, planes)] + [w.twin()])

    def pair_copy(k):
        return pltpu.make_async_remote_copy(
            src_ref=outgoing.at[lax.rem(k, depth)],
            dst_ref=incoming.at[lax.rem(k, 2)],
            send_sem=pair_sent.at[lax.rem(k, depth)],
            recv_sem=pair_received.at[lax.rem(k, 2)],
            device_id=w.twin(),
            device_id_type=MESH,
        )

    def back_copy(turn):
        k = turn + 1
        return pltpu.make_async_remote_copy(
            src_ref=sums.at[lax.rem(turn, lanes), 0],
            dst_ref=back_out.at[k],
            send_sem=back_sent.at[k],
            recv_sem=back_received.at[k],
            device_id=plane(z - k),
            device_id_type=MESH,
        )

    def kept_copy(turn):
        return pltpu.make_async_copy(
            sums.at[lax.rem(turn, lanes), 0], back_out.at[0], back_sent.at[0]
        )

    def feed_copy(turn):
        return pltpu.make_async_copy(
            sums.at[lax.rem(turn, lanes), 1],
            feed_out.at[lax.rem(turn + 1, planes)],
            feed_local.at[turn],
        )

    def shipped(turn):
        feed_copy(turn).wait()

        @pl.when(turn == planes - 1)
        def _():
            kept_copy(turn).wait()

        @pl.when(turn < planes - 1)
        def _():
            back_copy(turn).wait_send()

    loads = [
        pltpu.make_async_copy(source, weights.at[i], local.at[i])
        for i, source in enumerate((gate, upward, down))
    ]
    for load in loads:
        load.start()

    def load_rows(k):
        at = lax.rem(z - k + planes, planes)
        return (
            pltpu.make_async_copy(tokens.at[at], rows.at[k], row_local.at[k, 0]),
            pltpu.make_async_copy(pulls.at[at], grads.at[k], row_local.at[k, 1]),
        )

    for k in range(planes):
        for load in load_rows(k):
            load.start()
    for load in loads:
        load.wait()

    def compute(k, slot):
        for at in range(0, units, STEP_COLUMNS):
            columns = slice(at, min(at + STEP_COLUMNS, units))
            here = rows[k]
            gate_value = jnp.dot(here, weights[0, :, columns], preferred_element_type=jnp.float32)
            up_value = jnp.dot(here, weights[1, :, columns], preferred_element_type=jnp.float32)
            pull = jnp.dot(grads[k], weights[2, :, columns], preferred_element_type=jnp.float32)
            bent, slope = gelu_parts(gate_value)
            acts[k, :, columns] = (bent * up_value).astype(acts.dtype)
            gates[k, :, columns] = (pull * up_value * slope).astype(gates.dtype)
            ups[k, :, columns] = (pull * bent).astype(ups.dtype)

        def part(j, _):
            at = pl.ds(pl.multiple_of(j * STEP_COLUMNS, STEP_COLUMNS), STEP_COLUMNS)
            back = product_nt(gates[k], weights[0, at, :]) + product_nt(ups[k], weights[1, at, :])
            feed = product_nt(acts[k], weights[2, at, :])
            for i, value in enumerate((back, feed)):
                own[slot, i, :, at] = value[:share]
                outgoing[slot, i, :, at] = value[share:].astype(outgoing.dtype)
            return 0

        lax.fori_loop(0, width // STEP_COLUMNS, part, 0)

    def settle(turn):
        pair = pair_copy(turn)
        pair.wait_recv()
        pair.wait_send()

        @pl.when(turn >= lanes)
        def _():
            shipped(turn - lanes)

        for i in range(2):
            arrived = incoming[lax.rem(turn, 2), i].astype(jnp.float32)
            total = own[lax.rem(turn, depth), i] + arrived
            sums[lax.rem(turn, lanes), i] = total.astype(sums.dtype)

        @pl.when(turn == planes - 1)
        def _():
            kept_copy(turn).start()

        @pl.when(turn < planes - 1)
        def _():
            back_copy(turn).start()

        feed_copy(turn).start()

    def step(turn, _):
        k = lax.rem(turn + 1, planes)
        for load in load_rows(k):
            load.wait()
        compute(k, lax.rem(turn, depth))
        if depth > 1:

            @pl.when(turn > 0)
            def _():
                settle(turn - 1)

        pair_copy(turn).start()
        if depth == 1:
            settle(turn)
        return 0

    lax.fori_loop(0, planes, step, 0)
    if depth > 1:
        settle(jnp.int32(planes - 1))

    tokens = planes * 2 * share
    outs = (gate_out, upward_out, down_out)
    for i, (left, right) in enumerate(((rows, gates), (rows, ups), (grads, acts))):

        def weigh(j, _, i=i, left=left, right=right):
            at = pl.ds(pl.multiple_of(j * STEP_COLUMNS, STEP_COLUMNS), STEP_COLUMNS)
            value = product_tn(
                left[:, :, at].reshape(tokens, STEP_COLUMNS), right[...].reshape(tokens, units)
            )
            weights[i, at, :] = value.astype(weights.dtype)
            return 0

        lax.fori_loop(0, width // STEP_COLUMNS, weigh, 0)
        pltpu.make_async_copy(weights.at[i], outs[i], local.at[i]).start()

    for i in range(3):
        pltpu.make_async_copy(weights.at[i], outs[i], local.at[i]).wait()
    for turn in range(planes):
        if turn >= planes - lanes:
            shipped(jnp.int32(turn))
        if turn < planes - 1:
            back_copy(turn).wait_recv()


def feed_forward(tokens, pulls, gate, upward, down):
    planes = lax.axis_size("ctx") // PLANE
    depth, lanes = (2, planes) if planes <= 4 else (1, 2)
    share, width = tokens.shape[1] // 2, tokens.shape[2]
    units = gate.shape[1]
    low = jnp.bfloat16
    block = 2 * share
    some = pl.BlockSpec(memory_space=pl.ANY)
    dma = pltpu.SemaphoreType.DMA
    flops = 9 * 2 * planes * block * width * units
    return pl.pallas_call(
        partial(feed_kernel, planes, depth, lanes),
        out_shape=[jax.ShapeDtypeStruct((planes, share, width), low)] * 2
        + [jax.ShapeDtypeStruct((width, units), low)] * 3,
        in_specs=[some] * 5,
        out_specs=[some] * 5,
        scratch_shapes=[
            pltpu.VMEM((3, width, units), low),
            pltpu.VMEM((planes, block, width), low),
            pltpu.VMEM((planes, block, width), low),
        ]
        + [pltpu.VMEM((planes, block, units), low)] * 3
        + [
            pltpu.VMEM((depth, 2, share, width), jnp.float32),
            pltpu.VMEM((depth, 2, share, width), low),
            pltpu.VMEM((2, 2, share, width), low),
            pltpu.VMEM((lanes, 2, share, width), low),
            dma((3,)),
            dma((planes, 2)),
            dma((depth,)),
            dma((2,)),
            dma((planes,)),
            dma((planes,)),
            dma((planes,)),
        ],
        compiler_params=pltpu.CompilerParams(
            collective_id=3, has_side_effects=True, vmem_limit_bytes=62 * 2**20
        ),
        cost_estimate=pl.CostEstimate(
            flops=flops, bytes_accessed=8 * width * units * 2, transcendentals=0
        ),
    )(tokens, pulls, gate, upward, down)


def shards(
    tokens,
    cotangent,
    query_weight,
    query_first,
    query_second,
    keyval_weight,
    keyval_first,
    keyval_second,
    merge_weight,
    merge_first,
    merge_second,
    gate_weight,
    gate_first,
    gate_second,
    up_weight,
    up_first,
    up_second,
    down_weight,
    down_first,
    down_second,
    gains,
    gains_first,
    gains_second,
):
    low = jnp.bfloat16
    z, xy = place()
    s = lax.axis_index("shard")
    blocks = lax.axis_size("ctx")
    planes = blocks // PLANE
    row_count = tokens.shape[0]
    share = row_count // 2
    width = tokens.shape[1]

    def own_rows(value):
        return lax.dynamic_slice_in_dim(value, s * share, share, 0)

    small = jnp.concatenate([keyval_weight.astype(low), gains.astype(low)], axis=0).T
    small = jnp.pad(small, ((0, 0), (0, -small.shape[1] % 128)))
    small_all, query_full, pulls_all = open_gather(
        small, query_weight.astype(low), own_rows(cotangent)
    )
    small_all = small_all.transpose(1, 2, 0, 3, 4).reshape(width, -1)
    query_full = query_full.reshape(width, -1)
    keyval_full = small_all[:, : 2 * HD]
    gain_used = small_all[:, 2 * HD : 2 * HD + 2].T.astype(jnp.float32)

    offset = lax.axis_index("ctx") * row_count
    positions = offset + jnp.arange(row_count, dtype=jnp.int32)
    inputs = tokens.astype(jnp.float32)
    normed = normalize(inputs, gain_used[0]).astype(low)

    keyval = jnp.dot(normed, keyval_full, preferred_element_type=jnp.float32)
    keyval_mine = jnp.where(s == 0, rotate(keyval[:, :HD], positions), keyval[:, HD:]).astype(low)
    cosine, sine = rotary_tables(positions)
    (
        merge_full,
        gate_full,
        upward_full,
        down_full,
        normed_all,
        queries,
        key_part,
        value_part,
        mixed_flat,
        log_total,
        hidden,
    ) = front(
        normed,
        query_full,
        keyval_mine,
        cosine,
        sine,
        own_rows(tokens),
        gain_used[1:],
        merge_weight.astype(low),
        unit_pieces(gate_weight),
        unit_pieces(up_weight),
        unit_pieces(down_weight),
    )
    merge_full, gate_full, upward_full, down_full = (
        v.reshape(width, -1) for v in (merge_full, gate_full, upward_full, down_full)
    )
    head_count = queries.shape[0]
    extent = WINDOW + row_count
    halo_planes = WINDOW // (PLANE * row_count)
    key_pos = offset - WINDOW + jnp.arange(extent, dtype=jnp.int32)
    allowed = (
        (key_pos[None, :] <= positions[:, None])
        & (key_pos[None, :] > positions[:, None] - WINDOW)
        & (key_pos[None, :] >= 0)
    )
    input_rows = own_rows(inputs)
    inverse_two = inverse_rms(hidden)

    backs, feeds, down_term, gate_term, upward_term = feed_forward(
        normed_all, pulls_all, gate_full, upward_full, down_full
    )
    normtwo_grad = jnp.sum(backs.astype(jnp.float32), axis=0)
    gain_two_grad = jnp.sum(normtwo_grad * hidden * inverse_two, axis=0)
    norm_two_pull = jax.vjp(partial(normalize, gain_row=gain_used[1]), hidden)[1]
    hidden_grad = own_rows(cotangent).astype(jnp.float32) + norm_two_pull(normtwo_grad)[0]
    hidden_low = in_order(hidden_grad.astype(low))
    mixed_grad = jnp.dot(hidden_low, merge_full, preferred_element_type=jnp.float32)
    mixed_grad = mixed_grad.reshape(row_count, head_count, HD).transpose(1, 0, 2).astype(low)

    feed_sum = feeds[0].astype(jnp.float32)
    for k in range(1, planes):
        feed_sum = feed_sum + turn(feeds[k], -k).astype(jnp.float32)
    block_output = in_order((hidden + feed_sum).astype(low))

    chance_again = jnp.exp(masked_scores(queries, key_part, allowed) - log_total)
    chance_grad = jnp.einsum(
        "hqd,kd->hqk", mixed_grad, value_part, preferred_element_type=jnp.float32
    )
    row_inner = jnp.sum(chance_again * chance_grad, axis=-1, keepdims=True)
    score_low = (chance_again * (chance_grad - row_inner)).astype(low)
    key_grad = jnp.einsum("hqk,hqd->kd", score_low, queries, preferred_element_type=jnp.float32)
    value_grad = jnp.einsum(
        "hqk,hqd->kd", chance_again.astype(low), mixed_grad, preferred_element_type=jnp.float32
    )
    query_grad_full = jnp.einsum(
        "hqk,kd->hqd", score_low, key_part, preferred_element_type=jnp.float32
    )
    query_lin_grad = (
        rotate(query_grad_full * HD ** (-0.5), -positions)
        .transpose(1, 0, 2)
        .reshape(row_count, head_count * HD)
        .astype(low)
    )
    merge_reduced, query_reduced, down_reduced, gate_reduced, upward_reduced = reduce_weights(
        [
            as_blocks(contract(hidden_low, mixed_flat, 0, 0)),
            as_blocks(contract(normed, query_lin_grad, 0, 0)),
            as_blocks(down_term),
            as_blocks(gate_term),
            as_blocks(upward_term),
        ],
        ("rows", "rows", "units", "units", "units"),
    )
    down_reduced, gate_reduced, upward_reduced = (
        join_units(g) for g in (down_reduced, gate_reduced, upward_reduced)
    )

    mine = jnp.where(s == 0, key_grad, value_grad)
    other = jnp.where(s == 0, value_grad, key_grad).astype(low)
    mine = mine + swap(other).astype(jnp.float32)
    frame = put(jnp.zeros(((halo_planes + 1) * PLANE * row_count, HD), jnp.float32), mine, xy * row_count)
    frame = frame.reshape(halo_planes + 1, PLANE, row_count, HD)
    pile = pick(frame, xy, 1)
    for m in range(1, PLANE):
        pile = pile + hop(pick(frame, xy ^ m, 1).astype(low), m).astype(jnp.float32)
    mine = pile[halo_planes]
    for k in range(1, halo_planes + 1):
        mine = mine + climb(pile[halo_planes - k].astype(low), -PLANE * k).astype(jnp.float32)
    mine = jnp.where(s == 0, rotate(mine, -positions), mine).astype(low)
    other = swap(mine)
    keyval_lin = jnp.concatenate(
        [jnp.where(s == 0, mine, other), jnp.where(s == 0, other, mine)], axis=1
    )

    normed_columns = pick(normed.reshape(row_count, blocks, 2, -1), s, 2)
    keyval_term = contract(normed_columns.reshape(row_count, -1), keyval_lin, 0, 0)
    keyval_term = keyval_term.reshape(blocks, -1, 2 * HD)
    keyval_reduced = reduce_small(keyval_term, low).T

    normone_part = contract(query_lin_grad, query_full, 1, 1)
    normone_other = lax.dynamic_slice_in_dim(normone_part, (1 - s) * share, share, 0)
    normone_grad = (
        own_rows(normone_part)
        + swap(normone_other.astype(low)).astype(jnp.float32)
        + contract(own_rows(keyval_lin), keyval_full, 1, 1)
    )
    gain_one_grad = jnp.sum(normone_grad * input_rows * inverse_rms(input_rows), axis=0)
    norm_one_pull = jax.vjp(partial(normalize, gain_row=gain_used[0]), input_rows)[1]
    tokens_grad = in_order(hidden_grad + norm_one_pull(normone_grad)[0])

    gain_terms = jnp.stack([gain_one_grad, gain_two_grad]).reshape(2, blocks, 2, -1)
    gain_terms = gain_terms.transpose(2, 1, 0, 3)
    gain_sums = pick(gain_terms, s) + swap(pick(gain_terms, 1 - s))
    gains_reduced = reduce_small(gain_sums, jnp.float32)

    query_variance, query_updated = adamw(
        query_weight, query_first, query_second, query_reduced, 4.0 / math.sqrt(D)
    )
    keyval_variance, keyval_updated = adamw(
        keyval_weight, keyval_first, keyval_second, keyval_reduced, 2.0 / math.sqrt(D)
    )
    merge_variance, merge_updated = adamw(
        merge_weight, merge_first, merge_second, merge_reduced, 8.0 / math.sqrt(NH * HD)
    )
    gate_variance, gate_updated = adamw(
        gate_weight, gate_first, gate_second, gate_reduced, 2.0 / math.sqrt(D)
    )
    up_variance, up_updated = adamw(
        up_weight, up_first, up_second, upward_reduced, 2.0 / math.sqrt(D)
    )
    down_variance, down_updated = adamw(
        down_weight, down_first, down_second, down_reduced, 2.0 / math.sqrt(FF)
    )
    gains_variance, gains_updated = adamw(gains, gains_first, gains_second, gains_reduced, 0.8)
    return (
        block_output,
        tokens_grad,
        query_reduced,
        query_variance,
        query_updated,
        keyval_reduced,
        keyval_variance,
        keyval_updated,
        merge_reduced,
        merge_variance,
        merge_updated,
        gate_reduced,
        gate_variance,
        gate_updated,
        upward_reduced,
        up_variance,
        up_updated,
        down_reduced,
        down_variance,
        down_updated,
        gains_reduced,
        gains_variance,
        gains_updated,
    )


def solution(mesh):
    return jax.shard_map(
        shards,
        mesh=mesh,
        in_specs=(
            P("ctx", None),
            P("ctx", None),
            P("ctx", "shard"),
            P("ctx", "shard"),
            P("ctx", "shard"),
            P(None, ("ctx", "shard")),
            P(None, ("ctx", "shard")),
            P(None, ("ctx", "shard")),
            P("ctx", "shard"),
            P("ctx", "shard"),
            P("ctx", "shard"),
            P("ctx", "shard"),
            P("ctx", "shard"),
            P("ctx", "shard"),
            P("ctx", "shard"),
            P("ctx", "shard"),
            P("ctx", "shard"),
            P("ctx", "shard"),
            P("ctx", "shard"),
            P("ctx", "shard"),
            P(None, ("ctx", "shard")),
            P(None, ("ctx", "shard")),
            P(None, ("ctx", "shard")),
        ),
        out_specs=(
            P("ctx", None),
            P("ctx", None),
            P("ctx", "shard"),
            P("ctx", "shard"),
            P("ctx", "shard"),
            P(None, ("ctx", "shard")),
            P(None, ("ctx", "shard")),
            P(None, ("ctx", "shard")),
            P("ctx", "shard"),
            P("ctx", "shard"),
            P("ctx", "shard"),
            P("ctx", "shard"),
            P("ctx", "shard"),
            P("ctx", "shard"),
            P("ctx", "shard"),
            P("ctx", "shard"),
            P("ctx", "shard"),
            P("ctx", "shard"),
            P("ctx", "shard"),
            P("ctx", "shard"),
            P(None, ("ctx", "shard")),
            P(None, ("ctx", "shard")),
            P(None, ("ctx", "shard")),
        ),
        check_vma=False,
    )
```

```python
from functools import partial
import math

import jax
import jax.numpy as jnp
from jax import lax
from jax.experimental import pallas as pl
from jax.experimental.pallas import tpu as pltpu
from jax.sharding import PartitionSpec as P

D = 2560
NH = 10
HD = 256
FF = 7680
WINDOW = 2048
STEP = 10


beta_first = 0.9
beta_second = 0.95
adam_epsilon = 1e-08
weight_decay = 0.1
norm_epsilon = 1e-06
rotary_base = 10000.0
masked_score = -1e30


def inverse_rms(values):
    return lax.rsqrt(jnp.mean(values * values, axis=-1, keepdims=True) + norm_epsilon)


def normalize(values, gain_row):
    return values * inverse_rms(values) * gain_row


def gelu_product(gate_value, upward):
    return jax.nn.gelu(gate_value, approximate=True) * upward


def rotate(values, positions):
    quarter = values.shape[-1] // 4
    frequency = rotary_base ** (-jnp.arange(quarter, dtype=jnp.float32) / quarter)
    angles = positions.astype(jnp.float32)[:, None] * frequency[None, :]
    cosine = jnp.cos(angles)
    sine_part = jnp.sin(angles)
    lower_half = values[..., :quarter]
    upper_half = values[..., quarter : 2 * quarter]
    return jnp.concatenate(
        [
            lower_half * cosine - upper_half * sine_part,
            upper_half * cosine + lower_half * sine_part,
            values[..., 2 * quarter :],
        ],
        axis=-1,
    )


def rotary_tables(positions):
    quarter = HD // 4
    frequency = rotary_base ** (-jnp.arange(quarter, dtype=jnp.float32) / quarter)
    angles = positions.astype(jnp.float32)[:, None] * frequency[None, :]
    cosine, sine = jnp.cos(angles), jnp.sin(angles)
    return jnp.concatenate([cosine, cosine], axis=1), jnp.concatenate([-sine, sine], axis=1)


def contract(left, right, left_dim, right_dim):
    return lax.dot_general(
        left, right, (((left_dim,), (right_dim,)), ((), ())), preferred_element_type=jnp.float32
    )


def adamw(weight, first_moment, second_moment, gradient, rate_value):
    moment_new = beta_first * first_moment + (1.0 - beta_first) * gradient
    second_new = beta_second * second_moment + (1.0 - beta_second) * gradient * gradient
    step_size = (
        moment_new
        / (1.0 - beta_first**STEP)
        / (jnp.sqrt(second_new / (1.0 - beta_second**STEP)) + adam_epsilon)
    )
    return (second_new, weight - rate_value * (step_size + weight_decay * weight))


PLANE = 4


def hop(value, mask):
    count = lax.axis_size("ctx")
    return lax.ppermute(value, "ctx", [(i, i ^ mask) for i in range(count)])


def swap(value):
    count = lax.axis_size("shard")
    return lax.ppermute(value, "shard", [(i, count - 1 - i) for i in range(count)])


def place():
    me = lax.axis_index("ctx")
    return me // PLANE, me % PLANE


def pick(value, index, axis=0):
    return lax.dynamic_index_in_dim(value, index, axis, keepdims=False)


def put(buffer, piece, *start):
    return lax.dynamic_update_slice(
        buffer, piece, tuple(start) + (0,) * (buffer.ndim - len(start))
    )


def reduce_column(column, kind=jnp.bfloat16):
    z, _ = place()
    total = pick(column, z)
    for k in range(1, column.shape[0]):
        total = total + hop(pick(column, z ^ k).astype(kind), PLANE * k).astype(jnp.float32)
    return total


def reduce_small(terms, kind):
    _, xy = place()
    split = terms.reshape((-1, PLANE) + terms.shape[1:])
    column = pick(split, xy, 1)
    for m in range(1, PLANE):
        column = column + hop(pick(split, xy ^ m, 1).astype(kind), m).astype(jnp.float32)
    return reduce_column(column, kind)


def unit_pieces(weight):
    planes = lax.axis_size("ctx") // PLANE
    units = weight.shape[1] // planes
    low = weight.astype(jnp.bfloat16)
    return jnp.stack([low[:, j * units : (j + 1) * units] for j in range(planes)])


def join_units(pieces):
    return jnp.concatenate([p.astype(jnp.float32) for p in pieces], axis=1)


def in_order(half):
    s = lax.axis_index("shard")
    other = swap(half)
    first = jnp.where(s == 0, half, other)
    last = jnp.where(s == 0, other, half)
    return jnp.concatenate([first, last], axis=0)


MESH = pl.DeviceIdType.MESH


def flip(index, mask):
    result = index
    bit = 1
    while bit <= mask:
        if mask & bit:
            result = result + bit * (1 - 2 * ((index // bit) % 2))
        bit *= 2
    return result


def greet(partners):
    barrier = pltpu.get_barrier_semaphore()
    for device in partners:
        pl.semaphore_signal(barrier, inc=1, device_id=device, device_id_type=MESH)
    pl.semaphore_wait(barrier, len(partners))


def send(source, target, sent, received, device):
    copy = pltpu.make_async_remote_copy(
        src_ref=source,
        dst_ref=target,
        send_sem=sent,
        recv_sem=received,
        device_id=device,
        device_id_type=MESH,
    )
    copy.start()
    return copy


def routes(planes, kz):
    return (1, 2) if kz < planes // 2 else (2, 1)


class Wires:
    def __init__(self, planes):
        self.planes = planes
        self.me = lax.axis_index("ctx")
        self.s = lax.axis_index("shard")
        self.z = self.me // PLANE
        self.xy = self.me % PLANE

    def across(self, mask):
        return (flip(self.me, mask), self.s)

    def twin(self):
        return (self.me, 1 - self.s)

    def partners(self):
        return [self.across(PLANE * k) for k in range(1, self.planes)] + [
            self.across(1),
            self.across(2),
        ]


def gelu_parts(u):
    scale = math.sqrt(2.0 / math.pi)
    square = u * u
    bend = jnp.tanh(scale * u * (1.0 + 0.044715 * square))
    half = 0.5 * (1.0 + bend)
    slope = half + 0.5 * u * (1.0 - bend * bend) * scale * (1.0 + 3.0 * 0.044715 * square)
    return u * half, slope


def product_nt(left, right):
    return lax.dot_general(
        left, right, (((1,), (1,)), ((), ())), preferred_element_type=jnp.float32
    )


def product_tn(left, right):
    return lax.dot_general(
        left, right, (((0,), (0,)), ((), ())), preferred_element_type=jnp.float32
    )


class Spread:
    def __init__(self, w, kind, source, whole, semaphores):
        self.w, self.kind, self.source = w, kind, source
        self.own_sem, self.sent, self.received, *twin = semaphores
        self.everything = whole
        self.whole = whole.at[w.s] if kind == "pair" else whole
        self.twin = twin
        self.copies = []
        self.keep = pltpu.make_async_copy(self.mine(0), self.spot(0, 0), self.own_sem.at[0])

    def mine(self, k):
        return self.source.at[flip(self.w.z, k)] if self.kind == "units" else self.source

    def spot(self, kz, m):
        return self.whole.at[flip(self.w.z, kz), flip(self.w.xy, m)]

    def push(self, kz, m, slot, source, target, device):
        self.copies.append(
            send(source, target, self.sent.at[slot, kz], self.received.at[kz, m], device)
        )

    def wait_for(self, kz, m):
        there = self.spot(kz, m)
        pltpu.make_async_copy(there, there, self.received.at[kz, m]).wait()
        if self.kind == "pair":
            self.hand_over(kz, m, there)

    def hand_over(self, kz, m, piece):
        self.copies.append(
            send(
                piece,
                self.spot(kz, m),
                self.twin[0].at[kz, m],
                self.twin[1].at[kz, m],
                self.w.twin(),
            )
        )

    def rise(self):
        self.keep.start()
        if self.kind == "pair":
            self.hand_over(0, 0, self.source)
        for k in range(1, self.w.planes):
            self.push(k, 0, 0, self.mine(k), self.spot(0, 0), self.w.across(PLANE * k))

    def spread(self, kz):
        first, second = routes(self.w.planes, kz)
        if kz:
            self.wait_for(kz, 0)
        mine = self.spot(kz, 0) if kz else self.mine(0)
        self.push(kz, first, 1, mine, self.spot(kz, 0), self.w.across(first))
        self.push(kz, second, 2, mine, self.spot(kz, 0), self.w.across(second))

    def relay(self, kz):
        first, second = routes(self.w.planes, kz)
        self.wait_for(kz, first)
        there = self.spot(kz, first)
        self.push(kz, 3, 3, there, there, self.w.across(second))

    def settle(self):
        planes = self.w.planes
        for kz in range(planes):
            first, second = routes(planes, kz)
            self.wait_for(kz, second)
            self.wait_for(kz, 3)
        self.keep.wait()

    def close(self):
        if self.kind == "pair":
            for kz in range(self.w.planes):
                for m in range(PLANE):
                    there = self.everything.at[
                        1 - self.w.s, flip(self.w.z, kz), flip(self.w.xy, m)
                    ]
                    pltpu.make_async_copy(there, there, self.twin[1].at[kz, m]).wait()
        for copy in self.copies:
            copy.wait_send()

    def steps(self):
        for kz in range(1, self.w.planes):
            yield partial(self.spread, kz)
            yield partial(self.relay, kz - 1)
        yield partial(self.relay, self.w.planes - 1)
        yield self.settle


def spread_semaphores(planes, kind):
    dma = pltpu.SemaphoreType.DMA
    kinds = [dma((1,)), dma((4, planes)), dma((planes, PLANE))]
    return kinds + [dma((planes, PLANE))] * 2 if kind == "pair" else kinds


class Column:
    def __init__(self, w, half, whole, semaphores):
        self.w, self.half, self.whole = w, half, whole
        self.own_sem, self.sent, self.received, self.twin_sent, self.twin_received = semaphores
        self.share = half.shape[0]
        self.keep = pltpu.make_async_copy(half, self.spot(0, 0), self.own_sem.at[0])
        self.copies = []

    def spot(self, k, part):
        return self.whole.at[flip(self.w.z, k), pl.ds(part * self.share, self.share)]

    def rise(self, k):
        self.copies.append(
            send(
                self.half,
                self.spot(0, 0),
                self.sent.at[k],
                self.received.at[k],
                self.w.across(PLANE * k),
            )
        )

    def hand_over(self, k):
        if k:
            there = self.spot(k, 0)
            pltpu.make_async_copy(there, there, self.received.at[k]).wait()
        self.copies.append(
            send(
                self.spot(k, 0) if k else self.half,
                self.spot(k, 1),
                self.twin_sent.at[k],
                self.twin_received.at[k],
                self.w.twin(),
            )
        )

    def close(self):
        self.keep.wait()
        for k in range(self.w.planes):
            there = self.spot(k, 1)
            pltpu.make_async_copy(there, there, self.twin_received.at[k]).wait()
        for copy in self.copies:
            copy.wait_send()


def column_semaphores(planes):
    return [pltpu.SemaphoreType.DMA((1,))] + [pltpu.SemaphoreType.DMA((planes,))] * 4


def split(refs, sizes):
    at, groups = 0, []
    for size in sizes:
        groups.append(refs[at : at + size])
        at += size
    return groups


def open_kernel(planes, small, weight, half, small_out, weight_out, half_out, *semaphores):
    w = Wires(planes)
    ours, theirs, rows = split(semaphores, (5, 3, 5))
    greet(w.partners() + [w.twin()])
    first = Spread(w, "pair", small, small_out, ours)
    second = Spread(w, "rows", weight, weight_out, theirs)
    column = Column(w, half, half_out, rows)
    first.rise()
    first.spread(0)
    second.rise()
    second.spread(0)
    for step in first.steps():
        step()
    column.keep.start()
    column.hand_over(0)
    later = list(second.steps())
    for k, step in enumerate(later):
        step()
        if k % 2 == 0 and 1 <= k // 2 + 1 < planes:
            column.rise(k // 2 + 1)
    for k in range(1, planes):
        column.hand_over(k)
    for part in (first, second, column):
        part.close()


def open_gather(small, weight, half):
    planes = lax.axis_size("ctx") // PLANE
    some = pl.BlockSpec(memory_space=pl.ANY)
    return pl.pallas_call(
        partial(open_kernel, planes),
        out_shape=[
            jax.ShapeDtypeStruct((2, planes, PLANE) + small.shape, small.dtype),
            jax.ShapeDtypeStruct((planes, PLANE) + weight.shape, weight.dtype),
            jax.ShapeDtypeStruct((planes, 2 * half.shape[0], half.shape[1]), half.dtype),
        ],
        in_specs=[some] * 3,
        out_specs=[some] * 3,
        scratch_shapes=spread_semaphores(planes, "pair")
        + spread_semaphores(planes, "rows")
        + column_semaphores(planes),
        compiler_params=pltpu.CompilerParams(collective_id=1, has_side_effects=True),
    )(small, weight, half)


class Halo:
    def __init__(self, w, mine, frame, reach, semaphores):
        self.w, self.mine, self.frame, self.reach = w, mine, frame, reach
        (
            self.own_sem,
            self.climb_sent,
            self.climb_received,
            self.sent,
            self.received,
            self.twin_sent,
            self.twin_received,
        ) = semaphores

    def there(self, back):
        return self.w.z >= back

    def spot(self, back, m, part=None):
        part = self.w.s if part is None else part
        return self.frame.at[part, self.rows(back, flip(self.w.xy, m))]

    def rows(self, back, xy):
        block = self.mine.shape[0]
        start = ((self.reach - back) * PLANE + xy) * block
        return pl.ds(pl.multiple_of(start, block), block)

    def keep(self):
        return pltpu.make_async_copy(self.mine, self.spot(0, 0), self.own_sem.at[0])

    def climb(self, back):
        w = self.w
        return pltpu.make_async_remote_copy(
            src_ref=self.mine,
            dst_ref=self.spot(back, 0),
            send_sem=self.climb_sent.at[back],
            recv_sem=self.climb_received.at[back],
            device_id=(lax.rem(w.me + PLANE * back, PLANE * w.planes), w.s),
            device_id_type=MESH,
        )

    def cross(self, back, m):
        return pltpu.make_async_remote_copy(
            src_ref=self.spot(back, 0),
            dst_ref=self.spot(back, 0),
            send_sem=self.sent.at[back, m],
            recv_sem=self.received.at[back, m],
            device_id=self.w.across(m),
            device_id_type=MESH,
        )

    def hand_over(self, back, m):
        return pltpu.make_async_remote_copy(
            src_ref=self.spot(back, m),
            dst_ref=self.spot(back, m),
            send_sem=self.twin_sent.at[back, m],
            recv_sem=self.twin_received.at[back, m],
            device_id=self.w.twin(),
            device_id_type=MESH,
        )

    def begin(self):
        w = self.w
        self.keep().start()
        for back in range(1, self.reach + 1):

            @pl.when(w.z + back < w.planes)
            def _(back=back):
                self.climb(back).start()

            @pl.when(w.z < back)
            def _(back=back):
                block = self.mine.shape[0]
                empty = jnp.zeros((2, PLANE * block, HD), self.frame.dtype)
                self.frame[:, pl.ds((self.reach - back) * PLANE * block, PLANE * block)] = empty

        self.keep().wait()
        self.share(0)

    def share(self, back):
        for m in range(1, PLANE):
            self.cross(back, m).start()
        self.hand_over(back, 0).start()

    def forward(self, back):
        @pl.when(self.there(back))
        def _():
            self.climb(back).wait_recv()
            self.share(back)

    def collect(self, back):
        @pl.when(self.there(back))
        def _():
            for m in range(1, PLANE):
                self.cross(back, m).wait_recv()
                self.hand_over(back, m).start()

    def settle(self, back):
        @pl.when(self.there(back))
        def _():
            for m in range(PLANE):
                landed = self.spot(back, m, 1 - self.w.s)
                pltpu.make_async_copy(landed, landed, self.twin_received.at[back, m]).wait()

    def close(self):
        for back in range(self.reach + 1):

            @pl.when(self.there(back))
            def _(back=back):
                for m in range(PLANE):
                    if m:
                        self.cross(back, m).wait_send()
                    self.hand_over(back, m).wait_send()

            if back:

                @pl.when(self.w.z + back < self.w.planes)
                def _(back=back):
                    self.climb(back).wait_send()


def halo_semaphores(reach):
    dma = pltpu.SemaphoreType.DMA
    return [dma((1,))] + [dma((reach + 1,))] * 2 + [dma((reach + 1, PLANE))] * 4


def turned(value, cosine, sine):
    front = value[:, : HD // 2]
    rolled = pltpu.roll(front, HD // 4, 1)
    return jnp.concatenate([front * cosine + rolled * sine, value[:, HD // 2 :]], axis=1)


QUERY_ROWS = 128


def window_mask(first_row, rows, extent, key_floor):
    i = lax.broadcasted_iota(jnp.int32, (rows, extent), 0) + first_row
    j = lax.broadcasted_iota(jnp.int32, (rows, extent), 1)
    return (j > i) & (j <= i + WINDOW) & (j >= key_floor)


def flat_rows(pieces):
    width = pieces.shape[-1]
    if pieces.shape[-2] % 16:
        return pieces.astype(jnp.float32).reshape(-1, width).astype(pieces.dtype)
    return pieces.reshape(-1, width)


def planes_at_once(planes, rows):
    group = 1
    while group * PLANE * rows % 128:
        group *= 2
    return min(group, planes)


def front_kernel(
    planes,
    normed,
    query_weight,
    keyval,
    cosine,
    sine,
    inputs,
    gain,
    merge,
    gate,
    upward,
    down,
    merge_out,
    gate_out,
    upward_out,
    down_out,
    rows_out,
    queries,
    key_out,
    value_out,
    mixed,
    log_total,
    hidden,
    query_full,
    merge_full,
    frame,
    branch,
    arrived,
    normed_two,
    local,
    pair_sem,
    *semaphores,
):
    w = Wires(planes)
    parts = split(semaphores, (3, 3, 3, 3, 5, 7))
    count = queries.shape[0]
    block, width = normed.shape
    share = block // 2
    reach = WINDOW // (PLANE * block)
    extent = WINDOW + block
    low = jnp.bfloat16
    greet(w.partners() + [w.across(3), w.twin()])
    load = pltpu.make_async_copy(query_weight, query_full, local.at[0])
    load.start()
    project = Spread(w, "rows", merge, merge_full, parts[0])
    spreads = [
        Spread(w, "units", source, whole, sems)
        for source, whole, sems in zip(
            (gate, upward, down), (gate_out, upward_out, down_out), parts[1:4]
        )
    ]
    column = Column(w, normed_two, rows_out, parts[4])
    halo = Halo(w, keyval, frame, reach, parts[5])
    halo.begin()
    project.rise()
    project.spread(0)
    spreads[0].spread(0)

    steps = list(project.steps())
    steps.insert(4, spreads[0].rise)
    steps.insert(6, partial(spreads[1].spread, 0))
    steps.insert(8, spreads[1].rise)
    later = list(spreads[0].steps())[:-1]
    later += [partial(spreads[2].spread, 0), spreads[2].rise]
    for part in spreads[1:]:
        later += list(part.steps())[:-1]

    def move(many=1):
        for _ in range(many):
            if steps:
                steps.pop(0)()

    load.wait()
    for h in range(count):
        columns = slice(h * HD, (h + 1) * HD)
        value = jnp.dot(normed[...], query_full[:, columns], preferred_element_type=jnp.float32)
        queries[h] = (turned(value, cosine[...], sine[...]) * HD ** (-0.5)).astype(low)
    for back in range(1, reach + 1):
        halo.forward(back)
    move()
    for back in range(reach + 1):
        halo.collect(back)
    move()
    for back in range(reach + 1):
        halo.settle(back)

    window = pl.ds(pl.multiple_of(w.xy * block, block), extent)
    key_out[...] = frame[0, window]
    value_out[...] = frame[1, window]
    key_floor = WINDOW - w.me * block
    for h in range(count):
        for start in range(0, block, QUERY_ROWS):
            rows = pl.ds(start, QUERY_ROWS)
            scores = product_nt(queries[h, rows], key_out[...])
            allowed = window_mask(start, QUERY_ROWS, extent, key_floor)
            scores = jnp.where(allowed, scores, masked_score)
            peak = jnp.max(scores, axis=-1, keepdims=True)
            shifted = jnp.exp(scores - peak)
            total = jnp.sum(shifted, axis=-1, keepdims=True)
            log_total[h, rows] = peak + jnp.log(total)
            chances = (shifted / total).astype(low)
            value = jnp.dot(chances, value_out[...], preferred_element_type=jnp.float32)
            mixed[rows, h * HD : (h + 1) * HD] = value.astype(low)
            move()
    move(len(steps))
    keep = pltpu.make_async_copy(merge_full, merge_out, local.at[1])
    keep.start()

    group = planes_at_once(planes, merge_full.shape[2])
    columns = group * PLANE * merge_full.shape[2]
    for j in range(planes // group):
        piece = flat_rows(merge_full[j * group : (j + 1) * group])
        branch[:, j * columns : (j + 1) * columns] = product_nt(mixed[...], piece)
    ours = pl.ds(pl.multiple_of(w.s * share, share), share)
    other = pl.ds(pl.multiple_of((1 - w.s) * share, share), share)
    pair = pltpu.make_async_remote_copy(
        src_ref=branch.at[other],
        dst_ref=arrived,
        send_sem=pair_sem.at[0],
        recv_sem=pair_sem.at[1],
        device_id=w.twin(),
        device_id_type=MESH,
    )
    pair.start()
    steps = later
    move(2)
    pair.wait_recv()
    value = inputs[...].astype(jnp.float32) + branch[ours] + arrived[...]
    hidden[...] = value
    inverse = lax.rsqrt(jnp.mean(value * value, axis=-1, keepdims=True) + norm_epsilon)
    normed_two[...] = (value * inverse * gain[...]).astype(low)
    column.keep.start()
    column.hand_over(0)
    for k in range(1, planes):
        column.rise(k)
    move(len(steps))
    for part in spreads:
        part.settle()
    for k in range(1, planes):
        column.hand_over(k)
    pair.wait_send()
    keep.wait()
    for part in (project, *spreads, column, halo):
        part.close()


def front(normed, query_weight, keyval, cosine, sine, inputs, gain, merge, gate, upward, down):
    planes = lax.axis_size("ctx") // PLANE
    block, width = normed.shape
    share = block // 2
    heads = query_weight.shape[1] // HD
    reach = WINDOW // (PLANE * block)
    extent = WINDOW + block
    low = jnp.bfloat16
    some, near = pl.BlockSpec(memory_space=pl.ANY), pl.BlockSpec(memory_space=pltpu.VMEM)
    whole = lambda piece: jax.ShapeDtypeStruct((planes, PLANE) + piece.shape[-2:], low)
    dma = pltpu.SemaphoreType.DMA
    return pl.pallas_call(
        partial(front_kernel, planes),
        out_shape=[whole(p) for p in (merge, gate, upward, down)]
        + [
            jax.ShapeDtypeStruct((planes, block, width), low),
            jax.ShapeDtypeStruct((heads, block, HD), low),
            jax.ShapeDtypeStruct((extent, HD), low),
            jax.ShapeDtypeStruct((extent, HD), low),
            jax.ShapeDtypeStruct((block, heads * HD), low),
            jax.ShapeDtypeStruct((heads, block, 1), jnp.float32),
            jax.ShapeDtypeStruct((share, width), jnp.float32),
        ],
        in_specs=[near, some, some, near, near, near, near] + [some] * 4,
        out_specs=[some] * 5 + [near] * 6,
        scratch_shapes=[
            pltpu.VMEM(query_weight.shape, low),
            pltpu.VMEM((planes, PLANE) + merge.shape, low),
            pltpu.VMEM((2, (reach + 1) * PLANE * block, HD), low),
            pltpu.VMEM((block, width), jnp.float32),
            pltpu.VMEM((share, width), jnp.float32),
            pltpu.VMEM((share, width), low),
            dma((2,)),
            dma((2,)),
        ]
        + spread_semaphores(planes, "rows")
        + spread_semaphores(planes, "units") * 3
        + column_semaphores(planes)
        + halo_semaphores(reach),
        compiler_params=pltpu.CompilerParams(
            collective_id=4, has_side_effects=True, vmem_limit_bytes=60 * 2**20
        ),
    )(normed, query_weight, keyval, cosine, sine, inputs, gain, merge, gate, upward, down)


STEP_COLUMNS = 256


def feed_kernel(
    planes,
    depth,
    lanes,
    tokens,
    pulls,
    gate,
    upward,
    down,
    back_out,
    feed_out,
    down_out,
    gate_out,
    upward_out,
    weights,
    rows,
    grads,
    acts,
    gates,
    ups,
    own,
    outgoing,
    incoming,
    sums,
    local,
    row_local,
    pair_sent,
    pair_received,
    back_sent,
    back_received,
    feed_local,
):
    w = Wires(planes)
    z = w.z
    share, width = tokens.shape[1] // 2, tokens.shape[2]
    units = weights.shape[2]

    def plane(index):
        return (lax.rem(index + planes, planes) * PLANE + w.xy, w.s)

    greet([plane(z + k) for k in range(1, planes)] + [w.twin()])

    def pair_copy(k):
        return pltpu.make_async_remote_copy(
            src_ref=outgoing.at[lax.rem(k, depth)],
            dst_ref=incoming.at[lax.rem(k, 2)],
            send_sem=pair_sent.at[lax.rem(k, depth)],
            recv_sem=pair_received.at[lax.rem(k, 2)],
            device_id=w.twin(),
            device_id_type=MESH,
        )

    def back_copy(turn):
        k = turn + 1
        return pltpu.make_async_remote_copy(
            src_ref=sums.at[lax.rem(turn, lanes), 0],
            dst_ref=back_out.at[k],
            send_sem=back_sent.at[k],
            recv_sem=back_received.at[k],
            device_id=plane(z - k),
            device_id_type=MESH,
        )

    def kept_copy(turn):
        return pltpu.make_async_copy(
            sums.at[lax.rem(turn, lanes), 0], back_out.at[0], back_sent.at[0]
        )

    def feed_copy(turn):
        return pltpu.make_async_copy(
            sums.at[lax.rem(turn, lanes), 1],
            feed_out.at[lax.rem(turn + 1, planes)],
            feed_local.at[turn],
        )

    def shipped(turn):
        feed_copy(turn).wait()

        @pl.when(turn == planes - 1)
        def _():
            kept_copy(turn).wait()

        @pl.when(turn < planes - 1)
        def _():
            back_copy(turn).wait_send()

    loads = [
        pltpu.make_async_copy(source, weights.at[i], local.at[i])
        for i, source in enumerate((gate, upward, down))
    ]
    for load in loads:
        load.start()

    def load_rows(k):
        at = lax.rem(z - k + planes, planes)
        return (
            pltpu.make_async_copy(tokens.at[at], rows.at[k], row_local.at[k, 0]),
            pltpu.make_async_copy(pulls.at[at], grads.at[k], row_local.at[k, 1]),
        )

    for k in range(planes):
        for load in load_rows(k):
            load.start()
    for load in loads:
        load.wait()

    def compute(k, slot):
        for at in range(0, units, STEP_COLUMNS):
            columns = slice(at, min(at + STEP_COLUMNS, units))
            here = rows[k]
            gate_value = jnp.dot(here, weights[0, :, columns], preferred_element_type=jnp.float32)
            up_value = jnp.dot(here, weights[1, :, columns], preferred_element_type=jnp.float32)
            pull = jnp.dot(grads[k], weights[2, :, columns], preferred_element_type=jnp.float32)
            bent, slope = gelu_parts(gate_value)
            acts[k, :, columns] = (bent * up_value).astype(acts.dtype)
            gates[k, :, columns] = (pull * up_value * slope).astype(gates.dtype)
            ups[k, :, columns] = (pull * bent).astype(ups.dtype)

        def part(j, _):
            at = pl.ds(pl.multiple_of(j * STEP_COLUMNS, STEP_COLUMNS), STEP_COLUMNS)
            back = product_nt(gates[k], weights[0, at, :]) + product_nt(ups[k], weights[1, at, :])
            feed = product_nt(acts[k], weights[2, at, :])
            for i, value in enumerate((back, feed)):
                own[slot, i, :, at] = value[:share]
                outgoing[slot, i, :, at] = value[share:].astype(outgoing.dtype)
            return 0

        lax.fori_loop(0, width // STEP_COLUMNS, part, 0)

    def settle(turn):
        pair = pair_copy(turn)
        pair.wait_recv()
        pair.wait_send()

        @pl.when(turn >= lanes)
        def _():
            shipped(turn - lanes)

        for i in range(2):
            arrived = incoming[lax.rem(turn, 2), i].astype(jnp.float32)
            total = own[lax.rem(turn, depth), i] + arrived
            sums[lax.rem(turn, lanes), i] = total.astype(sums.dtype)

        @pl.when(turn == planes - 1)
        def _():
            kept_copy(turn).start()

        @pl.when(turn < planes - 1)
        def _():
            back_copy(turn).start()

        feed_copy(turn).start()

    def step(turn, _):
        k = lax.rem(turn + 1, planes)
        for load in load_rows(k):
            load.wait()
        compute(k, lax.rem(turn, depth))
        if depth > 1:

            @pl.when(turn > 0)
            def _():
                settle(turn - 1)

        pair_copy(turn).start()
        if depth == 1:
            settle(turn)
        return 0

    lax.fori_loop(0, planes, step, 0)
    if depth > 1:
        settle(jnp.int32(planes - 1))

    tokens = planes * 2 * share
    outs = (gate_out, upward_out, down_out)
    for i, (left, right) in enumerate(((rows, gates), (rows, ups), (grads, acts))):

        def weigh(j, _, i=i, left=left, right=right):
            at = pl.ds(pl.multiple_of(j * STEP_COLUMNS, STEP_COLUMNS), STEP_COLUMNS)
            value = product_tn(
                left[:, :, at].reshape(tokens, STEP_COLUMNS), right[...].reshape(tokens, units)
            )
            weights[i, at, :] = value.astype(weights.dtype)
            return 0

        lax.fori_loop(0, width // STEP_COLUMNS, weigh, 0)
        pltpu.make_async_copy(weights.at[i], outs[i], local.at[i]).start()

    for i in range(3):
        pltpu.make_async_copy(weights.at[i], outs[i], local.at[i]).wait()
    for turn in range(planes):
        if turn >= planes - lanes:
            shipped(jnp.int32(turn))
        if turn < planes - 1:
            back_copy(turn).wait_recv()


def feed_forward(tokens, pulls, gate, upward, down):
    planes = lax.axis_size("ctx") // PLANE
    depth, lanes = (2, planes) if planes <= 4 else (1, 2)
    share, width = tokens.shape[1] // 2, tokens.shape[2]
    units = gate.shape[1]
    low = jnp.bfloat16
    block = 2 * share
    some = pl.BlockSpec(memory_space=pl.ANY)
    dma = pltpu.SemaphoreType.DMA
    flops = 9 * 2 * planes * block * width * units
    return pl.pallas_call(
        partial(feed_kernel, planes, depth, lanes),
        out_shape=[jax.ShapeDtypeStruct((planes, share, width), low)] * 2
        + [jax.ShapeDtypeStruct((width, units), low)] * 3,
        in_specs=[some] * 5,
        out_specs=[some] * 5,
        scratch_shapes=[
            pltpu.VMEM((3, width, units), low),
            pltpu.VMEM((planes, block, width), low),
            pltpu.VMEM((planes, block, width), low),
        ]
        + [pltpu.VMEM((planes, block, units), low)] * 3
        + [
            pltpu.VMEM((depth, 2, share, width), jnp.float32),
            pltpu.VMEM((depth, 2, share, width), low),
            pltpu.VMEM((2, 2, share, width), low),
            pltpu.VMEM((lanes, 2, share, width), low),
            dma((3,)),
            dma((planes, 2)),
            dma((depth,)),
            dma((2,)),
            dma((planes,)),
            dma((planes,)),
            dma((planes,)),
        ],
        compiler_params=pltpu.CompilerParams(
            collective_id=3, has_side_effects=True, vmem_limit_bytes=62 * 2**20
        ),
        cost_estimate=pl.CostEstimate(
            flops=flops, bytes_accessed=8 * width * units * 2, transcendentals=0
        ),
    )(tokens, pulls, gate, upward, down)


RING = 3


class Ring:
    def __init__(self, buffers, semaphores):
        self.near, self.column = buffers[:2], buffers[2:]
        self.near_loaded, self.column_loaded = semaphores
        self.counts = [0, 0]
        self.leaving = {}

    def take(self, stage):
        slot = self.counts[stage] % RING
        self.counts[stage] += 1
        copy = self.leaving.pop((stage, slot), None)
        if copy is not None:
            copy()
        return slot

    def close(self):
        for copy in self.leaving.values():
            copy()


def ring_scratch(rows, width):
    buffers = [pltpu.VMEM((RING, rows, width), jnp.bfloat16)] * 5
    return buffers, [pltpu.SemaphoreType.DMA((RING, 2)), pltpu.SemaphoreType.DMA((RING, 3))]


class Reduce:
    def __init__(self, w, ring, term, result, far, near, semaphores):
        self.w, self.ring, self.term, self.result = w, ring, term, result
        self.far, self.near = far, near
        self.far_sent, self.far_received, self.sent, self.received = semaphores
        self.copies = []
        self.slots = {}

    def piece(self, kz, m):
        return self.term.at[flip(self.w.z, kz), flip(self.w.xy, m)]

    def far_out(self, kz):
        first, second = routes(self.w.planes, kz)
        for slot, m in ((1, 3), (0, second)):
            self.copies.append(
                send(
                    self.piece(kz, m),
                    self.far.at[kz, slot],
                    self.far_sent.at[kz, slot],
                    self.far_received.at[kz, slot],
                    self.w.across(second),
                )
            )

    def arrived(self, there, semaphore):
        pltpu.make_async_copy(there, there, semaphore).wait()

    def near_in(self, kz):
        first, _ = routes(self.w.planes, kz)
        slot = self.ring.take(0)
        loads = [
            pltpu.make_async_copy(source, buffer.at[slot], self.ring.near_loaded.at[slot, i])
            for i, (source, buffer) in enumerate(
                zip((self.piece(kz, first), self.far.at[kz, 1]), self.ring.near)
            )
        ]
        loads[0].start()
        self.arrived(self.far.at[kz, 1], self.far_received.at[kz, 1])
        loads[1].start()
        self.slots[0, kz] = slot, loads

    def near_out(self, kz):
        first, _ = routes(self.w.planes, kz)
        slot, loads = self.slots.pop((0, kz))
        for load in loads:
            load.wait()
        a, b = self.ring.near
        a[slot] = (a[slot].astype(jnp.float32) + b[slot].astype(jnp.float32)).astype(a.dtype)
        copy = send(
            a.at[slot], self.near.at[kz], self.sent.at[0, kz], self.received.at[0, kz],
            self.w.across(first),
        )
        self.ring.leaving[0, slot] = copy.wait_send

    def column_in(self, kz):
        slot = self.ring.take(1)
        sources = (self.piece(kz, 0), self.far.at[kz, 0], self.near.at[kz])
        loads = [
            pltpu.make_async_copy(source, buffer.at[slot], self.ring.column_loaded.at[slot, i])
            for i, (source, buffer) in enumerate(zip(sources, self.ring.column))
        ]
        loads[0].start()
        self.arrived(self.far.at[kz, 0], self.far_received.at[kz, 0])
        loads[1].start()
        self.arrived(self.near.at[kz], self.received.at[0, kz])
        loads[2].start()
        self.slots[1, kz] = slot, loads

    def column_out(self, kz):
        slot, loads = self.slots.pop((1, kz))
        for load in loads:
            load.wait()
        a, b, c = self.ring.column
        total = a[slot].astype(jnp.float32) + b[slot].astype(jnp.float32) + c[slot].astype(jnp.float32)
        a[slot] = total.astype(a.dtype)
        target = self.result.at[self.w.z]
        if kz:
            copy = send(
                a.at[slot], target, self.sent.at[1, kz], self.received.at[1, kz],
                self.w.across(PLANE * kz),
            )
            self.ring.leaving[1, slot] = copy.wait_send
        else:
            copy = pltpu.make_async_copy(a.at[slot], target, self.sent.at[1, 0])
            copy.start()
            self.ring.leaving[1, slot] = copy.wait

    def close(self):
        for k in range(1, self.w.planes):
            self.arrived(self.result.at[flip(self.w.z, k)], self.received.at[1, k])
        for copy in self.copies:
            copy.wait_send()


def reduce_semaphores(planes):
    dma = pltpu.SemaphoreType.DMA
    return [dma((planes, 2)), dma((planes, 2)), dma((2, planes)), dma((2, planes))]


def piece_order(planes):
    half = planes // 2
    return [k for pair in zip(reversed(range(half, planes)), reversed(range(half))) for k in pair]


class HaloReturn:
    def __init__(self, w, frame, crossed, falling, landed, reach, semaphores):
        self.w, self.frame, self.crossed = w, frame, crossed
        self.falling, self.landed, self.reach = falling, landed, reach
        self.sent, self.received, self.fall_sent, self.fall_received = semaphores
        self.block = falling.shape[1]

    def rows(self, back, m):
        start = ((self.reach - back) * PLANE + flip(self.w.xy, m)) * self.block
        return pl.ds(pl.multiple_of(start, self.block), self.block)

    def cross(self, back, m):
        return pltpu.make_async_remote_copy(
            src_ref=self.frame.at[self.rows(back, m)],
            dst_ref=self.crossed.at[back, m - 1],
            send_sem=self.sent.at[back, m],
            recv_sem=self.received.at[back, m],
            device_id=self.w.across(m),
            device_id_type=MESH,
        )

    def fall(self, back):
        w = self.w
        count = PLANE * w.planes
        return pltpu.make_async_remote_copy(
            src_ref=self.falling.at[back - 1],
            dst_ref=self.landed.at[back - 1],
            send_sem=self.fall_sent.at[back],
            recv_sem=self.fall_received.at[back],
            device_id=(lax.rem(w.me - PLANE * back + count, count), w.s),
            device_id_type=MESH,
        )

    def begin(self):
        for back in reversed(range(self.reach + 1)):

            @pl.when(self.w.z >= back)
            def _(back=back):
                for m in range(1, PLANE):
                    self.cross(back, m).start()

    def pile(self, back):
        total = self.frame[self.rows(back, 0)].astype(jnp.float32)
        for m in range(1, PLANE):
            self.cross(back, m).wait_recv()
            total = total + self.crossed[back, m - 1].astype(jnp.float32)
        return total

    def drop(self, back):
        @pl.when(self.w.z >= back)
        def _():
            self.falling[back - 1] = self.pile(back).astype(self.falling.dtype)
            self.fall(back).start()

    def land(self, total):
        total[...] = self.pile(0)
        for back in range(1, self.reach + 1):

            @pl.when(self.w.z + back < self.w.planes)
            def _(back=back):
                self.fall(back).wait_recv()
                total[...] += self.landed[back - 1].astype(jnp.float32)

    def close(self):
        for back in range(self.reach + 1):

            @pl.when(self.w.z >= back)
            def _(back=back):
                for m in range(1, PLANE):
                    self.cross(back, m).wait_send()
                if back:
                    self.fall(back).wait_send()


def return_semaphores(reach):
    dma = pltpu.SemaphoreType.DMA
    return [dma((reach + 1, PLANE))] * 2 + [dma((reach + 1,))] * 2


def rear_kernel(
    planes,
    backs,
    feeds,
    hidden,
    pull,
    gain,
    merge_full,
    query_full,
    mixed,
    queries,
    keys,
    values,
    log_total,
    cosine,
    sine,
    normed,
    normed_columns,
    down_term,
    gate_term,
    upward_term,
    feed_out,
    hidden_grad,
    gain_two_grad,
    normone,
    keyval_out,
    merge_term,
    query_term,
    *rest,
):
    results, fars, nears, rest = split(rest, (6, 6, 6, len(rest) - 18))
    (
        weight,
        stage,
        keyval_term,
        hidden_low,
        mixed_grad,
        query_grad,
        sums,
        outgoing,
        arrived_sums,
        frame,
        crossed,
        falling,
        landed,
        home,
        keyval_low,
        wide,
        narrow,
        arrived,
        local,
        stage_sem,
        pair_sem,
        feed_sent,
        feed_received,
    ), rest = split(rest, (23, len(rest) - 23))
    rings, rest = split(rest, (21, len(rest) - 21))
    reduce_sems, return_sems = split(rest, (24, 4))
    w = Wires(planes)
    z, s, xy = w.z, w.s, w.xy
    block, width = normed.shape
    share = block // 2
    heads = queries.shape[0]
    reach = WINDOW // (PLANE * block)
    extent = WINDOW + block
    low = jnp.bfloat16
    greet(w.partners() + [w.across(3), w.twin()])

    wide_ring, deep_ring, small_ring = (
        Ring(rings[7 * i : 7 * i + 5], rings[7 * i + 5 : 7 * i + 7]) for i in range(3)
    )
    terms = (down_term, gate_term, upward_term, merge_term, query_term, keyval_term)
    parts = [
        Reduce(w, ring, *refs, reduce_sems[4 * i : 4 * i + 4])
        for i, (ring, refs) in enumerate(
            zip(
                (wide_ring, wide_ring, wide_ring, deep_ring, deep_ring, small_ring),
                zip(terms, results, fars, nears),
            )
        )
    ]
    pieces = [(part, kz) for part in parts for kz in piece_order(planes)]
    ready = [0, 3 * planes]
    ahead = planes

    def feed_far(upto):
        while ready[0] < min(upto, ready[1]):
            part, kz = pieces[ready[0]]
            part.far_out(kz)
            ready[0] += 1

    def steps():
        for n in range(len(pieces) + 3):
            if n < len(pieces):
                part, kz = pieces[n]
                feed_far(n + 1 + ahead)
                yield partial(part.near_in, kz)
            for at, name in ((n - 1, "near_out"), (n - 2, "column_in"), (n - 3, "column_out")):
                if 0 <= at < len(pieces):
                    part, kz = pieces[at]
                    yield partial(getattr(part, name), kz)

    moves = steps()

    def move(many=1):
        for _ in range(many):
            step = next(moves, None)
            if step is not None:
                step()

    load = pltpu.make_async_copy(merge_full, weight, local.at[0])
    load.start()
    feed_far(ahead)
    feed_copies = []
    for k in range(1, planes):
        feed_copies.append(
            send(
                feeds.at[k],
                feed_out.at[k],
                feed_sent.at[k],
                feed_received.at[k],
                (lax.rem(z - k + planes, planes) * PLANE + xy, s),
            )
        )
    keep = pltpu.make_async_copy(feeds.at[0], feed_out.at[0], feed_sent.at[0])
    keep.start()

    pulled = jnp.sum(backs[...].astype(jnp.float32), axis=0)
    value = hidden[...]
    inverse = lax.rsqrt(jnp.mean(value * value, axis=-1, keepdims=True) + norm_epsilon)
    gain_two_grad[...] = jnp.sum(pulled * value * inverse, axis=0, keepdims=True)
    scaled = pulled * gain[...]
    lean = jnp.mean(value * scaled, axis=-1, keepdims=True)
    total = pull[...].astype(jnp.float32) + inverse * (scaled - value * (inverse * inverse * lean))
    hidden_grad[...] = total
    ours = pl.ds(pl.multiple_of(s * share, share), share)
    other = pl.ds(pl.multiple_of((1 - s) * share, share), share)
    hidden_low[ours] = total.astype(low)
    pair = send(hidden_low.at[ours], hidden_low.at[ours], pair_sem.at[0], pair_sem.at[1], w.twin())
    load.wait()
    there = hidden_low.at[other]
    pltpu.make_async_copy(there, there, pair_sem.at[1]).wait()
    pair.wait_send()

    group = planes_at_once(planes, weight.shape[2])
    span = group * PLANE * weight.shape[2]
    groups = planes // group

    total = None
    for j in range(groups):
        piece = flat_rows(weight[j * group : (j + 1) * group])
        part = jnp.dot(
            hidden_low[:, j * span : (j + 1) * span], piece, preferred_element_type=jnp.float32
        )
        total = part if total is None else total + part
    mixed_grad[...] = total.astype(low)
    load = pltpu.make_async_copy(query_full, weight, local.at[0])
    load.start()

    staged = {}

    def weigh(left, right, out):
        for j in range(groups):
            slot = j % 2
            if slot in staged:
                staged.pop(slot).wait()
            value = product_tn(left[:, j * span : (j + 1) * span], right[...])
            stage[slot] = value.reshape(stage.shape[1:]).astype(low)
            copy = pltpu.make_async_copy(
                stage.at[slot], out.at[pl.ds(j * group, group)], stage_sem.at[slot]
            )
            copy.start()
            staged[slot] = copy
        for slot in list(staged):
            staged.pop(slot).wait()

    weigh(hidden_low, mixed, merge_term)
    ready[1] = 4 * planes
    move(2)

    key_floor = WINDOW - w.me * block
    j_at = lax.broadcasted_iota(jnp.int32, (extent, block), 0)
    i_at = lax.broadcasted_iota(jnp.int32, (extent, block), 1)
    for h in range(heads):
        columns = slice(h * HD, (h + 1) * HD)
        allowed = (j_at > i_at) & (j_at <= i_at + WINDOW) & (j_at >= key_floor)
        scores = jnp.where(allowed, product_nt(keys[...], queries[h]), masked_score)
        chances = jnp.exp(scores - log_total[h])
        pulls = product_nt(values[...], mixed_grad[:, columns])
        inner = jnp.sum(chances * pulls, axis=0, keepdims=True)
        score_low = (chances * (pulls - inner)).astype(low)
        value_part = jnp.dot(
            chances.astype(low), mixed_grad[:, columns], preferred_element_type=jnp.float32
        )
        key_part = jnp.dot(score_low, queries[h], preferred_element_type=jnp.float32)
        if h:
            sums[0] += key_part
            sums[1] += value_part
        else:
            sums[0] = key_part
            sums[1] = value_part
        turned_back = product_tn(score_low, keys[...]) * HD ** (-0.5)
        query_grad[:, columns] = turned(turned_back, cosine[...], -sine[...]).astype(low)
        move(2)

    outgoing[...] = sums[1 - s].astype(low)
    pair = send(outgoing, arrived_sums, pair_sem.at[2], pair_sem.at[3], w.twin())
    weigh(normed, query_grad, query_term)
    ready[1] = 5 * planes
    move(1)
    empty = jnp.zeros((PLANE * block, HD), low)
    frame[0 : PLANE * block] = empty
    frame[reach * PLANE * block :] = empty
    pair.wait_recv()
    window = pl.ds(pl.multiple_of(xy * block, block), extent)
    frame[window] = (sums[s] + arrived_sums[...].astype(jnp.float32)).astype(low)
    halo = HaloReturn(w, frame, crossed, falling, landed, reach, return_sems)
    halo.begin()

    load.wait()
    for j in range(groups):
        piece = flat_rows(weight[j * group : (j + 1) * group])
        wide[:, j * span : (j + 1) * span] = product_nt(query_grad[...], piece)
    narrow[...] = wide[other].astype(low)
    pair_two = send(narrow, arrived, pair_sem.at[4], pair_sem.at[5], w.twin())
    move(2)
    for back in reversed(range(1, reach + 1)):
        halo.drop(back)
    move(2)
    pair_two.wait_recv()
    normone[...] = wide[ours] + arrived[...].astype(jnp.float32)
    halo.land(home)

    @pl.when(s == 0)
    def _():
        home[...] = turned(home[...], cosine[...], -sine[...])

    keyval_low[s] = home[...].astype(low)
    pair_three = send(
        keyval_low.at[s], keyval_low.at[s], pair_sem.at[6], pair_sem.at[7], w.twin()
    )
    move(2)
    there = keyval_low.at[1 - s]
    pltpu.make_async_copy(there, there, pair_sem.at[7]).wait()
    keyval_out[...] = keyval_low[...]
    for i in range(2):
        value = product_tn(normed_columns[...], keyval_low[i])
        keyval_term[:, :, :, i * HD : (i + 1) * HD] = value.reshape(
            keyval_term.shape[:3] + (HD,)
        ).astype(low)
    ready[1] = 6 * planes

    move(4 * len(pieces) + 12)
    for copy in (pair, pair_two, pair_three):
        copy.wait_send()
    keep.wait()
    for copy in feed_copies:
        copy.wait()
    halo.close()
    for ring in (wide_ring, deep_ring, small_ring):
        ring.close()
    for part in parts:
        part.close()


def rear(
    backs,
    feeds,
    hidden,
    pull,
    gain,
    merge_full,
    query_full,
    mixed,
    queries,
    keys,
    values,
    log_total,
    cosine,
    sine,
    normed,
    normed_columns,
    down_term,
    gate_term,
    upward_term,
):
    planes = lax.axis_size("ctx") // PLANE
    block, width = normed.shape
    share = block // 2
    heads = queries.shape[0]
    reach = WINDOW // (PLANE * block)
    extent = WINDOW + block
    low, full = jnp.bfloat16, jnp.float32
    some, near = pl.BlockSpec(memory_space=pl.ANY), pl.BlockSpec(memory_space=pltpu.VMEM)
    shape = jax.ShapeDtypeStruct
    dma = pltpu.SemaphoreType.DMA
    group = planes_at_once(planes, merge_full.shape[2])
    keyval_rows = normed_columns.shape[1] // (planes * PLANE)
    deep = merge_full.shape[2:]
    sizes = [down_term.shape[2:]] * 3 + [deep] * 2 + [(keyval_rows, 2 * HD)]
    rings = [ring_scratch(*sizes[i]) for i in (0, 3, 5)]
    outs = pl.pallas_call(
        partial(rear_kernel, planes),
        out_shape=[
            shape((planes, share, width), low),
            shape((share, width), full),
            shape((1, width), full),
            shape((share, width), full),
            shape((2, block, HD), low),
            shape(merge_full.shape, low),
            shape(query_full.shape, low),
        ]
        + [shape((planes,) + size, low) for size in sizes]
        + [shape((planes, 2) + size, low) for size in sizes]
        + [shape((planes,) + size, low) for size in sizes],
        in_specs=[near, some, near, near, near, some, some] + [near] * 9 + [some] * 3,
        out_specs=[some, near, near, near, near, some, some] + [some] * 18,
        scratch_shapes=[
            pltpu.VMEM(merge_full.shape, low),
            pltpu.VMEM((2, group) + merge_full.shape[1:], low),
            pltpu.VMEM((planes, PLANE, keyval_rows, 2 * HD), low),
            pltpu.VMEM((block, width), low),
            pltpu.VMEM((block, heads * HD), low),
            pltpu.VMEM((block, heads * HD), low),
            pltpu.VMEM((2, extent, HD), full),
            pltpu.VMEM((extent, HD), low),
            pltpu.VMEM((extent, HD), low),
            pltpu.VMEM(((reach + 1) * PLANE * block, HD), low),
            pltpu.VMEM((reach + 1, PLANE - 1, block, HD), low),
            pltpu.VMEM((reach, block, HD), low),
            pltpu.VMEM((reach, block, HD), low),
            pltpu.VMEM((block, HD), full),
            pltpu.VMEM((2, block, HD), low),
            pltpu.VMEM((block, width), full),
            pltpu.VMEM((share, width), low),
            pltpu.VMEM((share, width), low),
            dma((1,)),
            dma((2,)),
            dma((8,)),
            dma((planes,)),
            dma((planes,)),
        ]
        + [item for buffers, semaphores in rings for item in buffers + semaphores]
        + reduce_semaphores(planes) * 6
        + return_semaphores(reach),
        compiler_params=pltpu.CompilerParams(
            collective_id=2, has_side_effects=True, vmem_limit_bytes=62 * 2**20
        ),
    )(
        backs,
        feeds,
        hidden,
        pull,
        gain,
        merge_full,
        query_full,
        mixed,
        queries,
        keys,
        values,
        log_total,
        cosine,
        sine,
        normed,
        normed_columns,
        down_term,
        gate_term,
        upward_term,
    )
    return outs[:5], outs[7:13]


def shards(
    tokens,
    cotangent,
    query_weight,
    query_first,
    query_second,
    keyval_weight,
    keyval_first,
    keyval_second,
    merge_weight,
    merge_first,
    merge_second,
    gate_weight,
    gate_first,
    gate_second,
    up_weight,
    up_first,
    up_second,
    down_weight,
    down_first,
    down_second,
    gains,
    gains_first,
    gains_second,
):
    low = jnp.bfloat16
    z, xy = place()
    s = lax.axis_index("shard")
    blocks = lax.axis_size("ctx")
    planes = blocks // PLANE
    row_count = tokens.shape[0]
    share = row_count // 2
    width = tokens.shape[1]

    def own_rows(value):
        return lax.dynamic_slice_in_dim(value, s * share, share, 0)

    small = jnp.concatenate([keyval_weight.astype(low), gains.astype(low)], axis=0).T
    small = jnp.pad(small, ((0, 0), (0, -small.shape[1] % 128)))
    small_all, query_full, pulls_all = open_gather(
        small, query_weight.astype(low), own_rows(cotangent)
    )
    small_all = small_all.transpose(1, 2, 0, 3, 4).reshape(width, -1)
    query_full = query_full.reshape(width, -1)
    keyval_full = small_all[:, : 2 * HD]
    gain_used = small_all[:, 2 * HD : 2 * HD + 2].T.astype(jnp.float32)

    offset = lax.axis_index("ctx") * row_count
    positions = offset + jnp.arange(row_count, dtype=jnp.int32)
    inputs = tokens.astype(jnp.float32)
    normed = normalize(inputs, gain_used[0]).astype(low)

    keyval = jnp.dot(normed, keyval_full, preferred_element_type=jnp.float32)
    keyval_mine = jnp.where(s == 0, rotate(keyval[:, :HD], positions), keyval[:, HD:]).astype(low)
    cosine, sine = rotary_tables(positions)
    (
        merge_full,
        gate_full,
        upward_full,
        down_full,
        normed_all,
        queries,
        key_part,
        value_part,
        mixed_flat,
        log_total,
        hidden,
    ) = front(
        normed,
        query_full,
        keyval_mine,
        cosine,
        sine,
        own_rows(tokens),
        gain_used[1:],
        merge_weight.astype(low),
        unit_pieces(gate_weight),
        unit_pieces(up_weight),
        unit_pieces(down_weight),
    )
    gate_full, upward_full, down_full = (
        v.reshape(width, -1) for v in (gate_full, upward_full, down_full)
    )
    input_rows = own_rows(inputs)

    backs, feeds, down_term, gate_term, upward_term = feed_forward(
        normed_all, pulls_all, gate_full, upward_full, down_full
    )
    pieces = (planes, PLANE, width // blocks, -1)
    keyval_rows = width // blocks // 2
    normed_columns = pick(normed.reshape(row_count, blocks, 2, keyval_rows), s, 2)
    normed_columns = jnp.pad(normed_columns, ((0, 0), (0, 0), (0, -keyval_rows % 8)))
    (
        (feeds, hidden_grad, gain_two_grad, normone_grad, keyval_lin),
        (down_parts, gate_parts, upward_parts, merge_parts, query_parts, keyval_parts),
    ) = rear(
        backs,
        feeds,
        hidden,
        own_rows(cotangent),
        gain_used[1:],
        merge_full,
        query_full.reshape(pieces),
        mixed_flat,
        queries,
        key_part,
        value_part,
        log_total.reshape(log_total.shape[0], 1, -1),
        cosine,
        sine,
        normed,
        normed_columns.reshape(row_count, -1),
        down_term.reshape(pieces),
        gate_term.reshape(pieces),
        upward_term.reshape(pieces),
    )
    down_reduced, gate_reduced, upward_reduced = (
        join_units(g) for g in (down_parts, gate_parts, upward_parts)
    )
    merge_reduced, query_reduced, keyval_sums = (
        jnp.sum(g.astype(jnp.float32), axis=0) for g in (merge_parts, query_parts, keyval_parts)
    )
    keyval_reduced = keyval_sums[:keyval_rows].T
    block_output = in_order((hidden + jnp.sum(feeds.astype(jnp.float32), axis=0)).astype(low))

    keyval_rows_lin = jnp.concatenate([own_rows(keyval_lin[0]), own_rows(keyval_lin[1])], axis=1)
    normone_grad = normone_grad + contract(keyval_rows_lin, keyval_full, 1, 1)
    gain_one_grad = jnp.sum(normone_grad * input_rows * inverse_rms(input_rows), axis=0)
    norm_one_pull = jax.vjp(partial(normalize, gain_row=gain_used[0]), input_rows)[1]
    tokens_grad = in_order(hidden_grad + norm_one_pull(normone_grad)[0])

    gain_terms = jnp.stack([gain_one_grad, gain_two_grad[0]]).reshape(2, blocks, 2, -1)
    gain_terms = gain_terms.transpose(2, 1, 0, 3)
    gain_sums = pick(gain_terms, s) + swap(pick(gain_terms, 1 - s))
    gains_reduced = reduce_small(gain_sums, jnp.float32)

    query_variance, query_updated = adamw(
        query_weight, query_first, query_second, query_reduced, 4.0 / math.sqrt(D)
    )
    keyval_variance, keyval_updated = adamw(
        keyval_weight, keyval_first, keyval_second, keyval_reduced, 2.0 / math.sqrt(D)
    )
    merge_variance, merge_updated = adamw(
        merge_weight, merge_first, merge_second, merge_reduced, 8.0 / math.sqrt(NH * HD)
    )
    gate_variance, gate_updated = adamw(
        gate_weight, gate_first, gate_second, gate_reduced, 2.0 / math.sqrt(D)
    )
    up_variance, up_updated = adamw(
        up_weight, up_first, up_second, upward_reduced, 2.0 / math.sqrt(D)
    )
    down_variance, down_updated = adamw(
        down_weight, down_first, down_second, down_reduced, 2.0 / math.sqrt(FF)
    )
    gains_variance, gains_updated = adamw(gains, gains_first, gains_second, gains_reduced, 0.8)
    return (
        block_output,
        tokens_grad,
        query_reduced,
        query_variance,
        query_updated,
        keyval_reduced,
        keyval_variance,
        keyval_updated,
        merge_reduced,
        merge_variance,
        merge_updated,
        gate_reduced,
        gate_variance,
        gate_updated,
        upward_reduced,
        up_variance,
        up_updated,
        down_reduced,
        down_variance,
        down_updated,
        gains_reduced,
        gains_variance,
        gains_updated,
    )


def solution(mesh):
    return jax.shard_map(
        shards,
        mesh=mesh,
        in_specs=(
            P("ctx", None),
            P("ctx", None),
            P("ctx", "shard"),
            P("ctx", "shard"),
            P("ctx", "shard"),
            P(None, ("ctx", "shard")),
            P(None, ("ctx", "shard")),
            P(None, ("ctx", "shard")),
            P("ctx", "shard"),
            P("ctx", "shard"),
            P("ctx", "shard"),
            P("ctx", "shard"),
            P("ctx", "shard"),
            P("ctx", "shard"),
            P("ctx", "shard"),
            P("ctx", "shard"),
            P("ctx", "shard"),
            P("ctx", "shard"),
            P("ctx", "shard"),
            P("ctx", "shard"),
            P(None, ("ctx", "shard")),
            P(None, ("ctx", "shard")),
            P(None, ("ctx", "shard")),
        ),
        out_specs=(
            P("ctx", None),
            P("ctx", None),
            P("ctx", "shard"),
            P("ctx", "shard"),
            P("ctx", "shard"),
            P(None, ("ctx", "shard")),
            P(None, ("ctx", "shard")),
            P(None, ("ctx", "shard")),
            P("ctx", "shard"),
            P("ctx", "shard"),
            P("ctx", "shard"),
            P("ctx", "shard"),
            P("ctx", "shard"),
            P("ctx", "shard"),
            P("ctx", "shard"),
            P("ctx", "shard"),
            P("ctx", "shard"),
            P("ctx", "shard"),
            P("ctx", "shard"),
            P("ctx", "shard"),
            P(None, ("ctx", "shard")),
            P(None, ("ctx", "shard")),
            P(None, ("ctx", "shard")),
        ),
        check_vma=False,
    )
```

```python
from functools import partial
import math

import jax
import jax.numpy as jnp
from jax import lax
from jax.experimental import pallas as pl
from jax.experimental.pallas import tpu as pltpu
from jax.sharding import PartitionSpec as P

D = 2560
NH = 10
HD = 256
FF = 7680
WINDOW = 2048
STEP = 10


beta_first = 0.9
beta_second = 0.95
adam_epsilon = 1e-08
weight_decay = 0.1
norm_epsilon = 1e-06
rotary_base = 10000.0
masked_score = -1e30


def inverse_rms(values):
    return lax.rsqrt(jnp.mean(values * values, axis=-1, keepdims=True) + norm_epsilon)


def normalize(values, gain_row):
    return values * inverse_rms(values) * gain_row


def gelu_product(gate_value, upward):
    return jax.nn.gelu(gate_value, approximate=True) * upward


def rotate(values, positions):
    quarter = values.shape[-1] // 4
    frequency = rotary_base ** (-jnp.arange(quarter, dtype=jnp.float32) / quarter)
    angles = positions.astype(jnp.float32)[:, None] * frequency[None, :]
    cosine = jnp.cos(angles)
    sine_part = jnp.sin(angles)
    lower_half = values[..., :quarter]
    upper_half = values[..., quarter : 2 * quarter]
    return jnp.concatenate(
        [
            lower_half * cosine - upper_half * sine_part,
            upper_half * cosine + lower_half * sine_part,
            values[..., 2 * quarter :],
        ],
        axis=-1,
    )


def rotary_tables(positions):
    quarter = HD // 4
    frequency = rotary_base ** (-jnp.arange(quarter, dtype=jnp.float32) / quarter)
    angles = positions.astype(jnp.float32)[:, None] * frequency[None, :]
    cosine, sine = jnp.cos(angles), jnp.sin(angles)
    return jnp.concatenate([cosine, cosine], axis=1), jnp.concatenate([-sine, sine], axis=1)


def contract(left, right, left_dim, right_dim):
    return lax.dot_general(
        left, right, (((left_dim,), (right_dim,)), ((), ())), preferred_element_type=jnp.float32
    )


def adamw(weight, first_moment, second_moment, gradient, rate_value):
    moment_new = beta_first * first_moment + (1.0 - beta_first) * gradient
    second_new = beta_second * second_moment + (1.0 - beta_second) * gradient * gradient
    step_size = (
        moment_new
        / (1.0 - beta_first**STEP)
        / (jnp.sqrt(second_new / (1.0 - beta_second**STEP)) + adam_epsilon)
    )
    return (second_new, weight - rate_value * (step_size + weight_decay * weight))


PLANE = 4


def hop(value, mask):
    count = lax.axis_size("ctx")
    return lax.ppermute(value, "ctx", [(i, i ^ mask) for i in range(count)])


def swap(value):
    count = lax.axis_size("shard")
    return lax.ppermute(value, "shard", [(i, count - 1 - i) for i in range(count)])


def place():
    me = lax.axis_index("ctx")
    return me // PLANE, me % PLANE


def pick(value, index, axis=0):
    return lax.dynamic_index_in_dim(value, index, axis, keepdims=False)


def put(buffer, piece, *start):
    return lax.dynamic_update_slice(
        buffer, piece, tuple(start) + (0,) * (buffer.ndim - len(start))
    )


def reduce_column(column, kind=jnp.bfloat16):
    z, _ = place()
    total = pick(column, z)
    for k in range(1, column.shape[0]):
        total = total + hop(pick(column, z ^ k).astype(kind), PLANE * k).astype(jnp.float32)
    return total


def reduce_small(terms, kind):
    _, xy = place()
    split = terms.reshape((-1, PLANE) + terms.shape[1:])
    column = pick(split, xy, 1)
    for m in range(1, PLANE):
        column = column + hop(pick(split, xy ^ m, 1).astype(kind), m).astype(jnp.float32)
    return reduce_column(column, kind)


def unit_pieces(weight):
    planes = lax.axis_size("ctx") // PLANE
    units = weight.shape[1] // planes
    low = weight.astype(jnp.bfloat16)
    return jnp.stack([low[:, j * units : (j + 1) * units] for j in range(planes)])


def early_units(units):
    return -(-(units // 2) // 128) * 128


def join_units(early, late):
    pieces = [p for pair in zip(early, late) for p in pair]
    return jnp.concatenate([p.astype(jnp.float32) for p in pieces], axis=1)


def in_order(half):
    s = lax.axis_index("shard")
    other = swap(half)
    first = jnp.where(s == 0, half, other)
    last = jnp.where(s == 0, other, half)
    return jnp.concatenate([first, last], axis=0)


MESH = pl.DeviceIdType.MESH


def flip(index, mask):
    result = index
    bit = 1
    while bit <= mask:
        if mask & bit:
            result = result + bit * (1 - 2 * ((index // bit) % 2))
        bit *= 2
    return result


def greet(partners):
    barrier = pltpu.get_barrier_semaphore()
    for device in partners:
        pl.semaphore_signal(barrier, inc=1, device_id=device, device_id_type=MESH)
    pl.semaphore_wait(barrier, len(partners))


def send(source, target, sent, received, device):
    copy = pltpu.make_async_remote_copy(
        src_ref=source,
        dst_ref=target,
        send_sem=sent,
        recv_sem=received,
        device_id=device,
        device_id_type=MESH,
    )
    copy.start()
    return copy


def routes(planes, kz):
    return (1, 2) if kz < planes // 2 else (2, 1)


def ladder(planes):
    return sorted(range(1, planes), key=lambda k: (bin(k).count("1"), -k))


def rungs(planes, k):
    bit, found = 1, []
    while bit < planes and not k & bit:
        found.append(bit)
        bit *= 2
    return found


class Wires:
    def __init__(self, planes):
        self.planes = planes
        self.me = lax.axis_index("ctx")
        self.s = lax.axis_index("shard")
        self.z = self.me // PLANE
        self.xy = self.me % PLANE

    def across(self, mask):
        return (flip(self.me, mask), self.s)

    def twin(self):
        return (self.me, 1 - self.s)

    def partners(self):
        return [self.across(PLANE * k) for k in range(1, self.planes)] + [
            self.across(1),
            self.across(2),
        ]


def gelu_parts(u):
    scale = math.sqrt(2.0 / math.pi)
    square = u * u
    bend = jnp.tanh(scale * u * (1.0 + 0.044715 * square))
    half = 0.5 * (1.0 + bend)
    slope = half + 0.5 * u * (1.0 - bend * bend) * scale * (1.0 + 3.0 * 0.044715 * square)
    return u * half, slope


def product_nt(left, right):
    return lax.dot_general(
        left, right, (((1,), (1,)), ((), ())), preferred_element_type=jnp.float32
    )


def product_tn(left, right):
    return lax.dot_general(
        left, right, (((0,), (0,)), ((), ())), preferred_element_type=jnp.float32
    )


class Spread:
    def __init__(self, w, kind, source, whole, semaphores):
        self.w, self.kind, self.source = w, kind, source
        self.own_sem, self.sent, self.received, *twin = semaphores
        self.everything = whole
        self.whole = whole.at[w.s] if kind == "pair" else whole
        self.twin = twin
        self.copies = []
        if kind == "column":
            self.keep = pltpu.make_async_copy(source, whole.at[:, w.xy], self.own_sem.at[0])
        else:
            self.keep = pltpu.make_async_copy(self.mine(0), self.spot(0, 0), self.own_sem.at[0])

    def mine(self, k):
        split = self.kind in ("units", "column")
        return self.source.at[flip(self.w.z, k)] if split else self.source

    def spot(self, kz, m):
        return self.whole.at[flip(self.w.z, kz), flip(self.w.xy, m)]

    def push(self, kz, m, slot, source, target, device):
        self.copies.append(
            send(source, target, self.sent.at[slot, kz], self.received.at[kz, m], device)
        )

    def wait_for(self, kz, m):
        there = self.spot(kz, m)
        pltpu.make_async_copy(there, there, self.received.at[kz, m]).wait()
        if self.kind == "pair":
            self.hand_over(kz, m, there)

    def hand_over(self, kz, m, piece):
        self.copies.append(
            send(
                piece,
                self.spot(kz, m),
                self.twin[0].at[kz, m],
                self.twin[1].at[kz, m],
                self.w.twin(),
            )
        )

    def rise(self):
        self.keep.start()
        if self.kind == "pair":
            self.hand_over(0, 0, self.source)
        if self.kind == "units":
            for k in range(1, self.w.planes):
                self.push(k, 0, 0, self.mine(k), self.spot(0, 0), self.w.across(PLANE * k))
        elif self.kind != "column":
            self.climb(0)

    def climb(self, kz):
        piece = self.spot(kz, 0) if kz else self.source
        for bit in rungs(self.w.planes, kz):
            self.push(kz | bit, 0, 0, piece, self.spot(kz, 0), self.w.across(PLANE * bit))

    def spread(self, kz):
        first, second = routes(self.w.planes, kz)
        if kz and self.kind != "column":
            self.wait_for(kz, 0)
            if self.kind != "units":
                self.climb(kz)
        mine = self.spot(kz, 0) if kz and self.kind != "column" else self.mine(kz)
        self.push(kz, first, 1, mine, self.spot(kz, 0), self.w.across(first))
        self.push(kz, second, 2, mine, self.spot(kz, 0), self.w.across(second))

    def relay(self, kz):
        first, second = routes(self.w.planes, kz)
        self.wait_for(kz, first)
        there = self.spot(kz, first)
        self.push(kz, 3, 3, there, there, self.w.across(second))

    def settle(self):
        planes = self.w.planes
        for kz in range(planes):
            first, second = routes(planes, kz)
            self.wait_for(kz, second)
            self.wait_for(kz, 3)
        self.keep.wait()

    def close(self):
        if self.kind == "pair":
            for kz in range(self.w.planes):
                for m in range(PLANE):
                    there = self.everything.at[
                        1 - self.w.s, flip(self.w.z, kz), flip(self.w.xy, m)
                    ]
                    pltpu.make_async_copy(there, there, self.twin[1].at[kz, m]).wait()
        for copy in self.copies:
            copy.wait_send()

    def steps(self):
        last = 0
        for kz in ladder(self.w.planes):
            yield partial(self.spread, kz)
            yield partial(self.relay, last)
            last = kz
        yield partial(self.relay, last)


def spread_semaphores(planes, kind):
    dma = pltpu.SemaphoreType.DMA
    kinds = [dma((1,)), dma((4, planes)), dma((planes, PLANE))]
    return kinds + [dma((planes, PLANE))] * 2 if kind == "pair" else kinds


class Column:
    def __init__(self, w, half, whole, semaphores):
        self.w, self.half, self.whole = w, half, whole
        self.own_sem, self.sent, self.received, self.twin_sent, self.twin_received = semaphores
        self.share = half.shape[0]
        self.keep = pltpu.make_async_copy(half, self.spot(0, 0), self.own_sem.at[0])
        self.copies = []

    def spot(self, k, part):
        return self.whole.at[flip(self.w.z, k), pl.ds(part * self.share, self.share)]

    def climb(self, k):
        piece = self.spot(k, 0) if k else self.half
        for bit in rungs(self.w.planes, k):
            self.copies.append(
                send(
                    piece,
                    self.spot(k, 0),
                    self.sent.at[k | bit],
                    self.received.at[k | bit],
                    self.w.across(PLANE * bit),
                )
            )

    def rise(self):
        self.keep.start()
        self.climb(0)
        self.hand_over(0)

    def pass_on(self, k):
        there = self.spot(k, 0)
        pltpu.make_async_copy(there, there, self.received.at[k]).wait()
        self.climb(k)
        self.hand_over(k)

    def hand_over(self, k):
        self.copies.append(
            send(
                self.spot(k, 0) if k else self.half,
                self.spot(k, 1),
                self.twin_sent.at[k],
                self.twin_received.at[k],
                self.w.twin(),
            )
        )

    def ready(self, k):
        if k == 0:
            self.keep.wait()
        there = self.spot(k, 1)
        pltpu.make_async_copy(there, there, self.twin_received.at[k]).wait()

    def close(self):
        for copy in self.copies:
            copy.wait_send()


class Deal:
    def __init__(self, w, pieces, whole, semaphores):
        self.w, self.pieces, self.whole = w, pieces, whole
        self.own_sem, self.sent, self.received = semaphores
        self.keep = pltpu.make_async_copy(pieces.at[w.z], whole.at[w.z], self.own_sem.at[0])
        self.copies = []

    def rise(self):
        w = self.w
        self.keep.start()
        for k in range(1, w.planes):
            self.copies.append(
                send(
                    self.pieces.at[flip(w.z, k)],
                    self.whole.at[w.z],
                    self.sent.at[k],
                    self.received.at[k],
                    w.across(PLANE * k),
                )
            )

    def close(self):
        self.keep.wait()
        for k in range(1, self.w.planes):
            there = self.whole.at[flip(self.w.z, k)]
            pltpu.make_async_copy(there, there, self.received.at[k]).wait()
        for copy in self.copies:
            copy.wait_send()


def deal_semaphores(planes):
    dma = pltpu.SemaphoreType.DMA
    return [dma((1,)), dma((planes,)), dma((planes,))]


def column_semaphores(planes):
    return [pltpu.SemaphoreType.DMA((1,))] + [pltpu.SemaphoreType.DMA((planes,))] * 4


def split(refs, sizes):
    at, groups = 0, []
    for size in sizes:
        groups.append(refs[at : at + size])
        at += size
    return groups


def open_kernel(planes, small, small_out, *semaphores):
    w = Wires(planes)
    greet(w.partners() + [w.twin()])
    part = Spread(w, "pair", small, small_out, semaphores)
    part.rise()
    part.spread(0)
    for step in part.steps():
        step()
    part.settle()
    part.close()


def open_gather(small):
    planes = lax.axis_size("ctx") // PLANE
    some = pl.BlockSpec(memory_space=pl.ANY)
    return pl.pallas_call(
        partial(open_kernel, planes),
        out_shape=jax.ShapeDtypeStruct((2, planes, PLANE) + small.shape, small.dtype),
        in_specs=[some],
        out_specs=some,
        scratch_shapes=spread_semaphores(planes, "pair"),
        compiler_params=pltpu.CompilerParams(collective_id=1, has_side_effects=True),
    )(small)


class Halo:
    def __init__(self, w, mine, frame, reach, semaphores):
        self.w, self.mine, self.frame, self.reach = w, mine, frame, reach
        (
            self.own_sem,
            self.climb_sent,
            self.climb_received,
            self.sent,
            self.received,
            self.twin_sent,
            self.twin_received,
        ) = semaphores

    def there(self, back):
        return self.w.z >= back

    def spot(self, back, m, part=None):
        part = self.w.s if part is None else part
        return self.frame.at[part, self.rows(back, flip(self.w.xy, m))]

    def rows(self, back, xy):
        block = self.mine.shape[0]
        start = ((self.reach - back) * PLANE + xy) * block
        return pl.ds(pl.multiple_of(start, block), block)

    def keep(self):
        return pltpu.make_async_copy(self.mine, self.spot(0, 0), self.own_sem.at[0])

    def climb(self, back):
        w = self.w
        return pltpu.make_async_remote_copy(
            src_ref=self.mine,
            dst_ref=self.spot(back, 0),
            send_sem=self.climb_sent.at[back],
            recv_sem=self.climb_received.at[back],
            device_id=(lax.rem(w.me + PLANE * back, PLANE * w.planes), w.s),
            device_id_type=MESH,
        )

    def cross(self, back, m):
        return pltpu.make_async_remote_copy(
            src_ref=self.spot(back, 0),
            dst_ref=self.spot(back, 0),
            send_sem=self.sent.at[back, m],
            recv_sem=self.received.at[back, m],
            device_id=self.w.across(m),
            device_id_type=MESH,
        )

    def hand_over(self, back, m):
        return pltpu.make_async_remote_copy(
            src_ref=self.spot(back, m),
            dst_ref=self.spot(back, m),
            send_sem=self.twin_sent.at[back, m],
            recv_sem=self.twin_received.at[back, m],
            device_id=self.w.twin(),
            device_id_type=MESH,
        )

    def begin(self):
        w = self.w
        self.keep().start()
        for back in range(1, self.reach + 1):

            @pl.when(w.z + back < w.planes)
            def _(back=back):
                self.climb(back).start()

            @pl.when(w.z < back)
            def _(back=back):
                block = self.mine.shape[0]
                empty = jnp.zeros((2, PLANE * block, HD), self.frame.dtype)
                self.frame[:, pl.ds((self.reach - back) * PLANE * block, PLANE * block)] = empty

        self.keep().wait()
        self.share(0)

    def share(self, back):
        for m in range(1, PLANE):
            self.cross(back, m).start()
        self.hand_over(back, 0).start()

    def forward(self, back):
        @pl.when(self.there(back))
        def _():
            self.climb(back).wait_recv()
            self.share(back)

    def collect(self, back):
        @pl.when(self.there(back))
        def _():
            for m in range(1, PLANE):
                self.cross(back, m).wait_recv()
                self.hand_over(back, m).start()

    def settle(self, back):
        @pl.when(self.there(back))
        def _():
            for m in range(PLANE):
                landed = self.spot(back, m, 1 - self.w.s)
                pltpu.make_async_copy(landed, landed, self.twin_received.at[back, m]).wait()

    def close(self):
        for back in range(self.reach + 1):

            @pl.when(self.there(back))
            def _(back=back):
                for m in range(PLANE):
                    if m:
                        self.cross(back, m).wait_send()
                    self.hand_over(back, m).wait_send()

            if back:

                @pl.when(self.w.z + back < self.w.planes)
                def _(back=back):
                    self.climb(back).wait_send()


def halo_semaphores(reach):
    dma = pltpu.SemaphoreType.DMA
    return [dma((1,))] + [dma((reach + 1,))] * 2 + [dma((reach + 1, PLANE))] * 4


def turned(value, cosine, sine):
    front = value[:, : HD // 2]
    rolled = pltpu.roll(front, HD // 4, 1)
    return jnp.concatenate([front * cosine + rolled * sine, value[:, HD // 2 :]], axis=1)


QUERY_ROWS = 128


def window_mask(first_row, rows, extent, key_floor):
    i = lax.broadcasted_iota(jnp.int32, (rows, extent), 0) + first_row
    j = lax.broadcasted_iota(jnp.int32, (rows, extent), 1)
    return (j > i) & (j <= i + WINDOW) & (j >= key_floor)


def flat_rows(pieces):
    width = pieces.shape[-1]
    if pieces.shape[-2] % 16:
        return pieces.astype(jnp.float32).reshape(-1, width).astype(pieces.dtype)
    return pieces.reshape(-1, width)


def planes_at_once(planes, rows):
    group = 1
    while group * PLANE * rows % 128:
        group *= 2
    return min(group, planes)


def front_kernel(
    planes,
    normed,
    keyval,
    cosine,
    sine,
    inputs,
    gain,
    pull,
    query,
    merge,
    gate,
    upward,
    down,
    gate_rest,
    upward_rest,
    down_rest,
    query_out,
    merge_out,
    gate_out,
    upward_out,
    down_out,
    gate_rest_out,
    upward_rest_out,
    down_rest_out,
    pulls_out,
    queries,
    key_out,
    value_out,
    mixed,
    log_total,
    hidden,
    normed_two,
    query_full,
    merge_full,
    frame,
    branch,
    arrived,
    local,
    pair_sem,
    *semaphores,
):
    w = Wires(planes)
    parts = split(semaphores, (3, 3, 3, 3, 3, 5, 7, 3, 3, 3))
    heads = queries.shape[0]
    block, width = normed.shape
    share = block // 2
    reach = WINDOW // (PLANE * block)
    extent = WINDOW + block
    low = jnp.bfloat16
    greet(w.partners() + [w.across(3), w.twin()])
    spreads = [
        Spread(w, kind, source, whole, sems)
        for kind, source, whole, sems in zip(
            ("rows", "rows", "units", "units", "units"),
            (query, merge, gate, upward, down),
            (query_full, merge_full, gate_out, upward_out, down_out),
            parts[:5],
        )
    ]
    pulls = Column(w, pull, pulls_out, parts[5])
    halo = Halo(w, keyval, frame, reach, parts[6])
    deals = [
        Deal(w, pieces, whole, sems)
        for pieces, whole, sems in zip(
            (gate_rest, upward_rest, down_rest),
            (gate_rest_out, upward_rest_out, down_rest_out),
            parts[7:],
        )
    ]

    steps, ends = [], []
    for i, part in enumerate(spreads):
        following = spreads[i + 1] if i + 1 < len(spreads) else None
        moves = list(part.steps())
        if following:
            moves.insert(len(moves) - 1, partial(following.spread, 0))
        if i == 0:
            moves.insert(2, following.rise)
        if i == 1:
            for at, later in enumerate(spreads[2:]):
                moves.insert(2 * at, later.rise)
        if i == 2:
            moves.insert(1, pulls.rise)
        if i == 3:
            moves.insert(1, deals[0].rise)
            moves.insert(4, deals[1].rise)
        if i == 4:
            moves.insert(1, deals[2].rise)
        steps += moves
        ends.append(len(steps))
    done = [0]

    def move(many=1, upto=None):
        stop = min(done[0] + many if upto is None else upto, len(steps))
        while done[0] < stop:
            steps[done[0]]()
            done[0] += 1

    halo.begin()
    spreads[0].rise()
    spreads[0].spread(0)
    move(2)
    for back in range(1, reach + 1):
        halo.forward(back)
    move(3)
    for back in range(reach + 1):
        halo.collect(back)
    move(upto=ends[0] + 2)
    for back in range(reach + 1):
        halo.settle(back)
    window = pl.ds(pl.multiple_of(w.xy * block, block), extent)
    key_out[...] = frame[0, window]
    value_out[...] = frame[1, window]
    spreads[0].settle()
    keep_query = pltpu.make_async_copy(query_full, query_out, local.at[0])
    keep_query.start()

    group = planes_at_once(planes, merge_full.shape[2])
    span = group * PLANE * merge_full.shape[2]
    groups = planes // group
    for h in range(heads):
        columns = slice(h * HD, (h + 1) * HD)
        total = None
        for j in range(groups):
            piece = flat_rows(query_full[j * group : (j + 1) * group, :, :, columns])
            value = jnp.dot(
                normed[:, j * span : (j + 1) * span], piece, preferred_element_type=jnp.float32
            )
            total = value if total is None else total + value
        queries[h] = (turned(total, cosine[...], sine[...]) * HD ** (-0.5)).astype(low)
    move()

    key_floor = WINDOW - w.me * block
    for h in range(heads):
        for start in range(0, block, QUERY_ROWS):
            rows = pl.ds(start, QUERY_ROWS)
            scores = product_nt(queries[h, rows], key_out[...])
            allowed = window_mask(start, QUERY_ROWS, extent, key_floor)
            scores = jnp.where(allowed, scores, masked_score)
            peak = jnp.max(scores, axis=-1, keepdims=True)
            shifted = jnp.exp(scores - peak)
            total = jnp.sum(shifted, axis=-1, keepdims=True)
            log_total[h, rows] = peak + jnp.log(total)
            chances = (shifted / total).astype(low)
            value = jnp.dot(chances, value_out[...], preferred_element_type=jnp.float32)
            mixed[rows, h * HD : (h + 1) * HD] = value.astype(low)
            move()
    move(upto=ends[1] + 2)
    spreads[1].settle()
    keep_merge = pltpu.make_async_copy(merge_full, merge_out, local.at[1])
    keep_merge.start()

    for j in range(groups):
        piece = flat_rows(merge_full[j * group : (j + 1) * group])
        branch[:, j * span : (j + 1) * span] = product_nt(mixed[...], piece)
    ours = pl.ds(pl.multiple_of(w.s * share, share), share)
    other = pl.ds(pl.multiple_of((1 - w.s) * share, share), share)
    pair = send(branch.at[other], arrived, pair_sem.at[0], pair_sem.at[1], w.twin())
    move(2)
    pair.wait_recv()
    value = inputs[...].astype(jnp.float32) + branch[ours] + arrived[...]
    hidden[...] = value
    inverse = lax.rsqrt(jnp.mean(value * value, axis=-1, keepdims=True) + norm_epsilon)
    normed_two[...] = (value * inverse * gain[...]).astype(low)
    move(upto=len(steps))
    for k in ladder(planes):
        pulls.pass_on(k)
    for part in spreads[2:]:
        part.settle()
    pair.wait_send()
    keep_query.wait()
    keep_merge.wait()
    for k in range(planes):
        pulls.ready(k)
    for part in (*spreads, *deals, pulls, halo):
        part.close()


def front(normed, keyval, cosine, sine, inputs, gain, pull, query, merge, early, late):
    planes = lax.axis_size("ctx") // PLANE
    block, width = normed.shape
    share = block // 2
    heads = query.shape[1] // HD
    reach = WINDOW // (PLANE * block)
    extent = WINDOW + block
    low = jnp.bfloat16
    some, near = pl.BlockSpec(memory_space=pl.ANY), pl.BlockSpec(memory_space=pltpu.VMEM)
    shape = jax.ShapeDtypeStruct
    dma = pltpu.SemaphoreType.DMA
    return pl.pallas_call(
        partial(front_kernel, planes),
        out_shape=[
            shape((planes, PLANE) + piece.shape[-2:], low)
            for piece in (query, merge, *early)
        ]
        + [shape(piece.shape, low) for piece in late]
        + [
            shape((planes, block, width), low),
            shape((heads, block, HD), low),
            shape((extent, HD), low),
            shape((extent, HD), low),
            shape((block, heads * HD), low),
            shape((heads, block, 1), jnp.float32),
            shape((share, width), jnp.float32),
            shape((share, width), low),
        ],
        in_specs=[near, some, near, near, near, near] + [some] * 9,
        out_specs=[some] * 9 + [near] * 7,
        scratch_shapes=[
            pltpu.VMEM((planes, PLANE) + query.shape, low),
            pltpu.VMEM((planes, PLANE) + merge.shape, low),
            pltpu.VMEM((2, (reach + 1) * PLANE * block, HD), low),
            pltpu.VMEM((block, width), jnp.float32),
            pltpu.VMEM((share, width), jnp.float32),
            dma((2,)),
            dma((2,)),
        ]
        + spread_semaphores(planes, "rows") * 2
        + spread_semaphores(planes, "units") * 3
        + column_semaphores(planes)
        + halo_semaphores(reach)
        + deal_semaphores(planes) * 3,
        compiler_params=pltpu.CompilerParams(
            collective_id=4, has_side_effects=True, vmem_limit_bytes=60 * 2**20
        ),
    )(normed, keyval, cosine, sine, inputs, gain, pull, query, merge, *early, *late)


KEPT = 8
LOADED = 2
LAG = 6


class Ring:
    def __init__(self, buffers, semaphores):
        self.near, self.column = buffers[:2], buffers[2:]
        self.near_loaded, self.column_loaded = semaphores
        self.counts = [0, 0]
        self.leaving = {}

    def take(self, stage):
        slot, spare = self.counts[stage] % KEPT, self.counts[stage] % LOADED
        self.counts[stage] += 1
        copy = self.leaving.pop((stage, slot), None)
        if copy is not None:
            copy()
        return slot, spare

    def close(self):
        for copy in self.leaving.values():
            copy()


def ring_scratch(rows, width):
    kept, loaded = (pltpu.VMEM((depth, rows, width), jnp.bfloat16) for depth in (KEPT, LOADED))
    dma = pltpu.SemaphoreType.DMA
    return [kept, loaded, kept, loaded, loaded], [dma((LOADED, 2)), dma((LOADED, 3))]


class Reduce:
    def __init__(self, w, ring, term, result, far, near, semaphores, halfway=False):
        self.w, self.ring, self.term, self.result = w, ring, term, result
        self.far, self.near, self.halfway = far, near, halfway
        self.sent, self.received, *self.far_sems = semaphores
        self.copies = []
        self.slots = {}

    def piece(self, kz, m):
        return self.term.at[flip(self.w.z, kz), flip(self.w.xy, m)]

    def far_out(self, kz):
        first, second = routes(self.w.planes, kz)
        for slot, m in ((1, 3), (0, second)):
            self.copies.append(
                send(
                    self.piece(kz, m),
                    self.far.at[kz, slot],
                    self.far_sems[0].at[kz, slot],
                    self.far_sems[1].at[kz, slot],
                    self.w.across(second),
                )
            )

    def arrived(self, there, semaphore):
        pltpu.make_async_copy(there, there, semaphore).wait()

    def far_in(self, kz, slot):
        if not self.halfway:
            self.arrived(self.far.at[kz, slot], self.far_sems[1].at[kz, slot])

    def near_in(self, kz):
        first, _ = routes(self.w.planes, kz)
        slot, spare = self.ring.take(0)
        loads = [
            pltpu.make_async_copy(source, buffer, self.ring.near_loaded.at[spare, i])
            for i, (source, buffer) in enumerate(
                (
                    (self.piece(kz, first), self.ring.near[0].at[slot]),
                    (self.far.at[kz, 1], self.ring.near[1].at[spare]),
                )
            )
        ]
        loads[0].start()
        self.far_in(kz, 1)
        loads[1].start()
        self.slots[0, kz] = slot, spare, loads

    def near_out(self, kz):
        first, _ = routes(self.w.planes, kz)
        slot, spare, loads = self.slots.pop((0, kz))
        for load in loads:
            load.wait()
        a, b = self.ring.near
        a[slot] = (a[slot].astype(jnp.float32) + b[spare].astype(jnp.float32)).astype(a.dtype)
        copy = send(
            a.at[slot], self.near.at[kz], self.sent.at[0, kz], self.received.at[0, kz],
            self.w.across(first),
        )
        self.ring.leaving[0, slot] = copy.wait_send

    def column_in(self, kz):
        slot, spare = self.ring.take(1)
        sources = (self.piece(kz, 0), self.far.at[kz, 0], self.near.at[kz])
        loads = [
            pltpu.make_async_copy(
                source,
                buffer.at[spare if i else slot],
                self.ring.column_loaded.at[spare, i],
            )
            for i, (source, buffer) in enumerate(zip(sources, self.ring.column))
        ]
        loads[0].start()
        self.far_in(kz, 0)
        loads[1].start()
        self.arrived(self.near.at[kz], self.received.at[0, kz])
        loads[2].start()
        self.slots[1, kz] = slot, spare, loads

    def column_out(self, kz):
        slot, spare, loads = self.slots.pop((1, kz))
        for load in loads:
            load.wait()
        a, b, c = self.ring.column
        total = sum(v.astype(jnp.float32) for v in (a[slot], b[spare], c[spare]))
        a[slot] = total.astype(a.dtype)
        target = self.result.at[self.w.z]
        if kz:
            copy = send(
                a.at[slot], target, self.sent.at[1, kz], self.received.at[1, kz],
                self.w.across(PLANE * kz),
            )
            self.ring.leaving[1, slot] = copy.wait_send
        else:
            copy = pltpu.make_async_copy(a.at[slot], target, self.sent.at[1, 0])
            copy.start()
            self.ring.leaving[1, slot] = copy.wait

    def close(self):
        for k in range(1, self.w.planes):
            self.arrived(self.result.at[flip(self.w.z, k)], self.received.at[1, k])
        for copy in self.copies:
            copy.wait_send()


def reduce_semaphores(planes, halfway=False):
    dma = pltpu.SemaphoreType.DMA
    return [dma((2, planes))] * 2 + ([] if halfway else [dma((planes, 2))] * 2)


class Cross(Reduce):
    def __init__(self, w, term, far, semaphores):
        self.w, self.term, self.far, self.halfway = w, term, far, False
        self.far_sems, self.copies = semaphores, []

    def close(self):
        for kz in range(self.w.planes):
            for slot in range(2):
                self.far_in(kz, slot)
        for copy in self.copies:
            copy.wait_send()


def piece_order(planes):
    half = planes // 2
    return [k for pair in zip(reversed(range(half, planes)), reversed(range(half))) for k in pair]


class HaloReturn:
    def __init__(self, w, frame, crossed, falling, landed, reach, semaphores):
        self.w, self.frame, self.crossed = w, frame, crossed
        self.falling, self.landed, self.reach = falling, landed, reach
        self.sent, self.received, self.fall_sent, self.fall_received = semaphores
        self.block = falling.shape[1]

    def rows(self, back, m):
        start = ((self.reach - back) * PLANE + flip(self.w.xy, m)) * self.block
        return pl.ds(pl.multiple_of(start, self.block), self.block)

    def cross(self, back, m):
        return pltpu.make_async_remote_copy(
            src_ref=self.frame.at[self.rows(back, m)],
            dst_ref=self.crossed.at[back, m - 1],
            send_sem=self.sent.at[back, m],
            recv_sem=self.received.at[back, m],
            device_id=self.w.across(m),
            device_id_type=MESH,
        )

    def fall(self, back):
        w = self.w
        count = PLANE * w.planes
        return pltpu.make_async_remote_copy(
            src_ref=self.falling.at[back - 1],
            dst_ref=self.landed.at[back - 1],
            send_sem=self.fall_sent.at[back],
            recv_sem=self.fall_received.at[back],
            device_id=(lax.rem(w.me - PLANE * back + count, count), w.s),
            device_id_type=MESH,
        )

    def begin(self):
        for back in reversed(range(self.reach + 1)):

            @pl.when(self.w.z >= back)
            def _(back=back):
                for m in range(1, PLANE):
                    self.cross(back, m).start()

    def pile(self, back):
        total = self.frame[self.rows(back, 0)].astype(jnp.float32)
        for m in range(1, PLANE):
            self.cross(back, m).wait_recv()
            total = total + self.crossed[back, m - 1].astype(jnp.float32)
        return total

    def drop(self, back):
        @pl.when(self.w.z >= back)
        def _():
            self.falling[back - 1] = self.pile(back).astype(self.falling.dtype)
            self.fall(back).start()

    def land(self, total):
        total[...] = self.pile(0)
        for back in range(1, self.reach + 1):

            @pl.when(self.w.z + back < self.w.planes)
            def _(back=back):
                self.fall(back).wait_recv()
                total[...] += self.landed[back - 1].astype(jnp.float32)

    def close(self):
        for back in range(self.reach + 1):

            @pl.when(self.w.z >= back)
            def _(back=back):
                for m in range(1, PLANE):
                    self.cross(back, m).wait_send()
                if back:
                    self.fall(back).wait_send()


def return_semaphores(reach):
    dma = pltpu.SemaphoreType.DMA
    return [dma((reach + 1, PLANE))] * 2 + [dma((reach + 1,))] * 2


def rear_kernel(
    planes,
    backs,
    feeds,
    hidden,
    pull,
    gain,
    merge_full,
    query_full,
    mixed,
    queries,
    keys,
    values,
    log_total,
    cosine,
    sine,
    normed,
    normed_columns,
    *rest,
):
    late_terms, early_terms, early_fars, outs, rest = split(rest, (3, 3, 3, 7, len(rest) - 16))
    feed_out, hidden_grad, gain_two_grad, normone, keyval_out, merge_term, query_term = outs
    results, fars, nears, rest = split(rest, (9, 6, 9, len(rest) - 24))
    (
        weight,
        stage,
        keyval_term,
        hidden_low,
        mixed_grad,
        query_grad,
        sums,
        outgoing,
        arrived_sums,
        frame,
        crossed,
        falling,
        landed,
        home,
        keyval_low,
        wide,
        narrow,
        arrived,
        local,
        stage_sem,
        pair_sem,
        feed_sent,
        feed_received,
    ), rest = split(rest, (23, len(rest) - 23))
    rings, early_sems, reduce_sems, return_sems = split(rest, (28, 6, 24, 4))
    w = Wires(planes)
    z, s, xy = w.z, w.s, w.xy
    block, width = normed.shape
    share = block // 2
    heads = queries.shape[0]
    reach = WINDOW // (PLANE * block)
    extent = WINDOW + block
    low = jnp.bfloat16
    greet(w.partners() + [w.across(3), w.twin()])

    early_ring, late_ring, deep_ring, small_ring = (
        Ring(rings[7 * i : 7 * i + 5], rings[7 * i + 5 : 7 * i + 7]) for i in range(4)
    )
    early_parts = [
        Reduce(w, early_ring, *refs, early_sems[2 * i : 2 * i + 2], halfway=True)
        for i, refs in enumerate(zip(early_terms, results, early_fars, nears))
    ]
    terms = (*late_terms, merge_term, query_term, keyval_term)
    late_parts = [
        Reduce(w, ring, *refs, reduce_sems[4 * i : 4 * i + 4])
        for i, (ring, refs) in enumerate(
            zip(
                (late_ring, late_ring, late_ring, deep_ring, deep_ring, small_ring),
                zip(terms, results[3:], fars, nears[3:]),
            )
        )
    ]
    parts = early_parts + late_parts
    order = piece_order(planes)
    pieces = [
        (part, kz) for pair in zip(early_parts, late_parts) for kz in order for part in pair
    ]
    pieces += [(late_parts[3], kz) for kz in order]
    pieces += [(part, kz) for kz in order for part in late_parts[4:]]
    crossing = [(part, kz) for part, kz in pieces if not part.halfway]
    ready = [0, 3 * planes]
    ahead = planes

    def feed_far(upto):
        while ready[0] < min(upto, ready[1]):
            part, kz = crossing[ready[0]]
            part.far_out(kz)
            ready[0] += 1

    def steps():
        met = 0
        for n in range(len(pieces) + LAG + 2):
            if n < len(pieces):
                part, kz = pieces[n]
                met += not part.halfway
                feed_far(met + ahead)
                yield partial(part.near_in, kz)
            lags = ((1, "near_out"), (LAG, "column_in"), (LAG + 1, "column_out"))
            for at, name in ((n - lag, name) for lag, name in lags):
                if 0 <= at < len(pieces):
                    part, kz = pieces[at]
                    yield partial(getattr(part, name), kz)

    moves = steps()

    def move(many=1):
        for _ in range(many):
            step = next(moves, None)
            if step is not None:
                step()

    load = pltpu.make_async_copy(merge_full, weight, local.at[0])
    load.start()
    feed_far(ahead)
    feed_copies = []
    for k in range(1, planes):
        feed_copies.append(
            send(
                feeds.at[k],
                feed_out.at[k],
                feed_sent.at[k],
                feed_received.at[k],
                w.across(PLANE * k),
            )
        )
    keep = pltpu.make_async_copy(feeds.at[0], feed_out.at[0], feed_sent.at[0])
    keep.start()

    pulled = jnp.sum(backs[...].astype(jnp.float32), axis=0)
    value = hidden[...]
    inverse = lax.rsqrt(jnp.mean(value * value, axis=-1, keepdims=True) + norm_epsilon)
    gain_two_grad[...] = jnp.sum(pulled * value * inverse, axis=0, keepdims=True)
    scaled = pulled * gain[...]
    lean = jnp.mean(value * scaled, axis=-1, keepdims=True)
    total = pull[...].astype(jnp.float32) + inverse * (scaled - value * (inverse * inverse * lean))
    hidden_grad[...] = total
    ours = pl.ds(pl.multiple_of(s * share, share), share)
    other = pl.ds(pl.multiple_of((1 - s) * share, share), share)
    hidden_low[ours] = total.astype(low)
    pair = send(hidden_low.at[ours], hidden_low.at[ours], pair_sem.at[0], pair_sem.at[1], w.twin())
    load.wait()
    there = hidden_low.at[other]
    pltpu.make_async_copy(there, there, pair_sem.at[1]).wait()
    pair.wait_send()

    group = planes_at_once(planes, weight.shape[2])
    span = group * PLANE * weight.shape[2]
    groups = planes // group

    total = None
    for j in range(groups):
        piece = flat_rows(weight[j * group : (j + 1) * group])
        part = jnp.dot(
            hidden_low[:, j * span : (j + 1) * span], piece, preferred_element_type=jnp.float32
        )
        total = part if total is None else total + part
    mixed_grad[...] = total.astype(low)
    load = pltpu.make_async_copy(query_full, weight, local.at[0])
    load.start()

    staged = {}

    def weigh(left, right, out):
        for j in range(groups):
            slot = j % 2
            if slot in staged:
                staged.pop(slot).wait()
            value = product_tn(left[:, j * span : (j + 1) * span], right[...])
            stage[slot] = value.reshape(stage.shape[1:]).astype(low)
            copy = pltpu.make_async_copy(
                stage.at[slot], out.at[pl.ds(j * group, group)], stage_sem.at[slot]
            )
            copy.start()
            staged[slot] = copy
        for slot in list(staged):
            staged.pop(slot).wait()

    weigh(hidden_low, mixed, merge_term)
    ready[1] = 4 * planes
    move(2)

    key_floor = WINDOW - w.me * block
    j_at = lax.broadcasted_iota(jnp.int32, (extent, QUERY_ROWS), 0)
    i_at = lax.broadcasted_iota(jnp.int32, (extent, QUERY_ROWS), 1)
    for h in range(heads):
        columns = slice(h * HD, (h + 1) * HD)
        for start in range(0, block, QUERY_ROWS):
            rows = slice(start, start + QUERY_ROWS)
            query, pulled = queries[h, rows], mixed_grad[rows, columns]
            allowed = (j_at > i_at + start) & (j_at <= i_at + (start + WINDOW)) & (j_at >= key_floor)
            scores = jnp.where(allowed, product_nt(keys[...], query), masked_score)
            chances = jnp.exp(scores - log_total[h, :, rows])
            pulls = product_nt(values[...], pulled)
            inner = jnp.sum(chances * pulls, axis=0, keepdims=True)
            score_low = (chances * (pulls - inner)).astype(low)
            value_part = jnp.dot(chances.astype(low), pulled, preferred_element_type=jnp.float32)
            key_part = jnp.dot(score_low, query, preferred_element_type=jnp.float32)
            if h or start:
                sums[0] += key_part
                sums[1] += value_part
            else:
                sums[0] = key_part
                sums[1] = value_part
            turned_back = product_tn(score_low, keys[...]) * HD ** (-0.5)
            query_grad[rows, columns] = turned(turned_back, cosine[rows], -sine[rows]).astype(low)
            move()

    outgoing[...] = sums[1 - s].astype(low)
    pair = send(outgoing, arrived_sums, pair_sem.at[2], pair_sem.at[3], w.twin())
    weigh(normed, query_grad, query_term)
    move(1)
    empty = jnp.zeros((PLANE * block, HD), low)
    frame[0 : PLANE * block] = empty
    frame[reach * PLANE * block :] = empty
    pair.wait_recv()
    window = pl.ds(pl.multiple_of(xy * block, block), extent)
    frame[window] = (sums[s] + arrived_sums[...].astype(jnp.float32)).astype(low)
    halo = HaloReturn(w, frame, crossed, falling, landed, reach, return_sems)
    halo.begin()

    load.wait()
    for j in range(groups):
        piece = flat_rows(weight[j * group : (j + 1) * group])
        wide[:, j * span : (j + 1) * span] = product_nt(query_grad[...], piece)
    narrow[...] = wide[other].astype(low)
    pair_two = send(narrow, arrived, pair_sem.at[4], pair_sem.at[5], w.twin())
    move(2)
    for back in reversed(range(1, reach + 1)):
        halo.drop(back)
    move(2)
    pair_two.wait_recv()
    normone[...] = wide[ours] + arrived[...].astype(jnp.float32)
    halo.land(home)

    @pl.when(s == 0)
    def _():
        home[...] = turned(home[...], cosine[...], -sine[...])

    keyval_low[s] = home[...].astype(low)
    pair_three = send(
        keyval_low.at[s], keyval_low.at[s], pair_sem.at[6], pair_sem.at[7], w.twin()
    )
    move(2)
    there = keyval_low.at[1 - s]
    pltpu.make_async_copy(there, there, pair_sem.at[7]).wait()
    keyval_out[...] = keyval_low[...]
    for i in range(2):
        value = product_tn(normed_columns[...], keyval_low[i])
        keyval_term[:, :, :, i * HD : (i + 1) * HD] = value.reshape(
            keyval_term.shape[:3] + (HD,)
        ).astype(low)
    ready[1] = 6 * planes

    move(4 * len(pieces) + 12)
    for copy in (pair, pair_two, pair_three):
        copy.wait_send()
    keep.wait()
    for copy in feed_copies:
        copy.wait()
    halo.close()
    for ring in (early_ring, late_ring, deep_ring, small_ring):
        ring.close()
    for part in parts:
        part.close()


def rear(
    backs,
    feeds,
    hidden,
    pull,
    gain,
    merge_full,
    query_full,
    mixed,
    queries,
    keys,
    values,
    log_total,
    cosine,
    sine,
    normed,
    normed_columns,
    late_terms,
    early_terms,
    early_fars,
):
    planes = lax.axis_size("ctx") // PLANE
    block, width = normed.shape
    share = block // 2
    heads = queries.shape[0]
    reach = WINDOW // (PLANE * block)
    extent = WINDOW + block
    low, full = jnp.bfloat16, jnp.float32
    some, near = pl.BlockSpec(memory_space=pl.ANY), pl.BlockSpec(memory_space=pltpu.VMEM)
    shape = jax.ShapeDtypeStruct
    dma = pltpu.SemaphoreType.DMA
    group = planes_at_once(planes, merge_full.shape[2])
    keyval_rows = normed_columns.shape[1] // (planes * PLANE)
    deep = merge_full.shape[2:]
    sizes = [late_terms[0].shape[2:]] * 3 + [deep] * 2 + [(keyval_rows, 2 * HD)]
    all_sizes = [early_terms[0].shape[2:]] * 3 + sizes
    rings = [ring_scratch(*all_sizes[i]) for i in (0, 3, 6, 8)]
    outs = pl.pallas_call(
        partial(rear_kernel, planes),
        out_shape=[
            shape((planes, share, width), low),
            shape((share, width), full),
            shape((1, width), full),
            shape((share, width), full),
            shape((2, block, HD), low),
            shape(merge_full.shape, low),
            shape(query_full.shape, low),
        ]
        + [shape((planes,) + size, low) for size in all_sizes]
        + [shape((planes, 2) + size, low) for size in sizes]
        + [shape((planes,) + size, low) for size in all_sizes],
        in_specs=[near, some, near, near, near, some, some] + [near] * 9 + [some] * 9,
        out_specs=[some, near, near, near, near, some, some] + [some] * 24,
        scratch_shapes=[
            pltpu.VMEM(merge_full.shape, low),
            pltpu.VMEM((2, group) + merge_full.shape[1:], low),
            pltpu.VMEM((planes, PLANE, keyval_rows, 2 * HD), low),
            pltpu.VMEM((block, width), low),
            pltpu.VMEM((block, heads * HD), low),
            pltpu.VMEM((block, heads * HD), low),
            pltpu.VMEM((2, extent, HD), full),
            pltpu.VMEM((extent, HD), low),
            pltpu.VMEM((extent, HD), low),
            pltpu.VMEM(((reach + 1) * PLANE * block, HD), low),
            pltpu.VMEM((reach + 1, PLANE - 1, block, HD), low),
            pltpu.VMEM((reach, block, HD), low),
            pltpu.VMEM((reach, block, HD), low),
            pltpu.VMEM((block, HD), full),
            pltpu.VMEM((2, block, HD), low),
            pltpu.VMEM((block, width), full),
            pltpu.VMEM((share, width), low),
            pltpu.VMEM((share, width), low),
            dma((1,)),
            dma((2,)),
            dma((8,)),
            dma((planes,)),
            dma((planes,)),
        ]
        + [item for buffers, semaphores in rings for item in buffers + semaphores]
        + reduce_semaphores(planes, halfway=True) * 3
        + reduce_semaphores(planes) * 6
        + return_semaphores(reach),
        compiler_params=pltpu.CompilerParams(
            collective_id=2, has_side_effects=True, vmem_limit_bytes=62 * 2**20
        ),
    )(
        backs,
        feeds,
        hidden,
        pull,
        gain,
        merge_full,
        query_full,
        mixed,
        queries,
        keys,
        values,
        log_total,
        cosine,
        sine,
        normed,
        normed_columns,
        *late_terms,
        *early_terms,
        *early_fars,
    )
    return outs[:5], outs[7:16]


STEP_COLUMNS = 256


def middle_kernel(
    planes,
    depth,
    lanes,
    half,
    pulls,
    gate,
    upward,
    down,
    gate_rest,
    upward_rest,
    down_rest,
    back_out,
    feed_out,
    gate_term,
    upward_term,
    down_term,
    *refs,
):
    wholes, terms, fars, rest = split(refs, (3, 3, 3, len(refs) - 9))
    (
        early,
        late,
        rows,
        grads,
        early_acts,
        late_acts,
        own,
        outgoing,
        incoming,
        sums,
        stage,
        local,
        row_local,
        stage_sem,
        pair_sent,
        pair_received,
        back_sent,
        back_received,
        feed_local,
    ), rest = split(rest, (19, len(rest) - 19))
    spread_sems, cross_sems, column_sems = split(rest, (9, 6, 5))
    w = Wires(planes)
    z = w.z
    share, width = half.shape
    count = planes * 2 * share
    greet(w.partners() + [w.twin()])
    column = Column(w, half, rows, column_sems)
    column.rise()
    loads = [
        pltpu.make_async_copy(source, early.at[i], local.at[i])
        for i, source in enumerate((gate, upward, down))
    ]
    for load in loads:
        load.start()
    pulled = []
    for k in range(planes):
        at = flip(z, k)
        pulled.append(pltpu.make_async_copy(pulls.at[at], grads.at[at], row_local.at[k]))
        pulled[k].start()
    spreads = [
        Spread(w, "column", source, whole, spread_sems[3 * i : 3 * i + 3])
        for i, (source, whole) in enumerate(zip((gate_rest, upward_rest, down_rest), wholes))
    ]
    parts = [
        Cross(w, term, far, cross_sems[2 * i : 2 * i + 2])
        for i, (term, far) in enumerate(zip(terms, fars))
    ]

    for part in spreads:
        part.rise()
        for kz in range(planes):
            part.spread(kz)
    steps = [partial(part.relay, kz) for part in spreads for kz in range(planes)]

    def move(many=1):
        for _ in range(many):
            if steps:
                steps.pop(0)()

    def bend(k, weights, acts):
        units = weights.shape[4]
        here = flip(z, k)
        for at in range(0, units, STEP_COLUMNS):
            columns = slice(at, min(at + STEP_COLUMNS, units))
            gate_value, up_value, pull = (
                jnp.dot(
                    left[here],
                    flat_rows(weights[i, :, :, :, columns]),
                    preferred_element_type=jnp.float32,
                )
                for i, left in enumerate((rows, rows, grads))
            )
            bent, slope = gelu_parts(gate_value)
            acts[0, here, :, columns] = (pull * up_value * slope).astype(acts.dtype)
            acts[1, here, :, columns] = (pull * bent).astype(acts.dtype)
            acts[2, here, :, columns] = (bent * up_value).astype(acts.dtype)

    for load in loads:
        load.wait()
    waiting = ladder(planes)
    for k in range(planes):
        while k and k in waiting:
            column.pass_on(waiting.pop(0))
        column.ready(k)
        pulled[k].wait()
        bend(k, early, early_acts)
        move(2)

    group, span = stage.shape[1], stage.shape[1] * stage.shape[2] * stage.shape[3]
    groups = planes // group
    staged = {}
    turns = 0
    for i, left in enumerate((rows, rows, grads)):
        for j in range(groups):
            slot = turns % 2
            turns += 1
            if slot in staged:
                staged.pop(slot).wait()
            value = product_tn(
                left[:, :, j * span : (j + 1) * span].reshape(count, span),
                early_acts[i].reshape(count, -1),
            )
            stage[slot] = value.reshape(stage.shape[1:]).astype(stage.dtype)
            copy = pltpu.make_async_copy(
                stage.at[slot], terms[i].at[pl.ds(j * group, group)], stage_sem.at[slot]
            )
            copy.start()
            staged[slot] = copy
        move(2)
    for slot in list(staged):
        staged.pop(slot).wait()
    for kz in piece_order(planes):
        for part in parts:
            part.far_out(kz)
    move(len(steps))
    for part in spreads:
        part.settle()
    loads = [
        pltpu.make_async_copy(whole, late.at[i], local.at[i]) for i, whole in enumerate(wholes)
    ]
    for load in loads:
        load.start()

    def pair_copy(turn):
        return pltpu.make_async_remote_copy(
            src_ref=outgoing.at[turn % depth],
            dst_ref=incoming.at[turn % 2],
            send_sem=pair_sent.at[turn % depth],
            recv_sem=pair_received.at[turn % 2],
            device_id=w.twin(),
            device_id_type=MESH,
        )

    def offset(turn):
        return planes - 1 - turn

    def back_copy(turn):
        k = offset(turn)
        return pltpu.make_async_remote_copy(
            src_ref=sums.at[turn % lanes, 0],
            dst_ref=back_out.at[k],
            send_sem=back_sent.at[k],
            recv_sem=back_received.at[k],
            device_id=w.across(PLANE * k),
            device_id_type=MESH,
        )

    def kept_copy(turn):
        return pltpu.make_async_copy(sums.at[turn % lanes, 0], back_out.at[0], back_sent.at[0])

    def feed_copy(turn):
        return pltpu.make_async_copy(
            sums.at[turn % lanes, 1], feed_out.at[offset(turn)], feed_local.at[turn]
        )

    def shipped(turn):
        feed_copy(turn).wait()
        if turn == planes - 1:
            kept_copy(turn).wait()
        else:
            back_copy(turn).wait_send()

    def settle(turn):
        pair = pair_copy(turn)
        pair.wait_recv()
        pair.wait_send()
        if turn >= lanes:
            shipped(turn - lanes)
        for i in range(2):
            total = own[turn % depth, i] + incoming[turn % 2, i].astype(jnp.float32)
            sums[turn % lanes, i] = total.astype(sums.dtype)
        if turn == planes - 1:
            kept_copy(turn).start()
        else:
            back_copy(turn).start()
        feed_copy(turn).start()

    def sides(k, slot):
        here = flip(z, k)

        def both(weights, acts, i, at):
            return product_nt(acts[i, here], flat_rows(weights[i, at]))

        def part(j, _):
            columns = pl.ds(pl.multiple_of(j * span, 128), span)
            at = pl.ds(j * group, group)
            back = sum(
                both(weights, acts, i, at)
                for weights, acts in ((early, early_acts), (late, late_acts))
                for i in (0, 1)
            )
            feed = both(early, early_acts, 2, at) + both(late, late_acts, 2, at)
            for i, value in enumerate((back, feed)):
                own[slot, i, :, columns] = value[:share]
                outgoing[slot, i, :, columns] = value[share:].astype(outgoing.dtype)
            return 0

        lax.fori_loop(0, groups, part, 0)

    for load in loads:
        load.wait()
    for turn in range(planes):
        k = offset(turn)
        bend(k, late, late_acts)
        sides(k, turn % depth)
        if depth > 1 and turn > 0:
            settle(turn - 1)
        pair_copy(turn).start()
        if depth == 1:
            settle(turn)
    if depth > 1:
        settle(planes - 1)

    for i, left in enumerate((rows, rows, grads)):

        def weigh(j, _, i=i, left=left):
            columns = pl.ds(pl.multiple_of(j * span, 128), span)
            value = product_tn(
                left[:, :, columns].reshape(count, span), late_acts[i].reshape(count, -1)
            )
            value = value.reshape((group,) + late.shape[2:])
            late[i, pl.ds(j * group, group)] = value.astype(late.dtype)
            return 0

        lax.fori_loop(0, groups, weigh, 0)
        out = (gate_term, upward_term, down_term)[i]
        pltpu.make_async_copy(late.at[i], out, local.at[i]).start()
    for i, out in enumerate((gate_term, upward_term, down_term)):
        pltpu.make_async_copy(late.at[i], out, local.at[i]).wait()
    for turn in range(planes):
        if turn >= planes - lanes:
            shipped(turn)
        if turn < planes - 1:
            back_copy(turn).wait_recv()
    for part in spreads + parts + [column]:
        part.close()


def middle(half, pulls, gate, upward, down, gate_rest, upward_rest, down_rest):
    planes = lax.axis_size("ctx") // PLANE
    depth, lanes = (2, planes) if planes <= 4 else (1, 2)
    block, width = pulls.shape[1:]
    share = block // 2
    early, late = gate.shape[3], gate_rest.shape[2]
    rows = gate_rest.shape[1]
    low = jnp.bfloat16
    some = pl.BlockSpec(memory_space=pl.ANY)
    shape = jax.ShapeDtypeStruct
    dma = pltpu.SemaphoreType.DMA
    group = planes_at_once(planes, rows)
    outs = pl.pallas_call(
        partial(middle_kernel, planes, depth, lanes),
        out_shape=[shape((planes, share, width), low)] * 2
        + [shape((planes, PLANE, rows, late), low)] * 6
        + [shape((planes, PLANE, rows, early), low)] * 3
        + [shape((planes, 2, rows, early), low)] * 3,
        in_specs=[some] * 8,
        out_specs=[some] * 14,
        scratch_shapes=[
            pltpu.VMEM((3, planes, PLANE, rows, early), low),
            pltpu.VMEM((3, planes, PLANE, rows, late), low),
            pltpu.VMEM((planes, block, width), low),
            pltpu.VMEM((planes, block, width), low),
            pltpu.VMEM((3, planes, block, early), low),
            pltpu.VMEM((3, planes, block, late), low),
            pltpu.VMEM((depth, 2, share, width), jnp.float32),
            pltpu.VMEM((depth, 2, share, width), low),
            pltpu.VMEM((2, 2, share, width), low),
            pltpu.VMEM((lanes, 2, share, width), low),
            pltpu.VMEM((2, group, PLANE, rows, early), low),
            dma((3,)),
            dma((planes,)),
            dma((2,)),
            dma((depth,)),
            dma((2,)),
            dma((planes,)),
            dma((planes,)),
            dma((planes,)),
        ]
        + spread_semaphores(planes, "units") * 3
        + [dma((planes, 2))] * 6
        + column_semaphores(planes),
        compiler_params=pltpu.CompilerParams(
            collective_id=3, has_side_effects=True, vmem_limit_bytes=63 * 2**20
        ),
    )(half, pulls, gate, upward, down, gate_rest, upward_rest, down_rest)
    return outs[:2], outs[2:5], outs[8:11], outs[11:14]


def shards(
    tokens,
    cotangent,
    query_weight,
    query_first,
    query_second,
    keyval_weight,
    keyval_first,
    keyval_second,
    merge_weight,
    merge_first,
    merge_second,
    gate_weight,
    gate_first,
    gate_second,
    up_weight,
    up_first,
    up_second,
    down_weight,
    down_first,
    down_second,
    gains,
    gains_first,
    gains_second,
):
    low = jnp.bfloat16
    z, xy = place()
    s = lax.axis_index("shard")
    blocks = lax.axis_size("ctx")
    planes = blocks // PLANE
    row_count = tokens.shape[0]
    share = row_count // 2
    width = tokens.shape[1]

    def own_rows(value):
        return lax.dynamic_slice_in_dim(value, s * share, share, 0)

    small = jnp.concatenate([keyval_weight.astype(low), gains.astype(low)], axis=0).T
    small = jnp.pad(small, ((0, 0), (0, -small.shape[1] % 128)))
    small_all = open_gather(small)
    small_all = small_all.transpose(1, 2, 0, 3, 4).reshape(width, -1)
    keyval_full = small_all[:, : 2 * HD]
    gain_used = small_all[:, 2 * HD : 2 * HD + 2].T.astype(jnp.float32)

    offset = lax.axis_index("ctx") * row_count
    positions = offset + jnp.arange(row_count, dtype=jnp.int32)
    inputs = tokens.astype(jnp.float32)
    normed = normalize(inputs, gain_used[0]).astype(low)

    keyval = jnp.dot(normed, keyval_full, preferred_element_type=jnp.float32)
    keyval_mine = jnp.where(s == 0, rotate(keyval[:, :HD], positions), keyval[:, HD:]).astype(low)
    unit_weights = [unit_pieces(v) for v in (gate_weight, up_weight, down_weight)]
    early = early_units(unit_weights[0].shape[2])
    early_pieces = [v[:, :, :early] for v in unit_weights]
    late_pieces = [v[:, :, early:] for v in unit_weights]
    cosine, sine = rotary_tables(positions)
    (
        query_full,
        merge_full,
        gate_full,
        upward_full,
        down_full,
        *late_columns,
        pulls_all,
        queries,
        key_part,
        value_part,
        mixed_flat,
        log_total,
        hidden,
        normed_two,
    ) = front(
        normed,
        keyval_mine,
        cosine,
        sine,
        own_rows(tokens),
        gain_used[1:],
        own_rows(cotangent),
        query_weight.astype(low),
        merge_weight.astype(low),
        early_pieces,
        late_pieces,
    )
    input_rows = own_rows(inputs)

    (backs, feeds), late_terms, early_terms, early_fars = middle(
        normed_two, pulls_all, gate_full, upward_full, down_full, *late_columns
    )
    keyval_rows = width // blocks // 2
    normed_columns = pick(normed.reshape(row_count, blocks, 2, keyval_rows), s, 2)
    normed_columns = jnp.pad(normed_columns, ((0, 0), (0, 0), (0, -keyval_rows % 8)))
    (
        (feeds, hidden_grad, gain_two_grad, normone_grad, keyval_lin),
        (*unit_parts, merge_parts, query_parts, keyval_parts),
    ) = rear(
        backs,
        feeds,
        hidden,
        own_rows(cotangent),
        gain_used[1:],
        merge_full,
        query_full,
        mixed_flat,
        queries,
        key_part,
        value_part,
        log_total.reshape(log_total.shape[0], 1, -1),
        cosine,
        sine,
        normed,
        normed_columns.reshape(row_count, -1),
        late_terms,
        early_terms,
        early_fars,
    )
    gate_reduced, upward_reduced, down_reduced = (
        join_units(*g) for g in zip(unit_parts[:3], unit_parts[3:])
    )
    merge_reduced, query_reduced, keyval_sums = (
        jnp.sum(g.astype(jnp.float32), axis=0) for g in (merge_parts, query_parts, keyval_parts)
    )
    keyval_reduced = keyval_sums[:keyval_rows].T
    block_output = in_order((hidden + jnp.sum(feeds.astype(jnp.float32), axis=0)).astype(low))

    keyval_rows_lin = jnp.concatenate([own_rows(keyval_lin[0]), own_rows(keyval_lin[1])], axis=1)
    normone_grad = normone_grad + contract(keyval_rows_lin, keyval_full, 1, 1)
    gain_one_grad = jnp.sum(normone_grad * input_rows * inverse_rms(input_rows), axis=0)
    norm_one_pull = jax.vjp(partial(normalize, gain_row=gain_used[0]), input_rows)[1]
    tokens_grad = in_order(hidden_grad + norm_one_pull(normone_grad)[0])

    gain_terms = jnp.stack([gain_one_grad, gain_two_grad[0]]).reshape(2, blocks, 2, -1)
    gain_terms = gain_terms.transpose(2, 1, 0, 3)
    gain_sums = pick(gain_terms, s) + swap(pick(gain_terms, 1 - s))
    gains_reduced = reduce_small(gain_sums, jnp.float32)

    query_variance, query_updated = adamw(
        query_weight, query_first, query_second, query_reduced, 4.0 / math.sqrt(D)
    )
    keyval_variance, keyval_updated = adamw(
        keyval_weight, keyval_first, keyval_second, keyval_reduced, 2.0 / math.sqrt(D)
    )
    merge_variance, merge_updated = adamw(
        merge_weight, merge_first, merge_second, merge_reduced, 8.0 / math.sqrt(NH * HD)
    )
    gate_variance, gate_updated = adamw(
        gate_weight, gate_first, gate_second, gate_reduced, 2.0 / math.sqrt(D)
    )
    up_variance, up_updated = adamw(
        up_weight, up_first, up_second, upward_reduced, 2.0 / math.sqrt(D)
    )
    down_variance, down_updated = adamw(
        down_weight, down_first, down_second, down_reduced, 2.0 / math.sqrt(FF)
    )
    gains_variance, gains_updated = adamw(gains, gains_first, gains_second, gains_reduced, 0.8)
    return (
        block_output,
        tokens_grad,
        query_reduced,
        query_variance,
        query_updated,
        keyval_reduced,
        keyval_variance,
        keyval_updated,
        merge_reduced,
        merge_variance,
        merge_updated,
        gate_reduced,
        gate_variance,
        gate_updated,
        upward_reduced,
        up_variance,
        up_updated,
        down_reduced,
        down_variance,
        down_updated,
        gains_reduced,
        gains_variance,
        gains_updated,
    )


def solution(mesh):
    return jax.shard_map(
        shards,
        mesh=mesh,
        in_specs=(
            P("ctx", None),
            P("ctx", None),
            P("ctx", "shard"),
            P("ctx", "shard"),
            P("ctx", "shard"),
            P(None, ("ctx", "shard")),
            P(None, ("ctx", "shard")),
            P(None, ("ctx", "shard")),
            P("ctx", "shard"),
            P("ctx", "shard"),
            P("ctx", "shard"),
            P("ctx", "shard"),
            P("ctx", "shard"),
            P("ctx", "shard"),
            P("ctx", "shard"),
            P("ctx", "shard"),
            P("ctx", "shard"),
            P("ctx", "shard"),
            P("ctx", "shard"),
            P("ctx", "shard"),
            P(None, ("ctx", "shard")),
            P(None, ("ctx", "shard")),
            P(None, ("ctx", "shard")),
        ),
        out_specs=(
            P("ctx", None),
            P("ctx", None),
            P("ctx", "shard"),
            P("ctx", "shard"),
            P("ctx", "shard"),
            P(None, ("ctx", "shard")),
            P(None, ("ctx", "shard")),
            P(None, ("ctx", "shard")),
            P("ctx", "shard"),
            P("ctx", "shard"),
            P("ctx", "shard"),
            P("ctx", "shard"),
            P("ctx", "shard"),
            P("ctx", "shard"),
            P("ctx", "shard"),
            P("ctx", "shard"),
            P("ctx", "shard"),
            P("ctx", "shard"),
            P("ctx", "shard"),
            P("ctx", "shard"),
            P(None, ("ctx", "shard")),
            P(None, ("ctx", "shard")),
            P(None, ("ctx", "shard")),
        ),
        check_vma=False,
    )
```

```python
from functools import partial
import math

import jax
import jax.numpy as jnp
from jax import lax
from jax.experimental import pallas as pl
from jax.experimental.pallas import tpu as pltpu
from jax.sharding import PartitionSpec as P

D = 2560
NH = 10
HD = 256
FF = 7680
WINDOW = 2048
STEP = 10


beta_first = 0.9
beta_second = 0.95
adam_epsilon = 1e-08
weight_decay = 0.1
norm_epsilon = 1e-06
rotary_base = 10000.0
masked_score = -1e30


def inverse_rms(values):
    return lax.rsqrt(jnp.mean(values * values, axis=-1, keepdims=True) + norm_epsilon)


def normalize(values, gain_row):
    return values * inverse_rms(values) * gain_row


def gelu_product(gate_value, upward):
    return jax.nn.gelu(gate_value, approximate=True) * upward


def rotate(values, positions):
    quarter = values.shape[-1] // 4
    frequency = rotary_base ** (-jnp.arange(quarter, dtype=jnp.float32) / quarter)
    angles = positions.astype(jnp.float32)[:, None] * frequency[None, :]
    cosine = jnp.cos(angles)
    sine_part = jnp.sin(angles)
    lower_half = values[..., :quarter]
    upper_half = values[..., quarter : 2 * quarter]
    return jnp.concatenate(
        [
            lower_half * cosine - upper_half * sine_part,
            upper_half * cosine + lower_half * sine_part,
            values[..., 2 * quarter :],
        ],
        axis=-1,
    )


def rotary_tables(positions):
    quarter = HD // 4
    frequency = rotary_base ** (-jnp.arange(quarter, dtype=jnp.float32) / quarter)
    angles = positions.astype(jnp.float32)[:, None] * frequency[None, :]
    cosine, sine = jnp.cos(angles), jnp.sin(angles)
    return jnp.concatenate([cosine, cosine], axis=1), jnp.concatenate([-sine, sine], axis=1)


def contract(left, right, left_dim, right_dim):
    return lax.dot_general(
        left, right, (((left_dim,), (right_dim,)), ((), ())), preferred_element_type=jnp.float32
    )


def adamw(weight, first_moment, second_moment, gradient, rate_value):
    moment_new = beta_first * first_moment + (1.0 - beta_first) * gradient
    second_new = beta_second * second_moment + (1.0 - beta_second) * gradient * gradient
    step_size = (
        moment_new
        / (1.0 - beta_first**STEP)
        / (jnp.sqrt(second_new / (1.0 - beta_second**STEP)) + adam_epsilon)
    )
    return (second_new, weight - rate_value * (step_size + weight_decay * weight))


PLANE = 4


def hop(value, mask):
    count = lax.axis_size("ctx")
    return lax.ppermute(value, "ctx", [(i, i ^ mask) for i in range(count)])


def swap(value):
    count = lax.axis_size("shard")
    return lax.ppermute(value, "shard", [(i, count - 1 - i) for i in range(count)])


def place():
    me = lax.axis_index("ctx")
    return me // PLANE, me % PLANE


def pick(value, index, axis=0):
    return lax.dynamic_index_in_dim(value, index, axis, keepdims=False)


def put(buffer, piece, *start):
    return lax.dynamic_update_slice(
        buffer, piece, tuple(start) + (0,) * (buffer.ndim - len(start))
    )


def reduce_column(column, kind=jnp.bfloat16):
    z, _ = place()
    total = pick(column, z)
    for k in range(1, column.shape[0]):
        total = total + hop(pick(column, z ^ k).astype(kind), PLANE * k).astype(jnp.float32)
    return total


def reduce_small(terms, kind):
    _, xy = place()
    split = terms.reshape((-1, PLANE) + terms.shape[1:])
    column = pick(split, xy, 1)
    for m in range(1, PLANE):
        column = column + hop(pick(split, xy ^ m, 1).astype(kind), m).astype(jnp.float32)
    return reduce_column(column, kind)


def unit_pieces(weight):
    planes = lax.axis_size("ctx") // PLANE
    units = weight.shape[1] // planes
    low = weight.astype(jnp.bfloat16)
    return jnp.stack([low[:, j * units : (j + 1) * units] for j in range(planes)])


def early_units(units):
    return -(-(units // 2) // 128) * 128


def join_units(early, late):
    pieces = [p for pair in zip(early, late) for p in pair]
    return jnp.concatenate([p.astype(jnp.float32) for p in pieces], axis=1)


def in_order(half):
    s = lax.axis_index("shard")
    other = swap(half)
    first = jnp.where(s == 0, half, other)
    last = jnp.where(s == 0, other, half)
    return jnp.concatenate([first, last], axis=0)


MESH = pl.DeviceIdType.MESH


def flip(index, mask):
    result = index
    bit = 1
    while bit <= mask:
        if mask & bit:
            result = result + bit * (1 - 2 * ((index // bit) % 2))
        bit *= 2
    return result


def greet(partners):
    barrier = pltpu.get_barrier_semaphore()
    for device in partners:
        pl.semaphore_signal(barrier, inc=1, device_id=device, device_id_type=MESH)
    pl.semaphore_wait(barrier, len(partners))


def send(source, target, sent, received, device):
    copy = pltpu.make_async_remote_copy(
        src_ref=source,
        dst_ref=target,
        send_sem=sent,
        recv_sem=received,
        device_id=device,
        device_id_type=MESH,
    )
    copy.start()
    return copy


def routes(planes, kz):
    return (1, 2) if kz < planes // 2 else (2, 1)


def ladder(planes):
    return sorted(range(1, planes), key=lambda k: (bin(k).count("1"), -k))


def rungs(planes, k):
    bit, found = 1, []
    while bit < planes and not k & bit:
        found.append(bit)
        bit *= 2
    return found


class Wires:
    def __init__(self, planes):
        self.planes = planes
        self.me = lax.axis_index("ctx")
        self.s = lax.axis_index("shard")
        self.z = self.me // PLANE
        self.xy = self.me % PLANE

    def across(self, mask):
        return (flip(self.me, mask), self.s)

    def twin(self):
        return (self.me, 1 - self.s)

    def partners(self):
        return [self.across(PLANE * k) for k in range(1, self.planes)] + [
            self.across(1),
            self.across(2),
        ]


def gelu_parts(u):
    scale = math.sqrt(2.0 / math.pi)
    square = u * u
    bend = jnp.tanh(scale * u * (1.0 + 0.044715 * square))
    half = 0.5 * (1.0 + bend)
    slope = half + 0.5 * u * (1.0 - bend * bend) * scale * (1.0 + 3.0 * 0.044715 * square)
    return u * half, slope


def product_nt(left, right):
    return lax.dot_general(
        left, right, (((1,), (1,)), ((), ())), preferred_element_type=jnp.float32
    )


def product_tn(left, right):
    return lax.dot_general(
        left, right, (((0,), (0,)), ((), ())), preferred_element_type=jnp.float32
    )


class Spread:
    def __init__(self, w, kind, source, whole, semaphores):
        self.w, self.kind, self.source = w, kind, source
        self.own_sem, self.sent, self.received, *twin = semaphores
        self.everything = whole
        self.whole = whole.at[w.s] if kind == "pair" else whole
        self.twin = twin
        self.copies = []
        if kind == "column":
            self.keep = pltpu.make_async_copy(source, whole.at[:, w.xy], self.own_sem.at[0])
        else:
            self.keep = pltpu.make_async_copy(self.mine(0), self.spot(0, 0), self.own_sem.at[0])

    def mine(self, k):
        split = self.kind in ("units", "column")
        return self.source.at[flip(self.w.z, k)] if split else self.source

    def spot(self, kz, m):
        return self.whole.at[flip(self.w.z, kz), flip(self.w.xy, m)]

    def push(self, kz, m, slot, source, target, device):
        self.copies.append(
            send(source, target, self.sent.at[slot, kz], self.received.at[kz, m], device)
        )

    def wait_for(self, kz, m):
        there = self.spot(kz, m)
        pltpu.make_async_copy(there, there, self.received.at[kz, m]).wait()
        if self.kind == "pair":
            self.hand_over(kz, m, there)

    def hand_over(self, kz, m, piece):
        self.copies.append(
            send(
                piece,
                self.spot(kz, m),
                self.twin[0].at[kz, m],
                self.twin[1].at[kz, m],
                self.w.twin(),
            )
        )

    def rise(self):
        self.keep.start()
        if self.kind == "pair":
            self.hand_over(0, 0, self.source)
        if self.kind == "units":
            for k in range(1, self.w.planes):
                self.push(k, 0, 0, self.mine(k), self.spot(0, 0), self.w.across(PLANE * k))
        elif self.kind != "column":
            self.climb(0)

    def climb(self, kz):
        piece = self.spot(kz, 0) if kz else self.source
        for bit in rungs(self.w.planes, kz):
            self.push(kz | bit, 0, 0, piece, self.spot(kz, 0), self.w.across(PLANE * bit))

    def spread(self, kz):
        first, second = routes(self.w.planes, kz)
        if kz and self.kind != "column":
            self.wait_for(kz, 0)
            if self.kind != "units":
                self.climb(kz)
        mine = self.spot(kz, 0) if kz and self.kind != "column" else self.mine(kz)
        self.push(kz, first, 1, mine, self.spot(kz, 0), self.w.across(first))
        self.push(kz, second, 2, mine, self.spot(kz, 0), self.w.across(second))

    def relay(self, kz):
        first, second = routes(self.w.planes, kz)
        self.wait_for(kz, first)
        there = self.spot(kz, first)
        self.push(kz, 3, 3, there, there, self.w.across(second))

    def settle(self):
        planes = self.w.planes
        for kz in range(planes):
            first, second = routes(planes, kz)
            self.wait_for(kz, second)
            self.wait_for(kz, 3)
        self.keep.wait()

    def close(self):
        if self.kind == "pair":
            for kz in range(self.w.planes):
                for m in range(PLANE):
                    there = self.everything.at[
                        1 - self.w.s, flip(self.w.z, kz), flip(self.w.xy, m)
                    ]
                    pltpu.make_async_copy(there, there, self.twin[1].at[kz, m]).wait()
        for copy in self.copies:
            copy.wait_send()

    def steps(self):
        last = 0
        for kz in ladder(self.w.planes):
            yield partial(self.spread, kz)
            yield partial(self.relay, last)
            last = kz
        yield partial(self.relay, last)


def spread_semaphores(planes, kind):
    dma = pltpu.SemaphoreType.DMA
    kinds = [dma((1,)), dma((4, planes)), dma((planes, PLANE))]
    return kinds + [dma((planes, PLANE))] * 2 if kind == "pair" else kinds


class Column:
    def __init__(self, w, half, whole, semaphores):
        self.w, self.half, self.whole = w, half, whole
        self.own_sem, self.sent, self.received, self.twin_sent, self.twin_received = semaphores
        self.share = half.shape[0]
        self.keep = pltpu.make_async_copy(half, self.spot(0, 0), self.own_sem.at[0])
        self.copies = []

    def spot(self, k, part):
        return self.whole.at[flip(self.w.z, k), pl.ds(part * self.share, self.share)]

    def climb(self, k):
        piece = self.spot(k, 0) if k else self.half
        for bit in rungs(self.w.planes, k):
            self.copies.append(
                send(
                    piece,
                    self.spot(k, 0),
                    self.sent.at[k | bit],
                    self.received.at[k | bit],
                    self.w.across(PLANE * bit),
                )
            )

    def rise(self):
        self.keep.start()
        self.climb(0)
        self.hand_over(0)

    def pass_on(self, k):
        there = self.spot(k, 0)
        pltpu.make_async_copy(there, there, self.received.at[k]).wait()
        self.climb(k)
        self.hand_over(k)

    def hand_over(self, k):
        self.copies.append(
            send(
                self.spot(k, 0) if k else self.half,
                self.spot(k, 1),
                self.twin_sent.at[k],
                self.twin_received.at[k],
                self.w.twin(),
            )
        )

    def ready(self, k):
        if k == 0:
            self.keep.wait()
        there = self.spot(k, 1)
        pltpu.make_async_copy(there, there, self.twin_received.at[k]).wait()

    def close(self):
        for copy in self.copies:
            copy.wait_send()


class Deal:
    def __init__(self, w, pieces, whole, semaphores):
        self.w, self.pieces, self.whole = w, pieces, whole
        self.own_sem, self.sent, self.received = semaphores
        self.keep = pltpu.make_async_copy(pieces.at[w.z], whole.at[w.z], self.own_sem.at[0])
        self.copies = []

    def rise(self):
        w = self.w
        self.keep.start()
        for k in range(1, w.planes):
            self.copies.append(
                send(
                    self.pieces.at[flip(w.z, k)],
                    self.whole.at[w.z],
                    self.sent.at[k],
                    self.received.at[k],
                    w.across(PLANE * k),
                )
            )

    def close(self):
        self.keep.wait()
        for k in range(1, self.w.planes):
            there = self.whole.at[flip(self.w.z, k)]
            pltpu.make_async_copy(there, there, self.received.at[k]).wait()
        for copy in self.copies:
            copy.wait_send()


def deal_semaphores(planes):
    dma = pltpu.SemaphoreType.DMA
    return [dma((1,)), dma((planes,)), dma((planes,))]


def column_semaphores(planes):
    return [pltpu.SemaphoreType.DMA((1,))] + [pltpu.SemaphoreType.DMA((planes,))] * 4


def split(refs, sizes):
    at, groups = 0, []
    for size in sizes:
        groups.append(refs[at : at + size])
        at += size
    return groups


def open_kernel(planes, small, small_out, *semaphores):
    w = Wires(planes)
    greet(w.partners() + [w.twin()])
    part = Spread(w, "pair", small, small_out, semaphores)
    part.rise()
    part.spread(0)
    for step in part.steps():
        step()
    part.settle()
    part.close()


def open_gather(small):
    planes = lax.axis_size("ctx") // PLANE
    some = pl.BlockSpec(memory_space=pl.ANY)
    return pl.pallas_call(
        partial(open_kernel, planes),
        out_shape=jax.ShapeDtypeStruct((2, planes, PLANE) + small.shape, small.dtype),
        in_specs=[some],
        out_specs=some,
        scratch_shapes=spread_semaphores(planes, "pair"),
        compiler_params=pltpu.CompilerParams(collective_id=1, has_side_effects=True),
    )(small)


class Halo:
    def __init__(self, w, mine, frame, reach, semaphores):
        self.w, self.mine, self.frame, self.reach = w, mine, frame, reach
        (
            self.own_sem,
            self.climb_sent,
            self.climb_received,
            self.sent,
            self.received,
            self.twin_sent,
            self.twin_received,
        ) = semaphores

    def there(self, back):
        return self.w.z >= back

    def spot(self, back, m, part=None):
        part = self.w.s if part is None else part
        return self.frame.at[part, self.rows(back, flip(self.w.xy, m))]

    def rows(self, back, xy):
        block = self.mine.shape[0]
        start = ((self.reach - back) * PLANE + xy) * block
        return pl.ds(pl.multiple_of(start, block), block)

    def keep(self):
        return pltpu.make_async_copy(self.mine, self.spot(0, 0), self.own_sem.at[0])

    def climb(self, back):
        w = self.w
        return pltpu.make_async_remote_copy(
            src_ref=self.mine,
            dst_ref=self.spot(back, 0),
            send_sem=self.climb_sent.at[back],
            recv_sem=self.climb_received.at[back],
            device_id=(lax.rem(w.me + PLANE * back, PLANE * w.planes), w.s),
            device_id_type=MESH,
        )

    def cross(self, back, m):
        return pltpu.make_async_remote_copy(
            src_ref=self.spot(back, 0),
            dst_ref=self.spot(back, 0),
            send_sem=self.sent.at[back, m],
            recv_sem=self.received.at[back, m],
            device_id=self.w.across(m),
            device_id_type=MESH,
        )

    def hand_over(self, back, m):
        return pltpu.make_async_remote_copy(
            src_ref=self.spot(back, m),
            dst_ref=self.spot(back, m),
            send_sem=self.twin_sent.at[back, m],
            recv_sem=self.twin_received.at[back, m],
            device_id=self.w.twin(),
            device_id_type=MESH,
        )

    def begin(self):
        w = self.w
        self.keep().start()
        for back in range(1, self.reach + 1):

            @pl.when(w.z + back < w.planes)
            def _(back=back):
                self.climb(back).start()

            @pl.when(w.z < back)
            def _(back=back):
                block = self.mine.shape[0]
                empty = jnp.zeros((2, PLANE * block, HD), self.frame.dtype)
                self.frame[:, pl.ds((self.reach - back) * PLANE * block, PLANE * block)] = empty

        self.keep().wait()
        self.share(0)

    def share(self, back):
        for m in range(1, PLANE):
            self.cross(back, m).start()
        self.hand_over(back, 0).start()

    def forward(self, back):
        @pl.when(self.there(back))
        def _():
            self.climb(back).wait_recv()
            self.share(back)

    def collect(self, back):
        @pl.when(self.there(back))
        def _():
            for m in range(1, PLANE):
                self.cross(back, m).wait_recv()
                self.hand_over(back, m).start()

    def settle(self, back):
        @pl.when(self.there(back))
        def _():
            for m in range(PLANE):
                landed = self.spot(back, m, 1 - self.w.s)
                pltpu.make_async_copy(landed, landed, self.twin_received.at[back, m]).wait()

    def close(self):
        for back in range(self.reach + 1):

            @pl.when(self.there(back))
            def _(back=back):
                for m in range(PLANE):
                    if m:
                        self.cross(back, m).wait_send()
                    self.hand_over(back, m).wait_send()

            if back:

                @pl.when(self.w.z + back < self.w.planes)
                def _(back=back):
                    self.climb(back).wait_send()


def halo_semaphores(reach):
    dma = pltpu.SemaphoreType.DMA
    return [dma((1,))] + [dma((reach + 1,))] * 2 + [dma((reach + 1, PLANE))] * 4


def turned(value, cosine, sine):
    front = value[:, : HD // 2]
    rolled = pltpu.roll(front, HD // 4, 1)
    return jnp.concatenate([front * cosine + rolled * sine, value[:, HD // 2 :]], axis=1)


QUERY_ROWS = 128


def window_mask(first_row, rows, extent, key_floor):
    i = lax.broadcasted_iota(jnp.int32, (rows, extent), 0) + first_row
    j = lax.broadcasted_iota(jnp.int32, (rows, extent), 1)
    return (j > i) & (j <= i + WINDOW) & (j >= key_floor)


def flat_rows(pieces):
    width = pieces.shape[-1]
    if pieces.shape[-2] % 16:
        return pieces.astype(jnp.float32).reshape(-1, width).astype(pieces.dtype)
    return pieces.reshape(-1, width)


def planes_at_once(planes, rows):
    group = 1
    while group * PLANE * rows % 128:
        group *= 2
    return min(group, planes)


def front_kernel(
    planes,
    normed,
    keyval,
    cosine,
    sine,
    inputs,
    gain,
    pull,
    query,
    merge,
    gate,
    upward,
    down,
    gate_rest,
    upward_rest,
    down_rest,
    query_out,
    merge_out,
    gate_out,
    upward_out,
    down_out,
    gate_rest_out,
    upward_rest_out,
    down_rest_out,
    pulls_out,
    queries,
    key_out,
    value_out,
    mixed,
    log_total,
    hidden,
    normed_two,
    query_full,
    merge_full,
    frame,
    branch,
    arrived,
    local,
    pair_sem,
    *semaphores,
):
    w = Wires(planes)
    parts = split(semaphores, (3, 3, 3, 3, 3, 5, 7, 3, 3, 3))
    heads = queries.shape[0]
    block, width = normed.shape
    share = block // 2
    reach = WINDOW // (PLANE * block)
    extent = WINDOW + block
    low = jnp.bfloat16
    greet(w.partners() + [w.across(3), w.twin()])
    spreads = [
        Spread(w, kind, source, whole, sems)
        for kind, source, whole, sems in zip(
            ("rows", "rows", "units", "units", "units"),
            (query, merge, gate, upward, down),
            (query_full, merge_full, gate_out, upward_out, down_out),
            parts[:5],
        )
    ]
    pulls = Column(w, pull, pulls_out, parts[5])
    halo = Halo(w, keyval, frame, reach, parts[6])
    deals = [
        Deal(w, pieces, whole, sems)
        for pieces, whole, sems in zip(
            (gate_rest, upward_rest, down_rest),
            (gate_rest_out, upward_rest_out, down_rest_out),
            parts[7:],
        )
    ]

    steps, ends = [], []
    for i, part in enumerate(spreads):
        following = spreads[i + 1] if i + 1 < len(spreads) else None
        moves = list(part.steps())
        if following:
            moves.insert(len(moves) - 1, partial(following.spread, 0))
        if i == 0:
            moves.insert(2, following.rise)
        if i == 1:
            for at, later in enumerate(spreads[2:]):
                moves.insert(2 * at, later.rise)
        if i == 2:
            moves.insert(1, pulls.rise)
        if i == 3:
            moves.insert(1, deals[0].rise)
            moves.insert(4, deals[1].rise)
        if i == 4:
            moves.insert(1, deals[2].rise)
        steps += moves
        ends.append(len(steps))
    done = [0]

    def move(many=1, upto=None):
        stop = min(done[0] + many if upto is None else upto, len(steps))
        while done[0] < stop:
            steps[done[0]]()
            done[0] += 1

    halo.begin()
    spreads[0].rise()
    spreads[0].spread(0)
    move(2)
    for back in range(1, reach + 1):
        halo.forward(back)
    move(3)
    for back in range(reach + 1):
        halo.collect(back)
    move(upto=ends[0] + 2)
    for back in range(reach + 1):
        halo.settle(back)
    window = pl.ds(pl.multiple_of(w.xy * block, block), extent)
    key_out[...] = frame[0, window]
    value_out[...] = frame[1, window]
    spreads[0].settle()
    keep_query = pltpu.make_async_copy(query_full, query_out, local.at[0])
    keep_query.start()

    group = planes_at_once(planes, merge_full.shape[2])
    span = group * PLANE * merge_full.shape[2]
    groups = planes // group
    for h in range(heads):
        columns = slice(h * HD, (h + 1) * HD)
        total = None
        for j in range(groups):
            piece = flat_rows(query_full[j * group : (j + 1) * group, :, :, columns])
            value = jnp.dot(
                normed[:, j * span : (j + 1) * span], piece, preferred_element_type=jnp.float32
            )
            total = value if total is None else total + value
        queries[h] = (turned(total, cosine[...], sine[...]) * HD ** (-0.5)).astype(low)
    move()

    key_floor = WINDOW - w.me * block
    for h in range(heads):
        for start in range(0, block, QUERY_ROWS):
            rows = pl.ds(start, QUERY_ROWS)
            scores = product_nt(queries[h, rows], key_out[...])
            allowed = window_mask(start, QUERY_ROWS, extent, key_floor)
            scores = jnp.where(allowed, scores, masked_score)
            peak = jnp.max(scores, axis=-1, keepdims=True)
            shifted = jnp.exp(scores - peak)
            total = jnp.sum(shifted, axis=-1, keepdims=True)
            log_total[h, rows] = peak + jnp.log(total)
            chances = (shifted / total).astype(low)
            value = jnp.dot(chances, value_out[...], preferred_element_type=jnp.float32)
            mixed[rows, h * HD : (h + 1) * HD] = value.astype(low)
            move()
    move(upto=ends[1] + 2)
    spreads[1].settle()
    keep_merge = pltpu.make_async_copy(merge_full, merge_out, local.at[1])
    keep_merge.start()

    for j in range(groups):
        piece = flat_rows(merge_full[j * group : (j + 1) * group])
        branch[:, j * span : (j + 1) * span] = product_nt(mixed[...], piece)
    ours = pl.ds(pl.multiple_of(w.s * share, share), share)
    other = pl.ds(pl.multiple_of((1 - w.s) * share, share), share)
    pair = send(branch.at[other], arrived, pair_sem.at[0], pair_sem.at[1], w.twin())
    move(2)
    pair.wait_recv()
    value = inputs[...].astype(jnp.float32) + branch[ours] + arrived[...]
    hidden[...] = value
    inverse = lax.rsqrt(jnp.mean(value * value, axis=-1, keepdims=True) + norm_epsilon)
    normed_two[...] = (value * inverse * gain[...]).astype(low)
    move(upto=len(steps))
    for k in ladder(planes):
        pulls.pass_on(k)
    for part in spreads[2:]:
        part.settle()
    pair.wait_send()
    keep_query.wait()
    keep_merge.wait()
    for k in range(planes):
        pulls.ready(k)
    for part in (*spreads, *deals, pulls, halo):
        part.close()


def front(normed, keyval, cosine, sine, inputs, gain, pull, query, merge, early, late):
    planes = lax.axis_size("ctx") // PLANE
    block, width = normed.shape
    share = block // 2
    heads = query.shape[1] // HD
    reach = WINDOW // (PLANE * block)
    extent = WINDOW + block
    low = jnp.bfloat16
    some, near = pl.BlockSpec(memory_space=pl.ANY), pl.BlockSpec(memory_space=pltpu.VMEM)
    shape = jax.ShapeDtypeStruct
    dma = pltpu.SemaphoreType.DMA
    return pl.pallas_call(
        partial(front_kernel, planes),
        out_shape=[
            shape((planes, PLANE) + piece.shape[-2:], low)
            for piece in (query, merge, *early)
        ]
        + [shape(piece.shape, low) for piece in late]
        + [
            shape((planes, block, width), low),
            shape((heads, block, HD), low),
            shape((extent, HD), low),
            shape((extent, HD), low),
            shape((block, heads * HD), low),
            shape((heads, block, 1), jnp.float32),
            shape((share, width), jnp.float32),
            shape((share, width), low),
        ],
        in_specs=[near, some, near, near, near, near] + [some] * 9,
        out_specs=[some] * 9 + [near] * 7,
        scratch_shapes=[
            pltpu.VMEM((planes, PLANE) + query.shape, low),
            pltpu.VMEM((planes, PLANE) + merge.shape, low),
            pltpu.VMEM((2, (reach + 1) * PLANE * block, HD), low),
            pltpu.VMEM((block, width), jnp.float32),
            pltpu.VMEM((share, width), jnp.float32),
            dma((2,)),
            dma((2,)),
        ]
        + spread_semaphores(planes, "rows") * 2
        + spread_semaphores(planes, "units") * 3
        + column_semaphores(planes)
        + halo_semaphores(reach)
        + deal_semaphores(planes) * 3,
        compiler_params=pltpu.CompilerParams(
            collective_id=4, has_side_effects=True, vmem_limit_bytes=60 * 2**20
        ),
    )(normed, keyval, cosine, sine, inputs, gain, pull, query, merge, *early, *late)


KEPT = 8
LOADED = 2
LAG = 9


class Ring:
    def __init__(self, buffers, semaphores):
        self.near, self.column = buffers[:2], buffers[2:]
        self.near_loaded, self.column_loaded = semaphores
        self.counts = [0, 0]
        self.leaving = {}

    def take(self, stage):
        slot, spare = self.counts[stage] % KEPT, self.counts[stage] % LOADED
        self.counts[stage] += 1
        copy = self.leaving.pop((stage, slot), None)
        if copy is not None:
            copy()
        return slot, spare

    def close(self):
        for copy in self.leaving.values():
            copy()


def ring_scratch(rows, width):
    kept, loaded = (pltpu.VMEM((depth, rows, width), jnp.bfloat16) for depth in (KEPT, LOADED))
    dma = pltpu.SemaphoreType.DMA
    return [kept, loaded, kept, loaded, loaded], [dma((LOADED, 2)), dma((LOADED, 3))]


class Reduce:
    def __init__(self, w, ring, term, result, far, near, semaphores, halfway=False):
        self.w, self.ring, self.term, self.result = w, ring, term, result
        self.far, self.near, self.halfway = far, near, halfway
        self.sent, self.received, *self.far_sems = semaphores
        self.copies = []
        self.slots = {}

    def piece(self, kz, m):
        return self.term.at[flip(self.w.z, kz), flip(self.w.xy, m)]

    def far_out(self, kz):
        first, second = routes(self.w.planes, kz)
        for slot, m in ((1, 3), (0, second)):
            self.copies.append(
                send(
                    self.piece(kz, m),
                    self.far.at[kz, slot],
                    self.far_sems[0].at[kz, slot],
                    self.far_sems[1].at[kz, slot],
                    self.w.across(second),
                )
            )

    def arrived(self, there, semaphore):
        pltpu.make_async_copy(there, there, semaphore).wait()

    def far_in(self, kz, slot):
        if not self.halfway:
            self.arrived(self.far.at[kz, slot], self.far_sems[1].at[kz, slot])

    def near_in(self, kz):
        first, _ = routes(self.w.planes, kz)
        slot, spare = self.ring.take(0)
        loads = [
            pltpu.make_async_copy(source, buffer, self.ring.near_loaded.at[spare, i])
            for i, (source, buffer) in enumerate(
                (
                    (self.piece(kz, first), self.ring.near[0].at[slot]),
                    (self.far.at[kz, 1], self.ring.near[1].at[spare]),
                )
            )
        ]
        loads[0].start()
        self.far_in(kz, 1)
        loads[1].start()
        self.slots[0, kz] = slot, spare, loads

    def near_out(self, kz):
        first, _ = routes(self.w.planes, kz)
        slot, spare, loads = self.slots.pop((0, kz))
        for load in loads:
            load.wait()
        a, b = self.ring.near
        a[slot] = (a[slot].astype(jnp.float32) + b[spare].astype(jnp.float32)).astype(a.dtype)
        copy = send(
            a.at[slot], self.near.at[kz], self.sent.at[0, kz], self.received.at[0, kz],
            self.w.across(first),
        )
        self.ring.leaving[0, slot] = copy.wait_send

    def column_in(self, kz):
        slot, spare = self.ring.take(1)
        sources = (self.piece(kz, 0), self.far.at[kz, 0], self.near.at[kz])
        loads = [
            pltpu.make_async_copy(
                source,
                buffer.at[spare if i else slot],
                self.ring.column_loaded.at[spare, i],
            )
            for i, (source, buffer) in enumerate(zip(sources, self.ring.column))
        ]
        loads[0].start()
        self.far_in(kz, 0)
        loads[1].start()
        self.arrived(self.near.at[kz], self.received.at[0, kz])
        loads[2].start()
        self.slots[1, kz] = slot, spare, loads

    def column_out(self, kz):
        slot, spare, loads = self.slots.pop((1, kz))
        for load in loads:
            load.wait()
        a, b, c = self.ring.column
        total = sum(v.astype(jnp.float32) for v in (a[slot], b[spare], c[spare]))
        a[slot] = total.astype(a.dtype)
        target = self.result.at[self.w.z]
        if kz:
            copy = send(
                a.at[slot], target, self.sent.at[1, kz], self.received.at[1, kz],
                self.w.across(PLANE * kz),
            )
            self.ring.leaving[1, slot] = copy.wait_send
        else:
            copy = pltpu.make_async_copy(a.at[slot], target, self.sent.at[1, 0])
            copy.start()
            self.ring.leaving[1, slot] = copy.wait

    def close(self):
        for k in range(1, self.w.planes):
            self.arrived(self.result.at[flip(self.w.z, k)], self.received.at[1, k])
        for copy in self.copies:
            copy.wait_send()


def reduce_semaphores(planes, halfway=False):
    dma = pltpu.SemaphoreType.DMA
    return [dma((2, planes))] * 2 + ([] if halfway else [dma((planes, 2))] * 2)


class Cross(Reduce):
    def __init__(self, w, term, far, semaphores):
        self.w, self.term, self.far, self.halfway = w, term, far, False
        self.far_sems, self.copies = semaphores, []

    def close(self):
        for kz in range(self.w.planes):
            for slot in range(2):
                self.far_in(kz, slot)
        for copy in self.copies:
            copy.wait_send()


def piece_order(planes):
    half = planes // 2
    return [k for pair in zip(reversed(range(half, planes)), reversed(range(half))) for k in pair]


class HaloReturn:
    def __init__(self, w, frame, crossed, falling, landed, reach, semaphores):
        self.w, self.frame, self.crossed = w, frame, crossed
        self.falling, self.landed, self.reach = falling, landed, reach
        self.sent, self.received, self.fall_sent, self.fall_received = semaphores
        self.block = falling.shape[1]

    def rows(self, back, m):
        start = ((self.reach - back) * PLANE + flip(self.w.xy, m)) * self.block
        return pl.ds(pl.multiple_of(start, self.block), self.block)

    def cross(self, back, m):
        return pltpu.make_async_remote_copy(
            src_ref=self.frame.at[self.rows(back, m)],
            dst_ref=self.crossed.at[back, m - 1],
            send_sem=self.sent.at[back, m],
            recv_sem=self.received.at[back, m],
            device_id=self.w.across(m),
            device_id_type=MESH,
        )

    def fall(self, back):
        w = self.w
        count = PLANE * w.planes
        return pltpu.make_async_remote_copy(
            src_ref=self.falling.at[back - 1],
            dst_ref=self.landed.at[back - 1],
            send_sem=self.fall_sent.at[back],
            recv_sem=self.fall_received.at[back],
            device_id=(lax.rem(w.me - PLANE * back + count, count), w.s),
            device_id_type=MESH,
        )

    def begin(self):
        for back in reversed(range(self.reach + 1)):

            @pl.when(self.w.z >= back)
            def _(back=back):
                for m in range(1, PLANE):
                    self.cross(back, m).start()

    def pile(self, back):
        total = self.frame[self.rows(back, 0)].astype(jnp.float32)
        for m in range(1, PLANE):
            self.cross(back, m).wait_recv()
            total = total + self.crossed[back, m - 1].astype(jnp.float32)
        return total

    def drop(self, back):
        @pl.when(self.w.z >= back)
        def _():
            self.falling[back - 1] = self.pile(back).astype(self.falling.dtype)
            self.fall(back).start()

    def land(self, total):
        total[...] = self.pile(0)
        for back in range(1, self.reach + 1):

            @pl.when(self.w.z + back < self.w.planes)
            def _(back=back):
                self.fall(back).wait_recv()
                total[...] += self.landed[back - 1].astype(jnp.float32)

    def close(self):
        for back in range(self.reach + 1):

            @pl.when(self.w.z >= back)
            def _(back=back):
                for m in range(1, PLANE):
                    self.cross(back, m).wait_send()
                if back:
                    self.fall(back).wait_send()


def return_semaphores(reach):
    dma = pltpu.SemaphoreType.DMA
    return [dma((reach + 1, PLANE))] * 2 + [dma((reach + 1,))] * 2


def rear_kernel(
    planes,
    backs,
    feeds,
    hidden,
    pull,
    gain,
    merge_full,
    query_full,
    mixed,
    queries,
    keys,
    values,
    log_total,
    cosine,
    sine,
    normed,
    normed_columns,
    *rest,
):
    late_terms, early_terms, early_fars, outs, rest = split(rest, (3, 3, 3, 7, len(rest) - 16))
    feed_out, hidden_grad, gain_two_grad, normone, keyval_out, merge_term, query_term = outs
    results, fars, nears, rest = split(rest, (9, 6, 9, len(rest) - 24))
    (
        weight,
        stage,
        keyval_term,
        hidden_low,
        mixed_grad,
        query_grad,
        sums,
        outgoing,
        arrived_sums,
        frame,
        crossed,
        falling,
        landed,
        home,
        keyval_low,
        wide,
        narrow,
        arrived,
        local,
        stage_sem,
        pair_sem,
        feed_sent,
        feed_received,
    ), rest = split(rest, (23, len(rest) - 23))
    rings, early_sems, reduce_sems, return_sems = split(rest, (28, 6, 24, 4))
    w = Wires(planes)
    z, s, xy = w.z, w.s, w.xy
    block, width = normed.shape
    share = block // 2
    heads = queries.shape[0]
    reach = WINDOW // (PLANE * block)
    extent = WINDOW + block
    low = jnp.bfloat16
    greet(w.partners() + [w.across(3), w.twin()])

    early_ring, late_ring, deep_ring, small_ring = (
        Ring(rings[7 * i : 7 * i + 5], rings[7 * i + 5 : 7 * i + 7]) for i in range(4)
    )
    early_parts = [
        Reduce(w, early_ring, *refs, early_sems[2 * i : 2 * i + 2], halfway=True)
        for i, refs in enumerate(zip(early_terms, results, early_fars, nears))
    ]
    terms = (*late_terms, merge_term, query_term, keyval_term)
    late_parts = [
        Reduce(w, ring, *refs, reduce_sems[4 * i : 4 * i + 4])
        for i, (ring, refs) in enumerate(
            zip(
                (late_ring, late_ring, late_ring, deep_ring, deep_ring, small_ring),
                zip(terms, results[3:], fars, nears[3:]),
            )
        )
    ]
    parts = early_parts + late_parts
    order = piece_order(planes)
    pieces = [
        (part, kz) for pair in zip(early_parts, late_parts) for kz in order for part in pair
    ]
    pieces += [(late_parts[3], kz) for kz in order]
    pieces += [(part, kz) for kz in order for part in late_parts[4:]]
    crossing = [(part, kz) for part, kz in pieces if not part.halfway]
    ready = [0, 3 * planes]
    ahead = planes + planes // 2

    def feed_far(upto):
        while ready[0] < min(upto, ready[1]):
            part, kz = crossing[ready[0]]
            part.far_out(kz)
            ready[0] += 1

    def steps():
        met = 0
        for n in range(len(pieces) + LAG + 2):
            if n < len(pieces):
                part, kz = pieces[n]
                met += not part.halfway
                feed_far(met + ahead)
                yield partial(part.near_in, kz)
            lags = ((1, "near_out"), (LAG, "column_in"), (LAG + 1, "column_out"))
            for at, name in ((n - lag, name) for lag, name in lags):
                if 0 <= at < len(pieces):
                    part, kz = pieces[at]
                    yield partial(getattr(part, name), kz)

    moves = steps()

    def move(many=1):
        for _ in range(many):
            step = next(moves, None)
            if step is not None:
                step()

    load = pltpu.make_async_copy(merge_full, weight, local.at[0])
    load.start()
    feed_far(ahead)
    feed_copies = []
    for k in range(1, planes):
        feed_copies.append(
            send(
                feeds.at[k],
                feed_out.at[k],
                feed_sent.at[k],
                feed_received.at[k],
                w.across(PLANE * k),
            )
        )
    keep = pltpu.make_async_copy(feeds.at[0], feed_out.at[0], feed_sent.at[0])
    keep.start()

    pulled = jnp.sum(backs[...].astype(jnp.float32), axis=0)
    value = hidden[...]
    inverse = lax.rsqrt(jnp.mean(value * value, axis=-1, keepdims=True) + norm_epsilon)
    gain_two_grad[...] = jnp.sum(pulled * value * inverse, axis=0, keepdims=True)
    scaled = pulled * gain[...]
    lean = jnp.mean(value * scaled, axis=-1, keepdims=True)
    total = pull[...].astype(jnp.float32) + inverse * (scaled - value * (inverse * inverse * lean))
    hidden_grad[...] = total
    ours = pl.ds(pl.multiple_of(s * share, share), share)
    other = pl.ds(pl.multiple_of((1 - s) * share, share), share)
    hidden_low[ours] = total.astype(low)
    pair = send(hidden_low.at[ours], hidden_low.at[ours], pair_sem.at[0], pair_sem.at[1], w.twin())
    load.wait()
    there = hidden_low.at[other]
    pltpu.make_async_copy(there, there, pair_sem.at[1]).wait()
    pair.wait_send()

    group = planes_at_once(planes, weight.shape[2])
    span = group * PLANE * weight.shape[2]
    groups = planes // group

    total = None
    for j in range(groups):
        piece = flat_rows(weight[j * group : (j + 1) * group])
        part = jnp.dot(
            hidden_low[:, j * span : (j + 1) * span], piece, preferred_element_type=jnp.float32
        )
        total = part if total is None else total + part
    mixed_grad[...] = total.astype(low)
    load = pltpu.make_async_copy(query_full, weight, local.at[0])
    load.start()

    staged = {}

    def weigh(left, right, out):
        for j in range(groups):
            slot = j % 2
            if slot in staged:
                staged.pop(slot).wait()
            value = product_tn(left[:, j * span : (j + 1) * span], right[...])
            stage[slot] = value.reshape(stage.shape[1:]).astype(low)
            copy = pltpu.make_async_copy(
                stage.at[slot], out.at[pl.ds(j * group, group)], stage_sem.at[slot]
            )
            copy.start()
            staged[slot] = copy
        for slot in list(staged):
            staged.pop(slot).wait()

    weigh(hidden_low, mixed, merge_term)
    ready[1] = 4 * planes
    move(2)

    key_floor = WINDOW - w.me * block
    j_at = lax.broadcasted_iota(jnp.int32, (extent, QUERY_ROWS), 0)
    i_at = lax.broadcasted_iota(jnp.int32, (extent, QUERY_ROWS), 1)
    for h in range(heads):
        columns = slice(h * HD, (h + 1) * HD)
        for start in range(0, block, QUERY_ROWS):
            rows = slice(start, start + QUERY_ROWS)
            query, pulled = queries[h, rows], mixed_grad[rows, columns]
            allowed = (j_at > i_at + start) & (j_at <= i_at + (start + WINDOW)) & (j_at >= key_floor)
            scores = jnp.where(allowed, product_nt(keys[...], query), masked_score)
            chances = jnp.exp(scores - log_total[h, :, rows])
            pulls = product_nt(values[...], pulled)
            inner = jnp.sum(chances * pulls, axis=0, keepdims=True)
            score_low = (chances * (pulls - inner)).astype(low)
            value_part = jnp.dot(chances.astype(low), pulled, preferred_element_type=jnp.float32)
            key_part = jnp.dot(score_low, query, preferred_element_type=jnp.float32)
            if h or start:
                sums[0] += key_part
                sums[1] += value_part
            else:
                sums[0] = key_part
                sums[1] = value_part
            turned_back = product_tn(score_low, keys[...]) * HD ** (-0.5)
            query_grad[rows, columns] = turned(turned_back, cosine[rows], -sine[rows]).astype(low)
            move()

    outgoing[...] = sums[1 - s].astype(low)
    pair = send(outgoing, arrived_sums, pair_sem.at[2], pair_sem.at[3], w.twin())
    weigh(normed, query_grad, query_term)
    move(1)
    empty = jnp.zeros((PLANE * block, HD), low)
    frame[0 : PLANE * block] = empty
    frame[reach * PLANE * block :] = empty
    pair.wait_recv()
    window = pl.ds(pl.multiple_of(xy * block, block), extent)
    frame[window] = (sums[s] + arrived_sums[...].astype(jnp.float32)).astype(low)
    halo = HaloReturn(w, frame, crossed, falling, landed, reach, return_sems)
    halo.begin()

    load.wait()
    for j in range(groups):
        piece = flat_rows(weight[j * group : (j + 1) * group])
        wide[:, j * span : (j + 1) * span] = product_nt(query_grad[...], piece)
    narrow[...] = wide[other].astype(low)
    pair_two = send(narrow, arrived, pair_sem.at[4], pair_sem.at[5], w.twin())
    move(2)
    for back in reversed(range(1, reach + 1)):
        halo.drop(back)
    move(2)
    pair_two.wait_recv()
    normone[...] = wide[ours] + arrived[...].astype(jnp.float32)
    halo.land(home)

    @pl.when(s == 0)
    def _():
        home[...] = turned(home[...], cosine[...], -sine[...])

    keyval_low[s] = home[...].astype(low)
    pair_three = send(
        keyval_low.at[s], keyval_low.at[s], pair_sem.at[6], pair_sem.at[7], w.twin()
    )
    move(2)
    there = keyval_low.at[1 - s]
    pltpu.make_async_copy(there, there, pair_sem.at[7]).wait()
    keyval_out[...] = keyval_low[...]
    for i in range(2):
        value = product_tn(normed_columns[...], keyval_low[i])
        keyval_term[:, :, :, i * HD : (i + 1) * HD] = value.reshape(
            keyval_term.shape[:3] + (HD,)
        ).astype(low)
    ready[1] = 6 * planes

    move(4 * len(pieces) + 12)
    for copy in (pair, pair_two, pair_three):
        copy.wait_send()
    keep.wait()
    for copy in feed_copies:
        copy.wait()
    halo.close()
    for ring in (early_ring, late_ring, deep_ring, small_ring):
        ring.close()
    for part in parts:
        part.close()


def rear(
    backs,
    feeds,
    hidden,
    pull,
    gain,
    merge_full,
    query_full,
    mixed,
    queries,
    keys,
    values,
    log_total,
    cosine,
    sine,
    normed,
    normed_columns,
    late_terms,
    early_terms,
    early_fars,
):
    planes = lax.axis_size("ctx") // PLANE
    block, width = normed.shape
    share = block // 2
    heads = queries.shape[0]
    reach = WINDOW // (PLANE * block)
    extent = WINDOW + block
    low, full = jnp.bfloat16, jnp.float32
    some, near = pl.BlockSpec(memory_space=pl.ANY), pl.BlockSpec(memory_space=pltpu.VMEM)
    shape = jax.ShapeDtypeStruct
    dma = pltpu.SemaphoreType.DMA
    group = planes_at_once(planes, merge_full.shape[2])
    keyval_rows = normed_columns.shape[1] // (planes * PLANE)
    deep = merge_full.shape[2:]
    sizes = [late_terms[0].shape[2:]] * 3 + [deep] * 2 + [(keyval_rows, 2 * HD)]
    all_sizes = [early_terms[0].shape[2:]] * 3 + sizes
    rings = [ring_scratch(*all_sizes[i]) for i in (0, 3, 6, 8)]
    outs = pl.pallas_call(
        partial(rear_kernel, planes),
        out_shape=[
            shape((planes, share, width), low),
            shape((share, width), full),
            shape((1, width), full),
            shape((share, width), full),
            shape((2, block, HD), low),
            shape(merge_full.shape, low),
            shape(query_full.shape, low),
        ]
        + [shape((planes,) + size, low) for size in all_sizes]
        + [shape((planes, 2) + size, low) for size in sizes]
        + [shape((planes,) + size, low) for size in all_sizes],
        in_specs=[near, some, near, near, near, some, some] + [near] * 9 + [some] * 9,
        out_specs=[some, near, near, near, near, some, some] + [some] * 24,
        scratch_shapes=[
            pltpu.VMEM(merge_full.shape, low),
            pltpu.VMEM((2, group) + merge_full.shape[1:], low),
            pltpu.VMEM((planes, PLANE, keyval_rows, 2 * HD), low),
            pltpu.VMEM((block, width), low),
            pltpu.VMEM((block, heads * HD), low),
            pltpu.VMEM((block, heads * HD), low),
            pltpu.VMEM((2, extent, HD), full),
            pltpu.VMEM((extent, HD), low),
            pltpu.VMEM((extent, HD), low),
            pltpu.VMEM(((reach + 1) * PLANE * block, HD), low),
            pltpu.VMEM((reach + 1, PLANE - 1, block, HD), low),
            pltpu.VMEM((reach, block, HD), low),
            pltpu.VMEM((reach, block, HD), low),
            pltpu.VMEM((block, HD), full),
            pltpu.VMEM((2, block, HD), low),
            pltpu.VMEM((block, width), full),
            pltpu.VMEM((share, width), low),
            pltpu.VMEM((share, width), low),
            dma((1,)),
            dma((2,)),
            dma((8,)),
            dma((planes,)),
            dma((planes,)),
        ]
        + [item for buffers, semaphores in rings for item in buffers + semaphores]
        + reduce_semaphores(planes, halfway=True) * 3
        + reduce_semaphores(planes) * 6
        + return_semaphores(reach),
        compiler_params=pltpu.CompilerParams(
            collective_id=2, has_side_effects=True, vmem_limit_bytes=62 * 2**20
        ),
    )(
        backs,
        feeds,
        hidden,
        pull,
        gain,
        merge_full,
        query_full,
        mixed,
        queries,
        keys,
        values,
        log_total,
        cosine,
        sine,
        normed,
        normed_columns,
        *late_terms,
        *early_terms,
        *early_fars,
    )
    return outs[:5], outs[7:16]


STEP_COLUMNS = 256


def middle_kernel(
    planes,
    depth,
    lanes,
    half,
    pulls,
    gate,
    upward,
    down,
    gate_rest,
    upward_rest,
    down_rest,
    back_out,
    feed_out,
    gate_term,
    upward_term,
    down_term,
    *refs,
):
    wholes, terms, fars, rest = split(refs, (3, 3, 3, len(refs) - 9))
    (
        early,
        late,
        rows,
        grads,
        early_acts,
        late_acts,
        own,
        outgoing,
        incoming,
        sums,
        stage,
        local,
        row_local,
        stage_sem,
        pair_sent,
        pair_received,
        back_sent,
        back_received,
        feed_local,
    ), rest = split(rest, (19, len(rest) - 19))
    spread_sems, cross_sems, column_sems = split(rest, (9, 6, 5))
    w = Wires(planes)
    z = w.z
    share, width = half.shape
    count = planes * 2 * share
    greet(w.partners() + [w.twin()])
    column = Column(w, half, rows, column_sems)
    column.rise()
    loads = [
        pltpu.make_async_copy(source, early.at[i], local.at[i])
        for i, source in enumerate((gate, upward, down))
    ]
    for load in loads:
        load.start()
    pulled = []
    for k in range(planes):
        at = flip(z, k)
        pulled.append(pltpu.make_async_copy(pulls.at[at], grads.at[at], row_local.at[k]))
        pulled[k].start()
    spreads = [
        Spread(w, "column", source, whole, spread_sems[3 * i : 3 * i + 3])
        for i, (source, whole) in enumerate(zip((gate_rest, upward_rest, down_rest), wholes))
    ]
    parts = [
        Cross(w, term, far, cross_sems[2 * i : 2 * i + 2])
        for i, (term, far) in enumerate(zip(terms, fars))
    ]

    for part in spreads:
        part.rise()
        for kz in range(planes):
            part.spread(kz)
    steps = [partial(part.relay, kz) for part in spreads for kz in range(planes)]

    def move(many=1):
        for _ in range(many):
            if steps:
                steps.pop(0)()

    def bend(k, weights, acts):
        units = weights.shape[4]
        here = flip(z, k)
        for at in range(0, units, STEP_COLUMNS):
            columns = slice(at, min(at + STEP_COLUMNS, units))
            gate_value, up_value, pull = (
                jnp.dot(
                    left[here],
                    flat_rows(weights[i, :, :, :, columns]),
                    preferred_element_type=jnp.float32,
                )
                for i, left in enumerate((rows, rows, grads))
            )
            bent, slope = gelu_parts(gate_value)
            acts[0, here, :, columns] = (pull * up_value * slope).astype(acts.dtype)
            acts[1, here, :, columns] = (pull * bent).astype(acts.dtype)
            acts[2, here, :, columns] = (bent * up_value).astype(acts.dtype)

    for load in loads:
        load.wait()
    waiting = ladder(planes)
    for k in range(planes):
        while k and k in waiting:
            column.pass_on(waiting.pop(0))
        column.ready(k)
        pulled[k].wait()
        bend(k, early, early_acts)
        move(2)

    group, span = stage.shape[1], stage.shape[1] * stage.shape[2] * stage.shape[3]
    groups = planes // group
    staged = {}
    turns = 0
    for i, left in enumerate((rows, rows, grads)):
        for j in range(groups):
            slot = turns % 2
            turns += 1
            if slot in staged:
                staged.pop(slot).wait()
            value = product_tn(
                left[:, :, j * span : (j + 1) * span].reshape(count, span),
                early_acts[i].reshape(count, -1),
            )
            stage[slot] = value.reshape(stage.shape[1:]).astype(stage.dtype)
            copy = pltpu.make_async_copy(
                stage.at[slot], terms[i].at[pl.ds(j * group, group)], stage_sem.at[slot]
            )
            copy.start()
            staged[slot] = copy
        move(2)
    for slot in list(staged):
        staged.pop(slot).wait()
    for kz in piece_order(planes):
        for part in parts:
            part.far_out(kz)
    move(len(steps))
    for part in spreads:
        part.settle()
    loads = [
        pltpu.make_async_copy(whole, late.at[i], local.at[i]) for i, whole in enumerate(wholes)
    ]
    for load in loads:
        load.start()

    def pair_copy(turn):
        return pltpu.make_async_remote_copy(
            src_ref=outgoing.at[turn % depth],
            dst_ref=incoming.at[turn % 2],
            send_sem=pair_sent.at[turn % depth],
            recv_sem=pair_received.at[turn % 2],
            device_id=w.twin(),
            device_id_type=MESH,
        )

    def offset(turn):
        return planes - 1 - turn

    def back_copy(turn):
        k = offset(turn)
        return pltpu.make_async_remote_copy(
            src_ref=sums.at[turn % lanes, 0],
            dst_ref=back_out.at[k],
            send_sem=back_sent.at[k],
            recv_sem=back_received.at[k],
            device_id=w.across(PLANE * k),
            device_id_type=MESH,
        )

    def kept_copy(turn):
        return pltpu.make_async_copy(sums.at[turn % lanes, 0], back_out.at[0], back_sent.at[0])

    def feed_copy(turn):
        return pltpu.make_async_copy(
            sums.at[turn % lanes, 1], feed_out.at[offset(turn)], feed_local.at[turn]
        )

    def shipped(turn):
        feed_copy(turn).wait()
        if turn == planes - 1:
            kept_copy(turn).wait()
        else:
            back_copy(turn).wait_send()

    def settle(turn):
        pair = pair_copy(turn)
        pair.wait_recv()
        pair.wait_send()
        if turn >= lanes:
            shipped(turn - lanes)
        for i in range(2):
            total = own[turn % depth, i] + incoming[turn % 2, i].astype(jnp.float32)
            sums[turn % lanes, i] = total.astype(sums.dtype)
        if turn == planes - 1:
            kept_copy(turn).start()
        else:
            back_copy(turn).start()
        feed_copy(turn).start()

    def sides(k, slot):
        here = flip(z, k)

        def both(weights, acts, i, at):
            return product_nt(acts[i, here], flat_rows(weights[i, at]))

        def part(j, _):
            columns = pl.ds(pl.multiple_of(j * span, 128), span)
            at = pl.ds(j * group, group)
            back = sum(
                both(weights, acts, i, at)
                for weights, acts in ((early, early_acts), (late, late_acts))
                for i in (0, 1)
            )
            feed = both(early, early_acts, 2, at) + both(late, late_acts, 2, at)
            for i, value in enumerate((back, feed)):
                own[slot, i, :, columns] = value[:share]
                outgoing[slot, i, :, columns] = value[share:].astype(outgoing.dtype)
            return 0

        lax.fori_loop(0, groups, part, 0)

    for load in loads:
        load.wait()
    for turn in range(planes):
        k = offset(turn)
        bend(k, late, late_acts)
        sides(k, turn % depth)
        if depth > 1 and turn > 0:
            settle(turn - 1)
        pair_copy(turn).start()
        if depth == 1:
            settle(turn)
    if depth > 1:
        settle(planes - 1)

    for i, left in enumerate((rows, rows, grads)):

        def weigh(j, _, i=i, left=left):
            columns = pl.ds(pl.multiple_of(j * span, 128), span)
            value = product_tn(
                left[:, :, columns].reshape(count, span), late_acts[i].reshape(count, -1)
            )
            value = value.reshape((group,) + late.shape[2:])
            late[i, pl.ds(j * group, group)] = value.astype(late.dtype)
            return 0

        lax.fori_loop(0, groups, weigh, 0)
        out = (gate_term, upward_term, down_term)[i]
        pltpu.make_async_copy(late.at[i], out, local.at[i]).start()
    for i, out in enumerate((gate_term, upward_term, down_term)):
        pltpu.make_async_copy(late.at[i], out, local.at[i]).wait()
    for turn in range(planes):
        if turn >= planes - lanes:
            shipped(turn)
        if turn < planes - 1:
            back_copy(turn).wait_recv()
    for part in spreads + parts + [column]:
        part.close()


def middle(half, pulls, gate, upward, down, gate_rest, upward_rest, down_rest):
    planes = lax.axis_size("ctx") // PLANE
    depth, lanes = (2, planes) if planes <= 4 else (1, 2)
    block, width = pulls.shape[1:]
    share = block // 2
    early, late = gate.shape[3], gate_rest.shape[2]
    rows = gate_rest.shape[1]
    low = jnp.bfloat16
    some = pl.BlockSpec(memory_space=pl.ANY)
    shape = jax.ShapeDtypeStruct
    dma = pltpu.SemaphoreType.DMA
    group = planes_at_once(planes, rows)
    outs = pl.pallas_call(
        partial(middle_kernel, planes, depth, lanes),
        out_shape=[shape((planes, share, width), low)] * 2
        + [shape((planes, PLANE, rows, late), low)] * 6
        + [shape((planes, PLANE, rows, early), low)] * 3
        + [shape((planes, 2, rows, early), low)] * 3,
        in_specs=[some] * 8,
        out_specs=[some] * 14,
        scratch_shapes=[
            pltpu.VMEM((3, planes, PLANE, rows, early), low),
            pltpu.VMEM((3, planes, PLANE, rows, late), low),
            pltpu.VMEM((planes, block, width), low),
            pltpu.VMEM((planes, block, width), low),
            pltpu.VMEM((3, planes, block, early), low),
            pltpu.VMEM((3, planes, block, late), low),
            pltpu.VMEM((depth, 2, share, width), jnp.float32),
            pltpu.VMEM((depth, 2, share, width), low),
            pltpu.VMEM((2, 2, share, width), low),
            pltpu.VMEM((lanes, 2, share, width), low),
            pltpu.VMEM((2, group, PLANE, rows, early), low),
            dma((3,)),
            dma((planes,)),
            dma((2,)),
            dma((depth,)),
            dma((2,)),
            dma((planes,)),
            dma((planes,)),
            dma((planes,)),
        ]
        + spread_semaphores(planes, "units") * 3
        + [dma((planes, 2))] * 6
        + column_semaphores(planes),
        compiler_params=pltpu.CompilerParams(
            collective_id=3, has_side_effects=True, vmem_limit_bytes=63 * 2**20
        ),
    )(half, pulls, gate, upward, down, gate_rest, upward_rest, down_rest)
    return outs[:2], outs[2:5], outs[8:11], outs[11:14]


def shards(
    tokens,
    cotangent,
    query_weight,
    query_first,
    query_second,
    keyval_weight,
    keyval_first,
    keyval_second,
    merge_weight,
    merge_first,
    merge_second,
    gate_weight,
    gate_first,
    gate_second,
    up_weight,
    up_first,
    up_second,
    down_weight,
    down_first,
    down_second,
    gains,
    gains_first,
    gains_second,
):
    low = jnp.bfloat16
    z, xy = place()
    s = lax.axis_index("shard")
    blocks = lax.axis_size("ctx")
    planes = blocks // PLANE
    row_count = tokens.shape[0]
    share = row_count // 2
    width = tokens.shape[1]

    def own_rows(value):
        return lax.dynamic_slice_in_dim(value, s * share, share, 0)

    small = jnp.concatenate([keyval_weight.astype(low), gains.astype(low)], axis=0).T
    small = jnp.pad(small, ((0, 0), (0, -small.shape[1] % 128)))
    small_all = open_gather(small)
    small_all = small_all.transpose(1, 2, 0, 3, 4).reshape(width, -1)
    keyval_full = small_all[:, : 2 * HD]
    gain_used = small_all[:, 2 * HD : 2 * HD + 2].T.astype(jnp.float32)

    offset = lax.axis_index("ctx") * row_count
    positions = offset + jnp.arange(row_count, dtype=jnp.int32)
    inputs = tokens.astype(jnp.float32)
    normed = normalize(inputs, gain_used[0]).astype(low)

    keyval = jnp.dot(normed, keyval_full, preferred_element_type=jnp.float32)
    keyval_mine = jnp.where(s == 0, rotate(keyval[:, :HD], positions), keyval[:, HD:]).astype(low)
    unit_weights = [unit_pieces(v) for v in (gate_weight, up_weight, down_weight)]
    early = early_units(unit_weights[0].shape[2])
    early_pieces = [v[:, :, :early] for v in unit_weights]
    late_pieces = [v[:, :, early:] for v in unit_weights]
    cosine, sine = rotary_tables(positions)
    (
        query_full,
        merge_full,
        gate_full,
        upward_full,
        down_full,
        *late_columns,
        pulls_all,
        queries,
        key_part,
        value_part,
        mixed_flat,
        log_total,
        hidden,
        normed_two,
    ) = front(
        normed,
        keyval_mine,
        cosine,
        sine,
        own_rows(tokens),
        gain_used[1:],
        own_rows(cotangent),
        query_weight.astype(low),
        merge_weight.astype(low),
        early_pieces,
        late_pieces,
    )
    input_rows = own_rows(inputs)

    (backs, feeds), late_terms, early_terms, early_fars = middle(
        normed_two, pulls_all, gate_full, upward_full, down_full, *late_columns
    )
    keyval_rows = width // blocks // 2
    normed_columns = pick(normed.reshape(row_count, blocks, 2, keyval_rows), s, 2)
    normed_columns = jnp.pad(normed_columns, ((0, 0), (0, 0), (0, -keyval_rows % 8)))
    (
        (feeds, hidden_grad, gain_two_grad, normone_grad, keyval_lin),
        (*unit_parts, merge_parts, query_parts, keyval_parts),
    ) = rear(
        backs,
        feeds,
        hidden,
        own_rows(cotangent),
        gain_used[1:],
        merge_full,
        query_full,
        mixed_flat,
        queries,
        key_part,
        value_part,
        log_total.reshape(log_total.shape[0], 1, -1),
        cosine,
        sine,
        normed,
        normed_columns.reshape(row_count, -1),
        late_terms,
        early_terms,
        early_fars,
    )
    gate_reduced, upward_reduced, down_reduced = (
        join_units(*g) for g in zip(unit_parts[:3], unit_parts[3:])
    )
    merge_reduced, query_reduced, keyval_sums = (
        jnp.sum(g.astype(jnp.float32), axis=0) for g in (merge_parts, query_parts, keyval_parts)
    )
    keyval_reduced = keyval_sums[:keyval_rows].T
    block_output = in_order((hidden + jnp.sum(feeds.astype(jnp.float32), axis=0)).astype(low))

    keyval_rows_lin = jnp.concatenate([own_rows(keyval_lin[0]), own_rows(keyval_lin[1])], axis=1)
    normone_grad = normone_grad + contract(keyval_rows_lin, keyval_full, 1, 1)
    gain_one_grad = jnp.sum(normone_grad * input_rows * inverse_rms(input_rows), axis=0)
    norm_one_pull = jax.vjp(partial(normalize, gain_row=gain_used[0]), input_rows)[1]
    tokens_grad = in_order(hidden_grad + norm_one_pull(normone_grad)[0])

    gain_terms = jnp.stack([gain_one_grad, gain_two_grad[0]]).reshape(2, blocks, 2, -1)
    gain_terms = gain_terms.transpose(2, 1, 0, 3)
    gain_sums = pick(gain_terms, s) + swap(pick(gain_terms, 1 - s))
    gains_reduced = reduce_small(gain_sums, jnp.float32)

    query_variance, query_updated = adamw(
        query_weight, query_first, query_second, query_reduced, 4.0 / math.sqrt(D)
    )
    keyval_variance, keyval_updated = adamw(
        keyval_weight, keyval_first, keyval_second, keyval_reduced, 2.0 / math.sqrt(D)
    )
    merge_variance, merge_updated = adamw(
        merge_weight, merge_first, merge_second, merge_reduced, 8.0 / math.sqrt(NH * HD)
    )
    gate_variance, gate_updated = adamw(
        gate_weight, gate_first, gate_second, gate_reduced, 2.0 / math.sqrt(D)
    )
    up_variance, up_updated = adamw(
        up_weight, up_first, up_second, upward_reduced, 2.0 / math.sqrt(D)
    )
    down_variance, down_updated = adamw(
        down_weight, down_first, down_second, down_reduced, 2.0 / math.sqrt(FF)
    )
    gains_variance, gains_updated = adamw(gains, gains_first, gains_second, gains_reduced, 0.8)
    return (
        block_output,
        tokens_grad,
        query_reduced,
        query_variance,
        query_updated,
        keyval_reduced,
        keyval_variance,
        keyval_updated,
        merge_reduced,
        merge_variance,
        merge_updated,
        gate_reduced,
        gate_variance,
        gate_updated,
        upward_reduced,
        up_variance,
        up_updated,
        down_reduced,
        down_variance,
        down_updated,
        gains_reduced,
        gains_variance,
        gains_updated,
    )


def solution(mesh):
    return jax.shard_map(
        shards,
        mesh=mesh,
        in_specs=(
            P("ctx", None),
            P("ctx", None),
            P("ctx", "shard"),
            P("ctx", "shard"),
            P("ctx", "shard"),
            P(None, ("ctx", "shard")),
            P(None, ("ctx", "shard")),
            P(None, ("ctx", "shard")),
            P("ctx", "shard"),
            P("ctx", "shard"),
            P("ctx", "shard"),
            P("ctx", "shard"),
            P("ctx", "shard"),
            P("ctx", "shard"),
            P("ctx", "shard"),
            P("ctx", "shard"),
            P("ctx", "shard"),
            P("ctx", "shard"),
            P("ctx", "shard"),
            P("ctx", "shard"),
            P(None, ("ctx", "shard")),
            P(None, ("ctx", "shard")),
            P(None, ("ctx", "shard")),
        ),
        out_specs=(
            P("ctx", None),
            P("ctx", None),
            P("ctx", "shard"),
            P("ctx", "shard"),
            P("ctx", "shard"),
            P(None, ("ctx", "shard")),
            P(None, ("ctx", "shard")),
            P(None, ("ctx", "shard")),
            P("ctx", "shard"),
            P("ctx", "shard"),
            P("ctx", "shard"),
            P("ctx", "shard"),
            P("ctx", "shard"),
            P("ctx", "shard"),
            P("ctx", "shard"),
            P("ctx", "shard"),
            P("ctx", "shard"),
            P("ctx", "shard"),
            P("ctx", "shard"),
            P("ctx", "shard"),
            P(None, ("ctx", "shard")),
            P(None, ("ctx", "shard")),
            P(None, ("ctx", "shard")),
        ),
        check_vma=False,
    )
```
